32 devices in a mesh: shard: 8 (over y, x, core), rep: 4 (over z).
Axes of the slice: x: 2, y: 2, z: 4, core: 2. Of those that a mesh axis runs over, the one named last changes fastest.
Arguments:
- tokens: bfloat16 [6304, 768], P(('shard', 'rep')), may hold values from -6 to 6
- cotangent: bfloat16 [6304, 768], P(('shard', 'rep')), may hold values from -6 to 6
- expert_index: int32 [6304, 2], P(('shard', 'rep')), may hold values from 0 to 2, as said below
- slot_index: int32 [6304, 2], P(('shard', 'rep')), may hold values from 0 to 111, as said below
- kept_mask: int32 [6304, 2], P(('shard', 'rep')), may hold values from 0 to 1, as said below
- gain_attn: float32 [768], P('shard'), may hold values from 0.5 to 1.5
- shift_attn: float32 [768], P('shard'), may hold values from -1.75 to 1.75
- w_qkv: float32 [768, 2304], P('shard'), may hold values from -0.3125 to 0.3125
- w_proj: float32 [768, 768], P('shard'), may hold values from -0.875 to 0.875
- gain_moe: float32 [768], P('shard'), may hold values from 0.5 to 1.5
- shift_moe: float32 [768], P('shard'), may hold values from -1.75 to 1.75
- w_router: float32 [768, 3], P('shard'), may hold values from -0.15625 to 0.15625
- w_in: float32 [768, 3, 3072], P('shard'), may hold values from -0.21875 to 0.21875
- w_out: float32 [3072, 3, 768], P('shard'), may hold values from -0.4375 to 0.4375
Outputs:
- output: bfloat16 [6304, 768], P(('shard', 'rep'))
- input_grad: bfloat16 [6304, 768], P(('shard', 'rep'))
- gain_attn_grad: float32 [768], P('shard')
- shift_attn_grad: float32 [768], P('shard')
- w_qkv_grad: float32 [768, 2304], P('shard')
- w_proj_grad: float32 [768, 768], P('shard')
- gain_moe_grad: float32 [768], P('shard')
- shift_moe_grad: float32 [768], P('shard')
- w_router_grad: float32 [768, 3], P('shard')
- w_in_grad: float32 [768, 3, 3072], P('shard')
- w_out_grad: float32 [3072, 3, 768], P('shard')
The draws below stay inside these ranges and needn't reach their ends.
Inputs may be any that keep to these rules, and one draw needn't show every extreme that they name: `expert_index`: each row names two different experts. Where kept_mask is 1, slot_index counts the earlier assignments to the same expert among the rows of one device, all first choices of those rows counted before any second choice; where kept_mask is 0 it is 0. `kept_mask`: 1 exactly where that count is under 112; on every device some expert fills all 112 slots.
All inputs are finite; a program needn't handle non-finite values.
Results may differ from the reference program's by a relative error of at most 0.022.
Values may be sent and summed in bfloat16 or wider, within the bound.
A program may use at most 384 MiB of HBM per device.

```python
import jax
import jax.numpy as jnp
from jax import lax

D = 768
HEADS = 12
HEAD_DIM = 64
FF = 3072
SEQ = 197
EXPERTS = 3
TOK_DEV = 197
CAP = 112
TOKENS = 6304


def route_table(key):
    first_key, step_key = jax.random.split(key)
    first_choice = jax.random.randint(first_key, (TOKENS,), 0, EXPERTS)
    step_choice = jax.random.randint(step_key, (TOKENS,), 1, EXPERTS)
    second_choice = (first_choice + step_choice) % EXPERTS
    chosen = jnp.stack([first_choice, second_choice], axis=1).astype(jnp.int32)
    blocks = TOKENS // TOK_DEV
    ordered = jnp.transpose(chosen.reshape(blocks, TOK_DEV, 2), (0, 2, 1)).reshape(blocks, 2 * TOK_DEV)
    onehot = (ordered[:, :, None] == jnp.arange(EXPERTS, dtype=jnp.int32)[None, None, :]).astype(jnp.int32)
    ranking = jnp.sum((jnp.cumsum(onehot, axis=1) - 1) * onehot, axis=2)
    ranking = jnp.transpose(ranking.reshape(blocks, 2, TOK_DEV), (0, 2, 1)).reshape(TOKENS, 2)
    kept_rows = (ranking < CAP).astype(jnp.int32)
    slot_rows = (ranking * kept_rows).astype(jnp.int32)
    return (chosen, slot_rows, kept_rows)


def draw_expert_index(key, part):
    return route_table(key)[0]


def draw_slot_index(key, part):
    return route_table(key)[1]


def draw_kept_mask(key, part):
    return route_table(key)[2]


def shard_levels(own_key, dims, shards, smallest, high):
    level, own = 1.0, jax.random.fold_in(own_key, 6)
    for position, shards_of in shards:
        heights = jnp.exp(jax.random.uniform(jax.random.fold_in(own, position), (shards_of,), jnp.float32, smallest / len(shards), high / len(shards)))
        level = level * jnp.repeat(heights, dims[position] // shards_of).reshape([-1 if axis == position else 1 for axis in range(len(dims))])
    return level


def noise(rng, shape, scale, most, cuts=(), held_as=jnp.bfloat16):
    entries = jax.random.normal(rng, shape, jnp.float32) * scale
    if len(cuts) > 0:
        entries = shard_levels(rng, shape, cuts, -0.22, 0.18) * entries
    return jnp.clip(entries, min=-most, max=most).astype(held_as)


def setup_inputs(seed: int = 0) -> dict:
    key_list = jax.random.split(jax.random.key(seed), 15)
    return {
        "tokens": noise(key_list[0], (TOKENS, D), 1.0, 6.0, ((0, 32),)),
        "cotangent": noise(key_list[1], (TOKENS, D), 1.0, 6.0, ((0, 32),)),
        "expert_index": draw_expert_index(jax.random.fold_in(key_list[14], 71), 0),
        "slot_index": draw_slot_index(jax.random.fold_in(key_list[14], 71), 0),
        "kept_mask": draw_kept_mask(jax.random.fold_in(key_list[14], 71), 0),
        "gain_attn": jnp.clip(1.0 + 0.1 * jax.random.normal(key_list[5], (D,), jnp.float32), 0.5, 1.5),
        "shift_attn": noise(key_list[6], (D,), 0.3, 1.75, ((0, 8),), jnp.float32),
        "w_qkv": noise(key_list[7], (D, 3 * D), (D // 2) ** -0.5, 0.3125, ((0, 8),), jnp.float32),
        "w_proj": noise(key_list[8], (D, D), (D // 16) ** -0.5, 0.875, ((0, 8),), jnp.float32),
        "gain_moe": jnp.clip(1.0 + 0.1 * jax.random.normal(key_list[9], (D,), jnp.float32), 0.5, 1.5),
        "shift_moe": noise(key_list[10], (D,), 0.3, 1.75, ((0, 8),), jnp.float32),
        "w_router": noise(key_list[11], (D, EXPERTS), (2 * D) ** -0.5, 0.15625, ((0, 8),), jnp.float32),
        "w_in": noise(key_list[12], (D, EXPERTS, FF), D ** -0.5, 0.21875, ((0, 8),), jnp.float32),
        "w_out": noise(key_list[13], (FF, EXPERTS, D), (FF // 16) ** -0.5, 0.4375, ((0, 8),), jnp.float32),
    }


@jax.custom_vjp
def low(v):
    return lax.optimization_barrier(v.astype(jnp.bfloat16)).astype(jnp.float32)

@jax.custom_vjp
def low_back(v):
    return v

def low_keep(v):
    return (low(v), None)

def low_pass(kept, grad):
    return (grad,)

def back_keep(v):
    return (v, None)

def back_low(kept, grad):
    return (low(grad),)
low.defvjp(low_keep, low_pass)
low_back.defvjp(back_keep, back_low)
epsilon = 1e-06
score_scale = 0.125
highest = lax.Precision.HIGHEST

def layer_norm(inputs, gain_vec, shift_vec):
    centred = inputs - lax.optimization_barrier(jnp.mean(inputs, axis=-1, keepdims=True))
    normed = centred * lax.rsqrt(lax.optimization_barrier(jnp.mean(centred * centred, axis=-1, keepdims=True)) + epsilon)
    return normed * gain_vec + shift_vec

def block_layer(block_items, params):
    hidden_in, chosen, slot_rows, kept_rows = block_items
    gain_first, shift_first, qkv_weight, proj_weight, gain_second, shift_second, router_weight, inner_weight, outer_weight = params
    images = hidden_in.shape[0] // SEQ
    ln_one = low(layer_norm(hidden_in, gain_first, shift_first))
    triple = low(low_back(jnp.dot(ln_one, qkv_weight, precision=highest)))
    queries = triple[:, :D].reshape(images, SEQ, HEADS, HEAD_DIM)
    key_rows = triple[:, D:2 * D].reshape(images, SEQ, HEADS, HEAD_DIM)
    value_rows = triple[:, 2 * D:].reshape(images, SEQ, HEADS, HEAD_DIM)
    scores = low_back(jnp.einsum('ishd,ithd->ihst', queries, key_rows, precision=highest))
    attn_probs = jax.nn.softmax(scores * score_scale, axis=-1)
    mixed_heads = jnp.einsum('ihst,ithd->ishd', low(attn_probs), value_rows, precision=highest).reshape(-1, D)
    mixed_heads = low(low_back(mixed_heads))
    residual = hidden_in + low_back(jnp.dot(mixed_heads, proj_weight, precision=highest))
    ln_two = low(layer_norm(residual, gain_second, shift_second))
    logits = low_back(jnp.dot(ln_two, router_weight, precision=highest))
    router_probs = jax.nn.softmax(logits, axis=-1)
    kept_float = kept_rows.astype(jnp.float32)
    onehot = (chosen[:, :, None] == jnp.arange(EXPERTS, dtype=jnp.int32)[None, None, :]).astype(jnp.float32)
    gate_values = lax.optimization_barrier(jnp.sum(onehot * router_probs[:, None, :], axis=-1)) * kept_float
    flat_slots = (chosen * CAP + slot_rows).reshape(-1)
    outgoing = (ln_two[:, None, :] * kept_float[:, :, None]).reshape(-1, D)
    buffer = jnp.zeros((EXPERTS * CAP, D), jnp.float32).at[flat_slots].add(outgoing).reshape(EXPERTS, CAP, D)
    hidden_pre = low_back(jnp.einsum('ecd,def->ecf', buffer, inner_weight, precision=highest))
    active = low(jax.nn.gelu(hidden_pre))
    expert_out = low_back(jnp.einsum('ecf,fed->ecd', active, outer_weight, precision=highest)).reshape(EXPERTS * CAP, D)
    picked = expert_out[flat_slots].reshape(-1, 2, D)
    return residual + lax.optimization_barrier(jnp.sum(gate_values[:, :, None] * picked, axis=1))

def reference(tokens, cotangent, expert_index, slot_index, kept_mask, gain_attn, shift_attn, w_qkv, w_proj, gain_moe, shift_moe, w_router, w_in, w_out):
    blocks = tokens.shape[0] // TOK_DEV

    def forward(inputs, gain_a, shift_a, qkv_weight, proj_weight, gain_m, shift_m, router_weight, inner_weight, outer_weight):
        lowered = (low(gain_a), low(shift_a), low(qkv_weight), low(proj_weight), low(gain_m), low(shift_m), low(router_weight), low(inner_weight), low(outer_weight))

        def per_block(block_items):
            return block_layer(block_items, lowered)
        stacked = (inputs.reshape(blocks, TOK_DEV, D), expert_index.reshape(blocks, TOK_DEV, 2), slot_index.reshape(blocks, TOK_DEV, 2), kept_mask.reshape(blocks, TOK_DEV, 2))
        return lax.map(jax.checkpoint(per_block), stacked).reshape(-1, D)
    output, pullback = jax.vjp(forward, tokens.astype(jnp.float32), gain_attn, shift_attn, w_qkv, w_proj, gain_moe, shift_moe, w_router, w_in, w_out)
    gradients = pullback(cotangent.astype(jnp.float32))
    return (output.astype(jnp.bfloat16), gradients[0].astype(jnp.bfloat16), gradients[1], gradients[2], gradients[3], gradients[4], gradients[5], gradients[6], gradients[7], gradients[8], gradients[9])
```

```python
import jax
import jax.numpy as jnp
from jax import lax
from jax.sharding import PartitionSpec as P

HEADS = 12
HEAD_DIM = 64
SEQ = 197
CAP = 112


epsilon = 1e-06
score_scale = 0.125


def normalize(inputs):
    centred = inputs - jnp.mean(inputs, axis=-1, keepdims=True)
    inverse = lax.rsqrt(jnp.mean(centred * centred, axis=-1, keepdims=True) + epsilon)
    return (centred * inverse, inverse)


def norm_back(upstream, normed, inverse):
    return inverse * (
        upstream
        - jnp.mean(upstream, axis=-1, keepdims=True)
        - normed * jnp.mean(upstream * normed, axis=-1, keepdims=True)
    )


def to_heads(matrix, images):
    return matrix.reshape(images, -1, HEADS, HEAD_DIM)


def shards(
    tokens,
    cotangent,
    expert_index,
    slot_index,
    kept_mask,
    gain_attn,
    shift_attn,
    w_qkv,
    w_proj,
    gain_moe,
    shift_moe,
    w_router,
    w_in,
    w_out,
):
    model_width = tokens.shape[1]
    images = tokens.shape[0] // SEQ
    rows = tokens.shape[0]
    experts = w_in.shape[1]
    group = lax.axis_size("shard")
    low = jnp.bfloat16
    wide = jnp.float32

    def gathered(value):
        return lax.all_gather(value, "shard", axis=0, tiled=True)

    qkv_full = gathered(w_qkv.astype(low))
    proj_full = gathered(w_proj.astype(low))
    smalls = gathered(
        jnp.concatenate(
            [
                jnp.stack([gain_attn, shift_attn, gain_moe, shift_moe], axis=1),
                w_router,
            ],
            axis=1,
        ).astype(low)
    )
    gain_first, shift_first, gain_second, shift_second = (
        smalls[:, index].astype(wide) for index in range(4)
    )
    router_full = smalls[:, 4:]
    inner_part = lax.all_to_all(w_in.astype(low), "shard", split_axis=2, concat_axis=0, tiled=True)
    outer_part = w_out.astype(low)
    upstream_all = gathered(cotangent).reshape(group, rows, model_width)
    flat_slots = jnp.where(kept_mask == 1, expert_index * CAP + slot_index, -1)
    slots_all = gathered(flat_slots).reshape(group, rows, 2)
    slot_numbers = jnp.arange(experts * CAP, dtype=jnp.int32)
    picks = slots_all[:, None, :, :] == slot_numbers[None, :, None, None]
    placed = jnp.any(picks, axis=-1)
    placed_low = placed.astype(low)

    inputs = tokens.astype(wide)
    normed_one, inverse_one = normalize(inputs)
    ln_one = (normed_one * gain_first + shift_first).astype(low)
    triple = jnp.dot(ln_one, qkv_full, preferred_element_type=wide).astype(low)
    queries = to_heads(triple[:, :model_width], images)
    key_rows = to_heads(triple[:, model_width : 2 * model_width], images)
    value_rows = to_heads(triple[:, 2 * model_width :], images)
    scores = (
        jnp.einsum("ishd,ithd->ihst", queries, key_rows, preferred_element_type=wide) * score_scale
    )
    attn_probs = jax.nn.softmax(scores, axis=-1)
    mixed_heads = (
        jnp.einsum(
            "ihst,ithd->ishd", attn_probs.astype(low), value_rows, preferred_element_type=wide
        )
        .reshape(-1, model_width)
        .astype(low)
    )
    residual = inputs + jnp.dot(mixed_heads, proj_full, preferred_element_type=wide)
    normed_two, inverse_two = normalize(residual)
    ln_two = (normed_two * gain_second + shift_second).astype(low)
    ln_two_all = gathered(ln_two).reshape(group, rows, model_width)
    logits = jnp.einsum("btd,de->bte", ln_two_all, router_full, preferred_element_type=wide)
    probs_all = jax.nn.softmax(logits, axis=-1)
    me = lax.axis_index("shard")
    router_probs = lax.dynamic_index_in_dim(probs_all, me, 0, keepdims=False)
    placed_own = lax.dynamic_index_in_dim(placed, me, 0, keepdims=False).astype(wide)
    probs_slots = jnp.repeat(jnp.transpose(probs_all, (0, 2, 1)), CAP, axis=1)
    gate_slots = jnp.sum(placed.astype(wide) * probs_slots, axis=-1)

    def to_slots(values):
        return jnp.einsum("bst,btd->bsd", placed_low, values, preferred_element_type=wide)

    def to_experts(values):
        width = values.shape[-1]
        return jnp.transpose(values.reshape(group, experts, CAP, width), (1, 0, 2, 3)).reshape(
            experts, group * CAP, width
        )

    def from_experts(values):
        width = values.shape[-1]
        return jnp.transpose(values.reshape(experts, group, CAP, width), (1, 0, 2, 3)).reshape(
            group, experts * CAP, width
        )

    def to_tokens(values):
        return jnp.einsum("bst,bsd->btd", placed_low, values, preferred_element_type=wide)

    dispatched = to_experts(to_slots(ln_two_all).astype(low))
    upstream_slots = to_slots(upstream_all)
    outer_grad = to_experts((upstream_slots * gate_slots[:, :, None]).astype(low))
    hidden_pre = jnp.einsum("ecd,def->ecf", dispatched, inner_part, preferred_element_type=wide)
    hidden_act, gelu_pull = jax.vjp(jax.nn.gelu, hidden_pre)
    active = hidden_act.astype(low)
    outer_wgrad = jnp.einsum("ecf,ecd->fed", active, outer_grad, preferred_element_type=wide)
    outer_owned = lax.psum(outer_wgrad.astype(low), "rep").astype(wide)
    active_grad = jnp.einsum("ecd,fed->ecf", outer_grad, outer_part, preferred_element_type=wide)
    inner_grad = gelu_pull(active_grad)[0].astype(low)
    inner_wgrad = jnp.einsum("ecd,ecf->def", dispatched, inner_grad, preferred_element_type=wide)
    inner_rows = lax.all_to_all(
        inner_wgrad.astype(low).reshape(group, -1, experts, inner_part.shape[2]),
        "shard",
        split_axis=0,
        concat_axis=0,
        tiled=True,
    )
    slot_grad = from_experts(
        jnp.einsum("ecf,def->ecd", inner_grad, inner_part, preferred_element_type=wide).astype(low)
    )

    def scattered(values):
        return lax.psum_scatter(values, "shard", scatter_dimension=0, tiled=True)

    raise_grad = scattered(to_tokens(slot_grad).astype(low).reshape(-1, model_width)).astype(wide)
    expert_out = from_experts(
        jnp.einsum("ecf,fed->ecd", active, outer_part, preferred_element_type=wide)
    )
    mixture = scattered(
        to_tokens((expert_out * gate_slots[:, :, None]).astype(low))
        .astype(low)
        .reshape(-1, model_width)
    )
    output = (residual + mixture.astype(wide)).astype(low)
    gate_part = scattered(jnp.sum(expert_out * upstream_slots, axis=-1)).reshape(experts * CAP)
    prob_grad = jnp.transpose(
        jnp.sum((placed_own * gate_part[:, None]).reshape(experts, CAP, rows), axis=1)
    )
    upstream = cotangent.astype(wide)
    logit_grad = (
        router_probs * (prob_grad - jnp.sum(router_probs * prob_grad, axis=-1, keepdims=True))
    ).astype(low)
    ln_two_grad = raise_grad + jnp.einsum(
        "te,de->td", logit_grad, router_full, preferred_element_type=wide
    )
    router_wgrad = jnp.einsum("td,te->de", ln_two, logit_grad, preferred_element_type=wide)
    gain_two_grad = jnp.sum(ln_two_grad * normed_two, axis=0)
    shift_two_grad = jnp.sum(ln_two_grad, axis=0)
    residual_grad = upstream + norm_back(ln_two_grad * gain_second, normed_two, inverse_two)
    attn_grad = residual_grad.astype(low)
    proj_wgrad = jnp.einsum("tc,td->cd", mixed_heads, attn_grad, preferred_element_type=wide)
    mixed_grad = to_heads(
        jnp.einsum("td,cd->tc", attn_grad, proj_full, preferred_element_type=wide).astype(low),
        images,
    )
    value_grad = jnp.einsum(
        "ihst,ishd->ithd", attn_probs.astype(low), mixed_grad, preferred_element_type=wide
    )
    prob_attn_grad = jnp.einsum(
        "ishd,ithd->ihst", mixed_grad, value_rows, preferred_element_type=wide
    )
    score_grad = (
        attn_probs
        * (prob_attn_grad - jnp.sum(attn_probs * prob_attn_grad, axis=-1, keepdims=True))
        * score_scale
    ).astype(low)
    query_grad = jnp.einsum("ihst,ithd->ishd", score_grad, key_rows, preferred_element_type=wide)
    key_grad = jnp.einsum("ihst,ishd->ithd", score_grad, queries, preferred_element_type=wide)
    triple_grad = jnp.concatenate(
        [
            query_grad.reshape(-1, model_width),
            key_grad.reshape(-1, model_width),
            value_grad.reshape(-1, model_width),
        ],
        axis=1,
    ).astype(low)
    qkv_wgrad = jnp.einsum("tc,td->cd", ln_one, triple_grad, preferred_element_type=wide)
    ln_one_grad = jnp.einsum("td,cd->tc", triple_grad, qkv_full, preferred_element_type=wide)
    gain_one_grad = jnp.sum(ln_one_grad * normed_one, axis=0)
    shift_one_grad = jnp.sum(ln_one_grad, axis=0)
    input_grad = (
        residual_grad + norm_back(ln_one_grad * gain_first, normed_one, inverse_one)
    ).astype(low)
    small_grads = jnp.concatenate(
        [
            jnp.stack([gain_one_grad, shift_one_grad, gain_two_grad, shift_two_grad], axis=1),
            router_wgrad,
        ],
        axis=1,
    )
    attn_shares = scattered(jnp.concatenate([qkv_wgrad, proj_wgrad, small_grads], axis=1).astype(low))
    inner_flat, attn_total = lax.psum((inner_rows, attn_shares), "rep")
    inner_owned = jnp.transpose(inner_flat.astype(wide), (1, 2, 0, 3)).reshape(w_in.shape)
    attn_total = attn_total.astype(wide)
    wide_end = w_qkv.shape[1]
    small_end = wide_end + model_width
    return (
        output,
        input_grad,
        attn_total[:, small_end],
        attn_total[:, small_end + 1],
        attn_total[:, :wide_end],
        attn_total[:, wide_end:small_end],
        attn_total[:, small_end + 2],
        attn_total[:, small_end + 3],
        attn_total[:, small_end + 4 :],
        inner_owned,
        outer_owned,
    )


def solution(mesh):
    return jax.shard_map(
        shards,
        mesh=mesh,
        in_specs=(
            P(("shard", "rep"), None),
            P(("shard", "rep"), None),
            P(("shard", "rep"), None),
            P(("shard", "rep"), None),
            P(("shard", "rep"), None),
            P("shard"),
            P("shard"),
            P("shard", None),
            P("shard", None),
            P("shard"),
            P("shard"),
            P("shard", None),
            P("shard", None, None),
            P("shard", None, None),
        ),
        out_specs=(
            P(("shard", "rep"), None),
            P(("shard", "rep"), None),
            P("shard"),
            P("shard"),
            P("shard", None),
            P("shard", None),
            P("shard"),
            P("shard"),
            P("shard", None),
            P("shard", None, None),
            P("shard", None, None),
        ),
        check_vma=False,
    )
```

```python
import jax
import jax.numpy as jnp
from jax import lax
from jax.experimental import pallas as pl
from jax.experimental.pallas import tpu as pltpu
from jax.sharding import PartitionSpec as P

MESH = pl.DeviceIdType.MESH
VMEM_BYTES = 64 * 1024 * 1024 - 256 * 1024

HEADS = 12
HEAD_DIM = 64
SEQ = 197
CAP = 112


epsilon = 1e-06
score_scale = 0.125


def normalize(inputs):
    centred = inputs - jnp.mean(inputs, axis=-1, keepdims=True)
    inverse = lax.rsqrt(jnp.mean(centred * centred, axis=-1, keepdims=True) + epsilon)
    return (centred * inverse, inverse)


def norm_back(upstream, normed, inverse):
    return inverse * (
        upstream
        - jnp.mean(upstream, axis=-1, keepdims=True)
        - normed * jnp.mean(upstream * normed, axis=-1, keepdims=True)
    )


def to_heads(matrix, images):
    return matrix.reshape(images, -1, HEADS, HEAD_DIM)


def shards(
    tokens,
    cotangent,
    expert_index,
    slot_index,
    kept_mask,
    gain_attn,
    shift_attn,
    w_qkv,
    w_proj,
    gain_moe,
    shift_moe,
    w_router,
    w_in,
    w_out,
):
    model_width = tokens.shape[1]
    images = tokens.shape[0] // SEQ
    rows = tokens.shape[0]
    experts = w_in.shape[1]
    group = lax.axis_size("shard")
    low = jnp.bfloat16
    wide = jnp.float32

    def gathered(value):
        return lax.all_gather(value, "shard", axis=0, tiled=True)

    qkv_full = gathered(w_qkv.astype(low))
    proj_full = gathered(w_proj.astype(low))
    smalls = gathered(
        jnp.concatenate(
            [
                jnp.stack([gain_attn, shift_attn, gain_moe, shift_moe], axis=1),
                w_router,
            ],
            axis=1,
        ).astype(low)
    )
    gain_first, shift_first, gain_second, shift_second = (
        smalls[:, index].astype(wide) for index in range(4)
    )
    router_full = smalls[:, 4:]
    inner_part = lax.all_to_all(w_in.astype(low), "shard", split_axis=2, concat_axis=0, tiled=True)
    outer_part = w_out.astype(low)
    upstream_all = gathered(cotangent).reshape(group, rows, model_width)
    flat_slots = jnp.where(kept_mask == 1, expert_index * CAP + slot_index, -1)
    slots_all = gathered(flat_slots).reshape(group, rows, 2)
    slot_numbers = jnp.arange(experts * CAP, dtype=jnp.int32)
    picks = slots_all[:, None, :, :] == slot_numbers[None, :, None, None]
    placed = jnp.any(picks, axis=-1)
    placed_low = placed.astype(low)

    inputs = tokens.astype(wide)
    normed_one, inverse_one = normalize(inputs)
    ln_one = (normed_one * gain_first + shift_first).astype(low)
    triple = jnp.dot(ln_one, qkv_full, preferred_element_type=wide).astype(low)
    queries = to_heads(triple[:, :model_width], images)
    key_rows = to_heads(triple[:, model_width : 2 * model_width], images)
    value_rows = to_heads(triple[:, 2 * model_width :], images)
    scores = (
        jnp.einsum("ishd,ithd->ihst", queries, key_rows, preferred_element_type=wide) * score_scale
    )
    attn_probs = jax.nn.softmax(scores, axis=-1)
    mixed_heads = (
        jnp.einsum(
            "ihst,ithd->ishd", attn_probs.astype(low), value_rows, preferred_element_type=wide
        )
        .reshape(-1, model_width)
        .astype(low)
    )
    residual = inputs + jnp.dot(mixed_heads, proj_full, preferred_element_type=wide)
    normed_two, inverse_two = normalize(residual)
    ln_two = (normed_two * gain_second + shift_second).astype(low)
    ln_two_all = gathered(ln_two).reshape(group, rows, model_width)
    logits = jnp.einsum("btd,de->bte", ln_two_all, router_full, preferred_element_type=wide)
    probs_all = jax.nn.softmax(logits, axis=-1)
    me = lax.axis_index("shard")
    router_probs = lax.dynamic_index_in_dim(probs_all, me, 0, keepdims=False)
    placed_own = lax.dynamic_index_in_dim(placed, me, 0, keepdims=False).astype(wide)
    probs_slots = jnp.repeat(jnp.transpose(probs_all, (0, 2, 1)), CAP, axis=1)
    gate_slots = jnp.sum(placed.astype(wide) * probs_slots, axis=-1)

    def to_slots(values):
        return jnp.einsum("bst,btd->bsd", placed_low, values, preferred_element_type=wide)

    def to_experts(values):
        width = values.shape[-1]
        return jnp.transpose(values.reshape(group, experts, CAP, width), (1, 0, 2, 3)).reshape(
            experts, group * CAP, width
        )

    def from_experts(values):
        width = values.shape[-1]
        return jnp.transpose(values.reshape(experts, group, CAP, width), (1, 0, 2, 3)).reshape(
            group, experts * CAP, width
        )

    def to_tokens(values):
        return jnp.einsum("bst,bsd->btd", placed_low, values, preferred_element_type=wide)

    dispatched = to_experts(to_slots(ln_two_all).astype(low))
    upstream_slots = to_slots(upstream_all)
    outer_grad = to_experts((upstream_slots * gate_slots[:, :, None]).astype(low))
    hidden_pre = jnp.einsum("ecd,def->ecf", dispatched, inner_part, preferred_element_type=wide)
    hidden_act, gelu_pull = jax.vjp(jax.nn.gelu, hidden_pre)
    active = hidden_act.astype(low)
    outer_wgrad = jnp.einsum("ecf,ecd->fed", active, outer_grad, preferred_element_type=wide)
    outer_owned = lax.psum(outer_wgrad.astype(low), "rep").astype(wide)
    active_grad = jnp.einsum("ecd,fed->ecf", outer_grad, outer_part, preferred_element_type=wide)
    inner_grad = gelu_pull(active_grad)[0].astype(low)
    inner_wgrad = jnp.einsum("ecd,ecf->def", dispatched, inner_grad, preferred_element_type=wide)
    inner_rows = lax.all_to_all(
        inner_wgrad.astype(low).reshape(group, -1, experts, inner_part.shape[2]),
        "shard",
        split_axis=0,
        concat_axis=0,
        tiled=True,
    )
    slot_grad = from_experts(
        jnp.einsum("ecf,def->ecd", inner_grad, inner_part, preferred_element_type=wide).astype(low)
    )

    def scattered(values):
        return lax.psum_scatter(values, "shard", scatter_dimension=0, tiled=True)

    raise_grad = scattered(to_tokens(slot_grad).astype(low).reshape(-1, model_width)).astype(wide)
    expert_out = from_experts(
        jnp.einsum("ecf,fed->ecd", active, outer_part, preferred_element_type=wide)
    )
    mixture = scattered(
        to_tokens((expert_out * gate_slots[:, :, None]).astype(low))
        .astype(low)
        .reshape(-1, model_width)
    )
    output = (residual + mixture.astype(wide)).astype(low)
    gate_part = scattered(jnp.sum(expert_out * upstream_slots, axis=-1)).reshape(experts * CAP)
    prob_grad = jnp.transpose(
        jnp.sum((placed_own * gate_part[:, None]).reshape(experts, CAP, rows), axis=1)
    )
    upstream = cotangent.astype(wide)
    logit_grad = (
        router_probs * (prob_grad - jnp.sum(router_probs * prob_grad, axis=-1, keepdims=True))
    ).astype(low)
    ln_two_grad = raise_grad + jnp.einsum(
        "te,de->td", logit_grad, router_full, preferred_element_type=wide
    )
    router_wgrad = jnp.einsum("td,te->de", ln_two, logit_grad, preferred_element_type=wide)
    gain_two_grad = jnp.sum(ln_two_grad * normed_two, axis=0)
    shift_two_grad = jnp.sum(ln_two_grad, axis=0)
    residual_grad = upstream + norm_back(ln_two_grad * gain_second, normed_two, inverse_two)
    attn_grad = residual_grad.astype(low)
    proj_wgrad = jnp.einsum("tc,td->cd", mixed_heads, attn_grad, preferred_element_type=wide)
    mixed_grad = to_heads(
        jnp.einsum("td,cd->tc", attn_grad, proj_full, preferred_element_type=wide).astype(low),
        images,
    )
    value_grad = jnp.einsum(
        "ihst,ishd->ithd", attn_probs.astype(low), mixed_grad, preferred_element_type=wide
    )
    prob_attn_grad = jnp.einsum(
        "ishd,ithd->ihst", mixed_grad, value_rows, preferred_element_type=wide
    )
    score_grad = (
        attn_probs
        * (prob_attn_grad - jnp.sum(attn_probs * prob_attn_grad, axis=-1, keepdims=True))
        * score_scale
    ).astype(low)
    query_grad = jnp.einsum("ihst,ithd->ishd", score_grad, key_rows, preferred_element_type=wide)
    key_grad = jnp.einsum("ihst,ishd->ithd", score_grad, queries, preferred_element_type=wide)
    triple_grad = jnp.concatenate(
        [
            query_grad.reshape(-1, model_width),
            key_grad.reshape(-1, model_width),
            value_grad.reshape(-1, model_width),
        ],
        axis=1,
    ).astype(low)
    qkv_wgrad = jnp.einsum("tc,td->cd", ln_one, triple_grad, preferred_element_type=wide)
    ln_one_grad = jnp.einsum("td,cd->tc", triple_grad, qkv_full, preferred_element_type=wide)
    gain_one_grad = jnp.sum(ln_one_grad * normed_one, axis=0)
    shift_one_grad = jnp.sum(ln_one_grad, axis=0)
    input_grad = (
        residual_grad + norm_back(ln_one_grad * gain_first, normed_one, inverse_one)
    ).astype(low)
    small_grads = jnp.concatenate(
        [
            jnp.stack([gain_one_grad, shift_one_grad, gain_two_grad, shift_two_grad], axis=1),
            router_wgrad,
        ],
        axis=1,
    )
    attn_shares = scattered(jnp.concatenate([qkv_wgrad, proj_wgrad, small_grads], axis=1).astype(low))
    inner_flat, attn_total = lax.psum((inner_rows, attn_shares), "rep")
    inner_owned = jnp.transpose(inner_flat.astype(wide), (1, 2, 0, 3)).reshape(w_in.shape)
    attn_total = attn_total.astype(wide)
    wide_end = w_qkv.shape[1]
    small_end = wide_end + model_width
    return (
        output,
        input_grad,
        attn_total[:, small_end],
        attn_total[:, small_end + 1],
        attn_total[:, :wide_end],
        attn_total[:, wide_end:small_end],
        attn_total[:, small_end + 2],
        attn_total[:, small_end + 3],
        attn_total[:, small_end + 4 :],
        inner_owned,
        outer_owned,
    )


TILE_ROWS = 256
SENT_ROWS = 208
TABLE_ROW = 200
PIECE = 96
NEGATIVE = -1e30


def mega(
    tok_ref,
    ups_ref,
    small_ref,
    qkv_ref,
    proj_ref,
    inner_hbm,
    outer_ref,
    out_ref,
    igrad_ref,
    go_hbm,
    gi_hbm,
    ga_hbm,
    smalls,
    small_sum,
    wq,
    wp,
    win,
    normed_a,
    inv_a,
    ln_a,
    tri,
    probs,
    heads,
    resid,
    mean_m,
    inv_m,
    rows_buf,
    onehot,
    work,
    og,
    route,
    act,
    slope,
    route_grad,
    st_back,
    sr_back,
    rr_back,
    sr_out,
    rr_out,
    grad_in,
    grad_in_own,
    grad_out,
    grad_attn,
    mid_in,
    mid_out,
    mid_attn,
    end_in,
    end_out,
    end_attn,
    res_grad,
    agrad,
    mgrad,
    small_grad,
    small_swap,
    send_sems,
    recv_sems,
    local_sems,
):
    low = jnp.bfloat16
    wide = jnp.float32
    width = tok_ref.shape[1]
    shard = lax.axis_index("shard")
    rep = lax.axis_index("rep")

    def flip(j):
        out = shard
        for bit in range(3):
            if (j >> bit) & 1:
                out = out + (1 - 2 * ((shard // (1 << bit)) % 2)) * (1 << bit)
        return out

    peers = [flip(j) for j in range(8)]
    pair = rep + 1 - 2 * (rep % 2)
    across = 3 - rep
    is_mid = jnp.logical_and(rep >= 1, rep <= 2)
    is_end = jnp.logical_not(is_mid)

    ups_base = 8 * TILE_ROWS
    for position in range(16):
        rows_buf[pl.ds(position * TILE_ROWS + SENT_ROWS, TILE_ROWS - SENT_ROWS), :] = jnp.zeros(
            (TILE_ROWS - SENT_ROWS, width), low
        )
    barrier = pltpu.get_barrier_semaphore()
    for j in range(1, 8):
        pl.semaphore_signal(barrier, inc=1, device_id=(peers[j], rep), device_id_type=MESH)
    pl.semaphore_signal(barrier, inc=1, device_id=(shard, pair), device_id_type=MESH)

    @pl.when(is_mid)
    def _():
        pl.semaphore_signal(barrier, inc=1, device_id=(shard, across), device_id_type=MESH)
        pl.semaphore_wait(barrier, 9)

    @pl.when(is_end)
    def _():
        pl.semaphore_wait(barrier, 8)

    count = [0]
    unsent = []
    settled = []

    def describe(src, dst, device):
        index = count[0]
        count[0] += 1
        return pltpu.make_async_remote_copy(
            src_ref=src,
            dst_ref=dst,
            send_sem=send_sems.at[index],
            recv_sem=recv_sems.at[index],
            device_id=device,
            device_id_type=MESH,
        )

    def send(src, dst, j):
        copy = describe(src, dst, (peers[j], rep))
        copy.start()
        unsent.append(copy)
        return copy

    def settle(copies):
        for copy in copies:
            copy.wait_send()
            settled.append(id(copy))

    local_count = [0]

    def local(src, dst):
        copy = pltpu.make_async_copy(src, dst, local_sems.at[local_count[0]])
        local_count[0] += 1
        copy.start()
        return copy

    def off(value, unit):
        return pl.multiple_of(value * unit, unit)

    class Gather:
        def __init__(self, view, first, second):
            self.view, self.first, self.second = view, first, second
            self.all = []

        def put(self, at, to, j, half=None):
            copy = send(self.view(at, at, half), self.view(at, to, half), j)
            self.all.append(copy)
            return copy

        def begin(self):
            self.from_x = self.put(0, 2, 2)
            self.from_y = self.put(0, 4, 4)
            self.from_s = [self.put(0, 1, 1)]

        def pass_on(self):
            self.from_x.wait_recv()
            self.far = [self.put(2, 6, 4, self.first)]
            self.from_s.append(self.put(2, 3, 1))
            self.from_y.wait_recv()
            self.far.append(self.put(4, 6, 2, self.second))
            self.from_s.append(self.put(4, 5, 1))

        def last(self):
            for copy in self.far:
                copy.wait_recv()
            self.from_s.append(self.put(6, 7, 1))

    def weight_view(ref):
        def view(at, to, half):
            start = off(peers[at], PIECE)
            if half is None:
                return ref.at[pl.ds(start, PIECE)]
            return ref.at[pl.ds(start + half[0], half[1])]

        return view

    def row_view(base):
        def view(at, to, half):
            first, size = half if half is not None else (0, SENT_ROWS)
            return rows_buf.at[pl.ds(base + to * TILE_ROWS + first, size)]

        return view

    own_rows = pl.ds(off(shard, PIECE), PIECE)
    small_copies = []
    smalls[0] = small_ref[...]
    for j in range(1, 8):
        small_copies.append(send(smalls.at[0], smalls.at[j], j))
    wq[own_rows, :] = qkv_ref[...].astype(low)
    gather_q = Gather(weight_view(wq), (0, 48), (48, 48))
    gather_q.begin()
    wp[own_rows, :] = proj_ref[...].astype(low)
    rows_buf[ups_base : ups_base + SENT_ROWS, :] = ups_ref[...]
    inputs = tok_ref[...].astype(wide)
    normed, inverse = normalize(inputs)
    normed_a[...] = normed
    inv_a[...] = inverse
    gather_q.pass_on()
    gather_p = Gather(weight_view(wp), (0, 48), (48, 48))
    gather_p.begin()
    part = win.shape[2]
    inner_copies = [
        send(
            inner_hbm.at[:, :, pl.ds(off(peers[j], part), part)],
            win.at[:, own_rows, :],
            j,
        )
        for j in range(1, 8)
    ]
    inner_own = local(inner_hbm.at[:, :, pl.ds(off(shard, part), part)], win.at[:, own_rows, :])
    gather_u = Gather(row_view(ups_base), (0, 112), (112, 96))
    gather_u.begin()
    for copy in small_copies:
        copy.wait_recv()
    total = smalls[0].astype(wide)
    for j in range(1, 8):
        total = total + smalls[j].astype(wide)
    small_sum[...] = total
    gain_first, shift_first = small_sum[3:4, :], small_sum[4:5, :]
    gain_second, shift_second = small_sum[5:6, :], small_sum[6:7, :]
    ln_a[...] = (normed_a[...] * gain_first + shift_first).astype(low)
    gather_q.last()
    for copy in gather_q.from_s:
        copy.wait_recv()

    def triple_step(i, carry):
        columns = pl.ds(off(i, 384), 384)
        tri[:, columns] = jnp.dot(
            ln_a[...], wq[:, columns], preferred_element_type=wide
        ).astype(low)
        return carry

    lax.fori_loop(0, 6, triple_step, 0)

    lane = lax.broadcasted_iota(jnp.int32, (TILE_ROWS, 128), 1)
    key_at = lax.broadcasted_iota(jnp.int32, (TILE_ROWS, TILE_ROWS), 1)

    def head_columns(p, third):
        return pl.ds(pl.multiple_of(third * width + p * 128, 128), 128)

    def contract(a, b, da, db):
        return lax.dot_general(a, b, (((da,), (db,)), ((), ())), preferred_element_type=wide)

    def one_head(values, side):
        return jnp.where((lane < 64) == (side == 0), values, jnp.zeros_like(values))

    def attend(p, carry):
        queries = tri[:, head_columns(p, 0)]
        key_rows = tri[:, head_columns(p, 1)]
        value_rows = tri[:, head_columns(p, 2)]
        mixed = []
        for side in range(2):
            scores = contract(one_head(queries, side), key_rows, 1, 1) * score_scale
            scores = jnp.where(key_at < SEQ, scores, NEGATIVE)
            powers = jnp.exp(scores - jnp.max(scores, axis=-1, keepdims=True))
            weights = powers / jnp.sum(powers, axis=-1, keepdims=True)
            probs[2 * p + side] = weights
            mixed.append(jnp.dot(weights.astype(low), value_rows, preferred_element_type=wide))
        heads[:, head_columns(p, 0)] = jnp.where(lane < 64, mixed[0], mixed[1]).astype(low)
        return carry

    lax.fori_loop(0, 3, attend, 0)
    gather_p.pass_on()
    lax.fori_loop(3, 6, attend, 0)
    gather_u.pass_on()
    gather_p.last()
    for copy in gather_p.from_s:
        copy.wait_recv()
    residual = tok_ref[...].astype(wide) + jnp.dot(
        heads[...], wp[...], preferred_element_type=wide
    )
    resid[...] = residual
    normed, inverse = normalize(residual)
    mean_m[...] = jnp.mean(residual, axis=-1, keepdims=True)
    inv_m[...] = inverse
    ln_two = (normed * gain_second + shift_second).astype(low)
    rows_buf[0:SENT_ROWS, :] = ln_two[0:SENT_ROWS, :]
    gather_l = Gather(row_view(0), (0, 112), (112, 96))
    gather_l.begin()
    gather_u.last()
    for copy in gather_u.from_s:
        copy.wait_recv()

    slots = onehot.shape[1]
    slot_at = lax.broadcasted_iota(jnp.int32, (slots, TILE_ROWS), 0).astype(wide)

    def route_step(j, carry):
        start = pl.multiple_of(ups_base + j * TILE_ROWS + 192, 16)
        table = rows_buf[pl.ds(start, 16), :].astype(wide)
        first = table[8:9, 0:256] * CAP + table[8:9, 256:512]
        second = table[9:10, 0:256] * CAP + table[9:10, 256:512]
        hit = jnp.logical_or(slot_at == first, slot_at == second)
        onehot[j] = jnp.where(hit, 1.0, 0.0).astype(low)
        return carry

    lax.fori_loop(0, 8, route_step, 0)
    router = small_sum[...].astype(low)
    lane16 = lax.broadcasted_iota(jnp.int32, (slots, 16), 1)
    expert_of = lax.broadcasted_iota(jnp.int32, (slots, 16), 0)
    own_lane = jnp.logical_and(expert_of >= lane16 * CAP, expert_of < lane16 * CAP + CAP)
    experts = win.shape[0]

    def expert_rows(e, j, blocks=1):
        return pl.ds(pl.multiple_of((e * 8 + j) * CAP, 16), blocks * CAP)

    def dispatch_step(j, carry):
        picks = onehot[j]
        ln_rows = rows_buf[pl.ds(off(j, TILE_ROWS), TILE_ROWS), :]
        up_rows = rows_buf[pl.ds(pl.multiple_of(ups_base + j * TILE_ROWS, 16), TILE_ROWS), :]
        sent = jnp.dot(picks, ln_rows, preferred_element_type=wide).astype(low)
        logits = jnp.where(lane16 < experts, contract(sent, router, 1, 1), NEGATIVE)
        powers = jnp.exp(logits - jnp.max(logits, axis=-1, keepdims=True))
        chances = powers / jnp.sum(powers, axis=-1, keepdims=True)
        gate = jnp.sum(jnp.where(own_lane, chances, 0.0), axis=-1, keepdims=True)
        ups = jnp.dot(picks, up_rows, preferred_element_type=wide)
        upward = (ups * gate).astype(low)
        for e in range(experts):
            rows = expert_rows(e, j)
            work[rows, :] = sent[e * CAP : (e + 1) * CAP]
            og[rows, :] = upward[e * CAP : (e + 1) * CAP]
            route[rows, :] = chances[e * CAP : (e + 1) * CAP]
        return carry

    def hidden_step(g):
        def step(e, carry):
            rows = pl.ds(g * 2 * CAP, 2 * CAP)
            sent = work[expert_rows(e, 2 * g, 2), :]
            value = jnp.dot(sent, win[e], preferred_element_type=wide)
            square = value * value
            bend = jnp.tanh(0.7978845608028654 * value * (1.0 + 0.044715 * square))
            act[e, rows, :] = (0.5 * value * (1.0 + bend)).astype(low)
            slope[e, rows, :] = (
                0.5 * (1.0 + bend)
                + 0.5
                * value
                * (1.0 - bend * bend)
                * (0.7978845608028654 * (1.0 + 0.134145 * square))
            ).astype(low)
            return carry

        lax.fori_loop(0, experts, step, 0)

    inner_own.wait()
    for copy in inner_copies:
        copy.wait_recv()
    gather_l.pass_on()
    gather_l.from_s[0].wait_recv()
    lax.fori_loop(0, 2, dispatch_step, 0)
    hidden_step(0)
    gather_l.last()
    for g in range(1, 4):
        gather_l.from_s[g].wait_recv()
        lax.fori_loop(2 * g, 2 * g + 2, dispatch_step, 0)
        hidden_step(g)

    class Copies:
        def __init__(self, own, mid, end, out, rows):
            self.own, self.mid, self.end, self.out, self.rows = own, mid, end, out, rows
            self.up = describe(own, end, (shard, pair))
            self.over = describe(own, mid, (shard, across))
            self.down = describe(end, end, (shard, pair))

        def add(self, target, other):
            size = self.rows

            def step(i, carry):
                at = pl.ds(pl.multiple_of(i * size, 16), size)
                target[at, :] = (
                    self.own[at, :].astype(wide) + other[at, :].astype(wide)
                ).astype(low)
                return carry

            lax.fori_loop(0, target.shape[0] // size, step, 0)

        def rise(self):
            @pl.when(is_end)
            def _():
                self.up.start()

        def cross(self):
            @pl.when(is_mid)
            def _():
                self.up.wait_recv()
                self.add(self.own, self.end)
                self.over.start()

        def fall(self):
            @pl.when(is_mid)
            def _():
                self.over.wait_recv()
                self.add(self.end, self.mid)
                self.down.start()

        def finish(self):
            @pl.when(is_end)
            def _():
                self.up.wait_send()
                self.down.wait_recv()

            write = local(self.end, self.out)

            @pl.when(is_mid)
            def _():
                self.over.wait_send()
                self.down.wait_send()

            write.wait()

    out_copies = [
        Copies(grad_out.at[e], mid_out.at[e], end_out.at[e], go_hbm.at[e], 64) for e in range(experts)
    ]
    in_copies = [
        Copies(grad_in_own.at[e], mid_in.at[e], end_in.at[e], gi_hbm.at[e], 16)
        for e in range(experts)
    ]
    attn_copies = Copies(grad_attn, mid_attn, end_attn, ga_hbm, 80)

    for e in range(experts):
        grad_out[e] = contract(act[e], og[expert_rows(e, 0, 8), :], 0, 0).astype(low)
        out_copies[e].rise()

    settle(gather_l.all)
    settle(gather_u.all)
    route_grad[...] = jnp.zeros(route_grad.shape, wide)
    half = act.shape[1] // 2
    lane_h = lax.broadcasted_iota(jnp.int32, (half, 16), 1)

    def back_step(i, carry):
        e = i // 2
        rows = pl.ds(off(i % 2, half), half)
        flat = pl.ds(pl.multiple_of(i * half, 16), half)
        upward = og[flat, :]
        gone = jnp.dot(act[e, rows, :], outer_ref[e], preferred_element_type=wide)
        chances = route[flat, :]
        gate = jnp.sum(jnp.where(lane_h == e, chances, 0.0), axis=-1, keepdims=True)
        pull = jnp.sum(upward.astype(wide) * gone, axis=-1, keepdims=True)
        logit = (pull * (jnp.where(lane_h == e, 1.0, 0.0) - chances)).astype(low)
        logit = jnp.where(lane_h < experts, logit, jnp.zeros_like(logit))
        rows_buf[flat, :] = (gone * gate).astype(low)
        inner = contract(upward, outer_ref[e], 1, 1) * slope[e, rows, :].astype(wide)
        inner = inner.astype(low)
        slope[e, rows, :] = inner
        og[flat, :] = (
            contract(inner, win[e], 1, 1) + jnp.dot(logit, router, preferred_element_type=wide)
        ).astype(low)
        route_grad[...] += contract(logit, work[flat, :], 0, 0)
        return carry

    lax.fori_loop(0, 2 * experts, back_step, 0)

    def combine_back(j):
        joined = jnp.concatenate([og[expert_rows(e, j), :] for e in range(experts)], axis=0)
        return contract(onehot[j], joined, 0, 0)[0:SENT_ROWS]

    def combine_out(j):
        joined = jnp.concatenate(
            [rows_buf[expert_rows(e, j), :] for e in range(experts)], axis=0
        )
        return contract(onehot[j], joined, 0, 0)[0:SENT_ROWS]

    stage_out = experts * 8 * CAP

    def odd_back(i, carry):
        st_back[i] = combine_back(2 * i + 1).astype(low)
        return carry

    lax.fori_loop(0, 4, odd_back, 0)
    swap_back = send(st_back, sr_back, 1)

    def inner_grad_step(e, carry):
        grad_in[e] = contract(work[expert_rows(e, 0, 8), :], slope[e], 0, 0).astype(low)
        return carry

    lax.fori_loop(0, experts, inner_grad_step, 0)
    swap_back.wait_recv()

    def even_back(i, carry):
        sr_back[i] = (combine_back(2 * i) + sr_back[i].astype(wide)).astype(low)
        return carry

    lax.fori_loop(0, 4, even_back, 0)
    back_copies = [send(sr_back.at[i], rr_back.at[i - 1], 2 * i) for i in range(1, 4)]
    grad_in_copies = [
        send(
            grad_in.at[:, pl.ds(off(peers[j], PIECE), PIECE), :],
            grad_in_own.at[:, :, pl.ds(off(shard, part), part)],
            j,
        )
        for j in range(1, 8)
    ]
    grad_in_local = local(
        grad_in.at[:, own_rows, :], grad_in_own.at[:, :, pl.ds(off(shard, part), part)]
    )

    def odd_out(i, carry):
        rows = pl.ds(pl.multiple_of(stage_out + i * SENT_ROWS, 16), SENT_ROWS)
        rows_buf[rows, :] = combine_out(2 * i + 1).astype(low)
        return carry

    lax.fori_loop(0, 4, odd_out, 0)
    swap_out = send(rows_buf.at[pl.ds(stage_out, 4 * SENT_ROWS)], sr_out, 1)
    out_copies[0].cross()
    swap_out.wait_recv()

    def even_out(i, carry):
        rows = pl.ds(off(i, SENT_ROWS), SENT_ROWS)
        sr_out[rows, :] = (combine_out(2 * i) + sr_out[rows, :].astype(wide)).astype(low)
        return carry

    lax.fori_loop(0, 4, even_out, 0)

    for copy in back_copies:
        copy.wait_recv()
    out_sends = [
        send(sr_out.at[pl.ds(i * SENT_ROWS, SENT_ROWS)], rr_out.at[i - 1], 2 * i)
        for i in range(1, 4)
    ]
    ln_grad = sr_back[0].astype(wide)
    for i in range(3):
        ln_grad = ln_grad + rr_back[i].astype(wide)
    normed = (resid[0:SENT_ROWS, :] - mean_m[0:SENT_ROWS, :]) * inv_m[0:SENT_ROWS, :]
    gain_m_grad = jnp.sum(ln_grad * normed, axis=0, keepdims=True)
    shift_m_grad = jnp.sum(ln_grad, axis=0, keepdims=True)
    upstream = jnp.where(
        lax.broadcasted_iota(jnp.int32, (SENT_ROWS, width), 0) < SEQ,
        ups_ref[...].astype(wide),
        0.0,
    )
    residual_grad = upstream + norm_back(
        ln_grad * gain_second, normed, inv_m[0:SENT_ROWS, :]
    )
    res_grad[...] = residual_grad
    agrad[...] = jnp.zeros(agrad.shape, low)
    agrad[0:SENT_ROWS, :] = residual_grad.astype(low)
    mgrad[...] = contract(agrad[...], wp[...], 1, 1).astype(low)

    def grad_rows(part, j):
        return pl.ds(pl.multiple_of(part * width + peers[j] * PIECE, 16), PIECE)

    def kept_rows(part, i):
        return pl.ds((i * 4 + part) * PIECE, PIECE)

    def come_rows(part, i):
        return pl.ds((16 + i * 4 + part) * PIECE, PIECE)

    def share(part):
        return [
            send(work.at[grad_rows(part, 2 * i + 1)], og.at[kept_rows(part, i)], 1)
            for i in range(4)
        ]

    def gather_share(part, copies):
        sent = []
        for i in range(4):
            copies[i].wait_recv()
            rows = kept_rows(part, i)
            og[rows, :] = (
                work[grad_rows(part, 2 * i), :].astype(wide) + og[rows, :].astype(wide)
            ).astype(low)
            if i > 0:
                sent.append(send(og.at[rows], og.at[come_rows(part, i - 1)], 2 * i))
        return sent

    def total_share(part, copies):
        total = og[kept_rows(part, 0), :].astype(wide)
        for i in range(3):
            copies[i].wait_recv()
            total = total + og[come_rows(part, i), :].astype(wide)
        grad_attn[pl.ds(part * PIECE, PIECE), :] = total.astype(low)

    def attend_back(p, carry):
        queries = tri[:, head_columns(p, 0)]
        key_rows = tri[:, head_columns(p, 1)]
        value_rows = tri[:, head_columns(p, 2)]
        mixed = mgrad[:, head_columns(p, 0)]
        results = []
        for side in range(2):
            weights = probs[2 * p + side]
            value_grad = contract(weights.astype(low), mixed, 0, 0)
            weight_grad = contract(one_head(mixed, side), value_rows, 1, 1)
            score_grad = (
                weights
                * (weight_grad - jnp.sum(weights * weight_grad, axis=-1, keepdims=True))
                * score_scale
            ).astype(low)
            query_grad = jnp.dot(score_grad, key_rows, preferred_element_type=wide)
            key_grad = contract(score_grad, queries, 0, 0)
            results.append((query_grad, key_grad, value_grad))
        for third in range(3):
            tri[:, head_columns(p, third)] = jnp.where(
                lane < 64, results[0][third], results[1][third]
            ).astype(low)
        return carry

    out_copies[1].cross()
    out_copies[0].fall()
    work[3 * width : 4 * width, :] = contract(heads[...], agrad[...], 0, 0).astype(low)
    share_p = share(3)
    lax.fori_loop(0, 3, attend_back, 0)
    out_copies[2].cross()
    out_copies[1].fall()
    lax.fori_loop(3, 6, attend_back, 0)
    out_copies[2].fall()
    grad_in_local.wait()
    for copy in grad_in_copies:
        copy.wait_recv()
    for e in range(experts):
        in_copies[e].rise()

    def weight_grad_of(part):
        work[part * width : (part + 1) * width, :] = contract(
            ln_a[...], tri[:, part * width : (part + 1) * width], 0, 0
        ).astype(low)

    weight_grad_of(2)
    share_v = share(2)
    come_p = gather_share(3, share_p)
    weight_grad_of(1)
    share_k = share(1)
    come_v = gather_share(2, share_v)
    weight_grad_of(0)
    share_q = share(0)
    come_k = gather_share(1, share_k)
    ln_grad = contract(tri[0:SENT_ROWS, :], wq[...], 1, 1)
    come_q = gather_share(0, share_q)
    normed = normed_a[0:SENT_ROWS, :]
    gain_a_grad = jnp.sum(ln_grad * normed, axis=0, keepdims=True)
    shift_a_grad = jnp.sum(ln_grad, axis=0, keepdims=True)
    row16 = lax.broadcasted_iota(jnp.int32, (16, width), 0)
    small = jnp.where(row16 < experts, route_grad[...], 0.0)
    for row, value in (
        (3, gain_a_grad),
        (4, shift_a_grad),
        (5, gain_m_grad),
        (6, shift_m_grad),
    ):
        small = small + jnp.where(row16 == row, value, 0.0)
    small_grad[0] = small.astype(low)
    swap = send(small_grad.at[0], small_swap.at[0], 1)
    igrad_ref[...] = (
        res_grad[...] + norm_back(ln_grad * gain_first, normed, inv_a[0:SENT_ROWS, :])
    ).astype(low)
    in_copies[0].cross()
    for step in range(2):
        swap.wait_recv()
        small_grad[step + 1] = (
            small_grad[step].astype(wide) + small_swap[step].astype(wide)
        ).astype(low)
        swap = send(small_grad.at[step + 1], small_swap.at[step + 1], 2 << step)
    in_copies[1].cross()
    in_copies[0].fall()
    total_share(3, come_p)
    total_share(2, come_v)
    in_copies[2].cross()
    in_copies[1].fall()
    total_share(1, come_k)
    total_share(0, come_q)
    swap.wait_recv()
    grad_attn[4 * PIECE : 4 * PIECE + 16, :] = (
        small_grad[2].astype(wide) + small_swap[2].astype(wide)
    ).astype(low)
    attn_copies.rise()
    output = resid[0:SENT_ROWS, :] + sr_out[0:SENT_ROWS, :].astype(wide)
    for i in range(3):
        out_sends[i].wait_recv()
        output = output + rr_out[i].astype(wide)
    out_ref[...] = output.astype(low)
    in_copies[2].fall()
    attn_copies.cross()
    attn_copies.fall()
    for copies in out_copies + in_copies + [attn_copies]:
        copies.finish()
    for copy in unsent:
        if id(copy) not in settled:
            copy.wait_send()
def grouped(
    tokens,
    cotangent,
    expert_index,
    slot_index,
    kept_mask,
    gain_attn,
    shift_attn,
    w_qkv,
    w_proj,
    gain_moe,
    shift_moe,
    w_router,
    w_in,
    w_out,
):
    low = jnp.bfloat16
    wide = jnp.float32
    rows, width = tokens.shape
    owned, experts, hidden = w_in.shape
    part = w_out.shape[0]
    shard = lax.axis_index("shard")
    tokens_in = jnp.pad(tokens, ((0, TILE_ROWS - rows), (0, 0)))
    placed = kept_mask == 1
    choice = jnp.pad(
        jnp.where(placed, expert_index, experts), ((0, 256 - rows), (0, 0)), constant_values=experts
    )
    slot = jnp.pad(jnp.where(placed, slot_index, 0), ((0, 256 - rows), (0, 0)))
    table = jnp.concatenate([choice, slot], axis=0).T.astype(low)
    table = jnp.pad(table, ((TABLE_ROW - rows, SENT_ROWS - TABLE_ROW - 2), (0, width - 512)))
    message = jnp.concatenate([cotangent, table], axis=0)
    small = jnp.concatenate(
        [w_router.T, jnp.stack([gain_attn, shift_attn, gain_moe, shift_moe])], axis=0
    ).astype(low)
    small = lax.dynamic_update_slice(
        jnp.zeros((16, width), low), small, (jnp.int32(0), shard * owned)
    )
    inner = jnp.transpose(w_in, (1, 0, 2)).astype(low)
    outer = jnp.transpose(w_out, (1, 0, 2)).astype(low)
    slots = experts * CAP
    total_slots = 8 * slots
    vmem = pltpu.VMEM
    token_shape = jax.ShapeDtypeStruct((SENT_ROWS, width), low)
    attn_rows = 4 * PIECE + 16
    scratch = [
        vmem((8, 16, width), low),
        vmem((16, width), wide),
        vmem((width, 3 * width), low),
        vmem((width, width), low),
        vmem((experts, width, part), low),
        vmem((TILE_ROWS, width), wide),
        vmem((TILE_ROWS, 1), wide),
        vmem((TILE_ROWS, width), low),
        vmem((TILE_ROWS, 3 * width), low),
        vmem((HEADS, TILE_ROWS, TILE_ROWS), wide),
        vmem((TILE_ROWS, width), low),
        vmem((TILE_ROWS, width), wide),
        vmem((TILE_ROWS, 1), wide),
        vmem((TILE_ROWS, 1), wide),
        vmem((16 * TILE_ROWS, width), low),
        vmem((8, slots, TILE_ROWS), low),
        vmem((4 * width, width), low),
        vmem((total_slots, width), low),
        vmem((total_slots, 16), wide),
        vmem((experts, 8 * CAP, part), low),
        vmem((experts, 8 * CAP, part), low),
        vmem((16, width), wide),
        vmem((4, SENT_ROWS, width), low),
        vmem((4, SENT_ROWS, width), low),
        vmem((3, SENT_ROWS, width), low),
        vmem((4 * SENT_ROWS, width), low),
        vmem((3, SENT_ROWS, width), low),
        vmem((experts, width, part), low),
        vmem((experts, owned, hidden), low),
        vmem((experts, part, width), low),
        vmem((attn_rows, width), low),
        vmem((experts, owned, hidden), low),
        vmem((experts, part, width), low),
        vmem((attn_rows, width), low),
        vmem((experts, owned, hidden), low),
        vmem((experts, part, width), low),
        vmem((attn_rows, width), low),
        vmem((SENT_ROWS, width), wide),
        vmem((TILE_ROWS, width), low),
        vmem((TILE_ROWS, width), low),
        vmem((3, 16, width), low),
        vmem((3, 16, width), low),
        pltpu.SemaphoreType.DMA((160,)),
        pltpu.SemaphoreType.DMA((160,)),
        pltpu.SemaphoreType.DMA((16,)),
    ]
    inside = pl.BlockSpec(memory_space=vmem)
    outside = pl.BlockSpec(memory_space=pl.ANY)
    output, input_grad, outer_sum, inner_sum, attn_sum = pl.pallas_call(
        mega,
        out_shape=(
            token_shape,
            token_shape,
            jax.ShapeDtypeStruct((experts, part, width), low),
            jax.ShapeDtypeStruct((experts, owned, hidden), low),
            jax.ShapeDtypeStruct((attn_rows, width), low),
        ),
        in_specs=[inside, inside, inside, inside, inside, outside, inside],
        out_specs=(inside, inside, outside, outside, outside),
        scratch_shapes=scratch,
        compiler_params=pltpu.CompilerParams(
            collective_id=0, has_side_effects=True, vmem_limit_bytes=VMEM_BYTES
        ),
    )(tokens_in, message, small, w_qkv, w_proj, inner, outer)
    attn_grads = attn_sum[: 4 * owned].astype(wide).reshape(4, owned, width)
    small_sum = lax.dynamic_slice(
        attn_sum, (jnp.int32(4 * owned), shard * owned), (16, owned)
    ).astype(wide)
    return (
        output[:rows],
        input_grad[:rows],
        small_sum[3],
        small_sum[4],
        jnp.concatenate([attn_grads[0], attn_grads[1], attn_grads[2]], axis=1),
        attn_grads[3],
        small_sum[5],
        small_sum[6],
        small_sum[:experts].T,
        jnp.transpose(inner_sum, (1, 0, 2)).astype(wide),
        jnp.transpose(outer_sum, (1, 0, 2)).astype(wide),
    )


def solution(mesh):
    sizes = (mesh.shape["shard"], mesh.shape["rep"])
    return jax.shard_map(
        grouped if sizes == (8, 4) else shards,
        mesh=mesh,
        in_specs=(
            P(("shard", "rep"), None),
            P(("shard", "rep"), None),
            P(("shard", "rep"), None),
            P(("shard", "rep"), None),
            P(("shard", "rep"), None),
            P("shard"),
            P("shard"),
            P("shard", None),
            P("shard", None),
            P("shard"),
            P("shard"),
            P("shard", None),
            P("shard", None, None),
            P("shard", None, None),
        ),
        out_specs=(
            P(("shard", "rep"), None),
            P(("shard", "rep"), None),
            P("shard"),
            P("shard"),
            P("shard", None),
            P("shard", None),
            P("shard"),
            P("shard"),
            P("shard", None),
            P("shard", None, None),
            P("shard", None, None),
        ),
        check_vma=False,
    )
```

```python
import jax
import jax.numpy as jnp
from jax import lax
from jax.experimental import pallas as pl
from jax.experimental.pallas import tpu as pltpu
from jax.sharding import PartitionSpec as P

MESH = pl.DeviceIdType.MESH
VMEM_BYTES = 64 * 1024 * 1024 - 256 * 1024

HEADS = 12
HEAD_DIM = 64
SEQ = 197
CAP = 112


epsilon = 1e-06
score_scale = 0.125


def normalize(inputs):
    centred = inputs - jnp.mean(inputs, axis=-1, keepdims=True)
    inverse = lax.rsqrt(jnp.mean(centred * centred, axis=-1, keepdims=True) + epsilon)
    return (centred * inverse, inverse)


def norm_back(upstream, normed, inverse):
    return inverse * (
        upstream
        - jnp.mean(upstream, axis=-1, keepdims=True)
        - normed * jnp.mean(upstream * normed, axis=-1, keepdims=True)
    )


def to_heads(matrix, images):
    return matrix.reshape(images, -1, HEADS, HEAD_DIM)


def shards(
    tokens,
    cotangent,
    expert_index,
    slot_index,
    kept_mask,
    gain_attn,
    shift_attn,
    w_qkv,
    w_proj,
    gain_moe,
    shift_moe,
    w_router,
    w_in,
    w_out,
):
    model_width = tokens.shape[1]
    images = tokens.shape[0] // SEQ
    rows = tokens.shape[0]
    experts = w_in.shape[1]
    group = lax.axis_size("shard")
    low = jnp.bfloat16
    wide = jnp.float32

    def gathered(value):
        return lax.all_gather(value, "shard", axis=0, tiled=True)

    qkv_full = gathered(w_qkv.astype(low))
    proj_full = gathered(w_proj.astype(low))
    smalls = gathered(
        jnp.concatenate(
            [
                jnp.stack([gain_attn, shift_attn, gain_moe, shift_moe], axis=1),
                w_router,
            ],
            axis=1,
        ).astype(low)
    )
    gain_first, shift_first, gain_second, shift_second = (
        smalls[:, index].astype(wide) for index in range(4)
    )
    router_full = smalls[:, 4:]
    inner_part = lax.all_to_all(w_in.astype(low), "shard", split_axis=2, concat_axis=0, tiled=True)
    outer_part = w_out.astype(low)
    upstream_all = gathered(cotangent).reshape(group, rows, model_width)
    flat_slots = jnp.where(kept_mask == 1, expert_index * CAP + slot_index, -1)
    slots_all = gathered(flat_slots).reshape(group, rows, 2)
    slot_numbers = jnp.arange(experts * CAP, dtype=jnp.int32)
    picks = slots_all[:, None, :, :] == slot_numbers[None, :, None, None]
    placed = jnp.any(picks, axis=-1)
    placed_low = placed.astype(low)

    inputs = tokens.astype(wide)
    normed_one, inverse_one = normalize(inputs)
    ln_one = (normed_one * gain_first + shift_first).astype(low)
    triple = jnp.dot(ln_one, qkv_full, preferred_element_type=wide).astype(low)
    queries = to_heads(triple[:, :model_width], images)
    key_rows = to_heads(triple[:, model_width : 2 * model_width], images)
    value_rows = to_heads(triple[:, 2 * model_width :], images)
    scores = (
        jnp.einsum("ishd,ithd->ihst", queries, key_rows, preferred_element_type=wide) * score_scale
    )
    attn_probs = jax.nn.softmax(scores, axis=-1)
    mixed_heads = (
        jnp.einsum(
            "ihst,ithd->ishd", attn_probs.astype(low), value_rows, preferred_element_type=wide
        )
        .reshape(-1, model_width)
        .astype(low)
    )
    residual = inputs + jnp.dot(mixed_heads, proj_full, preferred_element_type=wide)
    normed_two, inverse_two = normalize(residual)
    ln_two = (normed_two * gain_second + shift_second).astype(low)
    ln_two_all = gathered(ln_two).reshape(group, rows, model_width)
    logits = jnp.einsum("btd,de->bte", ln_two_all, router_full, preferred_element_type=wide)
    probs_all = jax.nn.softmax(logits, axis=-1)
    me = lax.axis_index("shard")
    router_probs = lax.dynamic_index_in_dim(probs_all, me, 0, keepdims=False)
    placed_own = lax.dynamic_index_in_dim(placed, me, 0, keepdims=False).astype(wide)
    probs_slots = jnp.repeat(jnp.transpose(probs_all, (0, 2, 1)), CAP, axis=1)
    gate_slots = jnp.sum(placed.astype(wide) * probs_slots, axis=-1)

    def to_slots(values):
        return jnp.einsum("bst,btd->bsd", placed_low, values, preferred_element_type=wide)

    def to_experts(values):
        width = values.shape[-1]
        return jnp.transpose(values.reshape(group, experts, CAP, width), (1, 0, 2, 3)).reshape(
            experts, group * CAP, width
        )

    def from_experts(values):
        width = values.shape[-1]
        return jnp.transpose(values.reshape(experts, group, CAP, width), (1, 0, 2, 3)).reshape(
            group, experts * CAP, width
        )

    def to_tokens(values):
        return jnp.einsum("bst,bsd->btd", placed_low, values, preferred_element_type=wide)

    dispatched = to_experts(to_slots(ln_two_all).astype(low))
    upstream_slots = to_slots(upstream_all)
    outer_grad = to_experts((upstream_slots * gate_slots[:, :, None]).astype(low))
    hidden_pre = jnp.einsum("ecd,def->ecf", dispatched, inner_part, preferred_element_type=wide)
    hidden_act, gelu_pull = jax.vjp(jax.nn.gelu, hidden_pre)
    active = hidden_act.astype(low)
    outer_wgrad = jnp.einsum("ecf,ecd->fed", active, outer_grad, preferred_element_type=wide)
    outer_owned = lax.psum(outer_wgrad.astype(low), "rep").astype(wide)
    active_grad = jnp.einsum("ecd,fed->ecf", outer_grad, outer_part, preferred_element_type=wide)
    inner_grad = gelu_pull(active_grad)[0].astype(low)
    inner_wgrad = jnp.einsum("ecd,ecf->def", dispatched, inner_grad, preferred_element_type=wide)
    inner_rows = lax.all_to_all(
        inner_wgrad.astype(low).reshape(group, -1, experts, inner_part.shape[2]),
        "shard",
        split_axis=0,
        concat_axis=0,
        tiled=True,
    )
    slot_grad = from_experts(
        jnp.einsum("ecf,def->ecd", inner_grad, inner_part, preferred_element_type=wide).astype(low)
    )

    def scattered(values):
        return lax.psum_scatter(values, "shard", scatter_dimension=0, tiled=True)

    raise_grad = scattered(to_tokens(slot_grad).astype(low).reshape(-1, model_width)).astype(wide)
    expert_out = from_experts(
        jnp.einsum("ecf,fed->ecd", active, outer_part, preferred_element_type=wide)
    )
    mixture = scattered(
        to_tokens((expert_out * gate_slots[:, :, None]).astype(low))
        .astype(low)
        .reshape(-1, model_width)
    )
    output = (residual + mixture.astype(wide)).astype(low)
    gate_part = scattered(jnp.sum(expert_out * upstream_slots, axis=-1)).reshape(experts * CAP)
    prob_grad = jnp.transpose(
        jnp.sum((placed_own * gate_part[:, None]).reshape(experts, CAP, rows), axis=1)
    )
    upstream = cotangent.astype(wide)
    logit_grad = (
        router_probs * (prob_grad - jnp.sum(router_probs * prob_grad, axis=-1, keepdims=True))
    ).astype(low)
    ln_two_grad = raise_grad + jnp.einsum(
        "te,de->td", logit_grad, router_full, preferred_element_type=wide
    )
    router_wgrad = jnp.einsum("td,te->de", ln_two, logit_grad, preferred_element_type=wide)
    gain_two_grad = jnp.sum(ln_two_grad * normed_two, axis=0)
    shift_two_grad = jnp.sum(ln_two_grad, axis=0)
    residual_grad = upstream + norm_back(ln_two_grad * gain_second, normed_two, inverse_two)
    attn_grad = residual_grad.astype(low)
    proj_wgrad = jnp.einsum("tc,td->cd", mixed_heads, attn_grad, preferred_element_type=wide)
    mixed_grad = to_heads(
        jnp.einsum("td,cd->tc", attn_grad, proj_full, preferred_element_type=wide).astype(low),
        images,
    )
    value_grad = jnp.einsum(
        "ihst,ishd->ithd", attn_probs.astype(low), mixed_grad, preferred_element_type=wide
    )
    prob_attn_grad = jnp.einsum(
        "ishd,ithd->ihst", mixed_grad, value_rows, preferred_element_type=wide
    )
    score_grad = (
        attn_probs
        * (prob_attn_grad - jnp.sum(attn_probs * prob_attn_grad, axis=-1, keepdims=True))
        * score_scale
    ).astype(low)
    query_grad = jnp.einsum("ihst,ithd->ishd", score_grad, key_rows, preferred_element_type=wide)
    key_grad = jnp.einsum("ihst,ishd->ithd", score_grad, queries, preferred_element_type=wide)
    triple_grad = jnp.concatenate(
        [
            query_grad.reshape(-1, model_width),
            key_grad.reshape(-1, model_width),
            value_grad.reshape(-1, model_width),
        ],
        axis=1,
    ).astype(low)
    qkv_wgrad = jnp.einsum("tc,td->cd", ln_one, triple_grad, preferred_element_type=wide)
    ln_one_grad = jnp.einsum("td,cd->tc", triple_grad, qkv_full, preferred_element_type=wide)
    gain_one_grad = jnp.sum(ln_one_grad * normed_one, axis=0)
    shift_one_grad = jnp.sum(ln_one_grad, axis=0)
    input_grad = (
        residual_grad + norm_back(ln_one_grad * gain_first, normed_one, inverse_one)
    ).astype(low)
    small_grads = jnp.concatenate(
        [
            jnp.stack([gain_one_grad, shift_one_grad, gain_two_grad, shift_two_grad], axis=1),
            router_wgrad,
        ],
        axis=1,
    )
    attn_shares = scattered(jnp.concatenate([qkv_wgrad, proj_wgrad, small_grads], axis=1).astype(low))
    inner_flat, attn_total = lax.psum((inner_rows, attn_shares), "rep")
    inner_owned = jnp.transpose(inner_flat.astype(wide), (1, 2, 0, 3)).reshape(w_in.shape)
    attn_total = attn_total.astype(wide)
    wide_end = w_qkv.shape[1]
    small_end = wide_end + model_width
    return (
        output,
        input_grad,
        attn_total[:, small_end],
        attn_total[:, small_end + 1],
        attn_total[:, :wide_end],
        attn_total[:, wide_end:small_end],
        attn_total[:, small_end + 2],
        attn_total[:, small_end + 3],
        attn_total[:, small_end + 4 :],
        inner_owned,
        outer_owned,
    )


TILE_ROWS = 256
SENT_ROWS = 208
CUTS = 4
Z_STEP = 3.2
Z_LAG = 1.5
DEPTH = 3
PIECE = 96
NEGATIVE = -1e30


def mega(
    tok_ref,
    cot_ref,
    expert_ref,
    slot_ref,
    kept_ref,
    gain_a_ref,
    shift_a_ref,
    gain_m_ref,
    shift_m_ref,
    router_ref,
    qkv_ref,
    proj_ref,
    inner_hbm,
    outer_ref,
    out_ref,
    igrad_ref,
    go_hbm,
    gi_hbm,
    ga_hbm,
    piece_ref,
    stage,
    piece,
    table_buf,
    smalls,
    small_sum,
    wq,
    wp,
    win,
    normed_a,
    inv_a,
    ln_a,
    tri,
    probs,
    heads,
    resid,
    mean_m,
    inv_m,
    rows_buf,
    onehot,
    work,
    og,
    route,
    act,
    slope,
    route_grad,
    st_back,
    sr_back,
    rr_back,
    sr_out,
    rr_out,
    grad_in,
    grad_in_own,
    grad_out,
    grad_attn,
    mid_in,
    mid_out,
    mid_attn,
    end_in,
    end_out,
    end_attn,
    res_grad,
    agrad,
    mgrad,
    small_grad,
    small_swap,
    send_sems,
    recv_sems,
    local_sems,
):
    low = jnp.bfloat16
    wide = jnp.float32
    width = tok_ref.shape[1]
    shard = lax.axis_index("shard")
    rep = lax.axis_index("rep")

    def flip(j):
        out = shard
        for bit in range(3):
            if (j >> bit) & 1:
                out = out + (1 - 2 * ((shard // (1 << bit)) % 2)) * (1 << bit)
        return out

    peers = [flip(j) for j in range(8)]
    pair = rep + 1 - 2 * (rep % 2)
    across = 3 - rep
    is_mid = jnp.logical_and(rep >= 1, rep <= 2)
    is_end = jnp.logical_not(is_mid)

    ups_base = 8 * TILE_ROWS
    for position in range(16):
        rows_buf[pl.ds(position * TILE_ROWS + SENT_ROWS, TILE_ROWS - SENT_ROWS), :] = jnp.zeros(
            (TILE_ROWS - SENT_ROWS, width), low
        )
    barrier = pltpu.get_barrier_semaphore()
    for j in range(1, 8):
        pl.semaphore_signal(barrier, inc=1, device_id=(peers[j], rep), device_id_type=MESH)
    pl.semaphore_signal(barrier, inc=1, device_id=(shard, pair), device_id_type=MESH)

    @pl.when(is_mid)
    def _():
        pl.semaphore_signal(barrier, inc=1, device_id=(shard, across), device_id_type=MESH)
        pl.semaphore_wait(barrier, 9)

    @pl.when(is_end)
    def _():
        pl.semaphore_wait(barrier, 8)

    count = [0]
    unsent = []
    settled = []

    def describe(src, dst, device):
        index = count[0]
        count[0] += 1
        return pltpu.make_async_remote_copy(
            src_ref=src,
            dst_ref=dst,
            send_sem=send_sems.at[index],
            recv_sem=recv_sems.at[index],
            device_id=device,
            device_id_type=MESH,
        )

    def send(src, dst, j):
        copy = describe(src, dst, (peers[j], rep) if j < 8 else (shard, pair))
        copy.start()
        unsent.append(copy)
        return copy

    def settle(copies):
        for copy in copies:
            copy.wait_send()
            settled.append(id(copy))

    local_count = [0]

    def local(src, dst):
        copy = pltpu.make_async_copy(src, dst, local_sems.at[local_count[0]])
        local_count[0] += 1
        copy.start()
        return copy

    def off(value, unit):
        return pl.multiple_of(value * unit, unit)

    class Gather:
        def __init__(self, view, first, second):
            self.view, self.first, self.second = view, first, second
            self.all = []

        def put(self, at, to, j, half=None):
            copy = send(self.view(at, at, half), self.view(at, to, half), j)
            self.all.append(copy)
            return copy

        def begin(self):
            self.from_x = self.put(0, 2, 2)
            self.from_y = self.put(0, 4, 4)
            self.from_s = [self.put(0, 1, 1)]

        def pass_on(self):
            self.from_x.wait_recv()
            self.far = [self.put(2, 6, 4, self.first)]
            self.from_s.append(self.put(2, 3, 1))
            self.from_y.wait_recv()
            self.far.append(self.put(4, 6, 2, self.second))
            self.from_s.append(self.put(4, 5, 1))

        def last(self):
            for copy in self.far:
                copy.wait_recv()
            self.from_s.append(self.put(6, 7, 1))

    def weight_view(ref):
        def view(at, to, half):
            start = off(peers[at], PIECE)
            if half is None:
                return ref.at[pl.ds(start, PIECE)]
            return ref.at[pl.ds(start + half[0], half[1])]

        return view

    def row_view(base):
        def view(at, to, half):
            first, size = half if half is not None else (0, SENT_ROWS)
            return rows_buf.at[pl.ds(base + to * TILE_ROWS + first, size)]

        return view

    own_rows = pl.ds(off(shard, PIECE), PIECE)
    small_copies = []
    staged = local(inner_hbm.at[0], stage)
    experts = router_ref.shape[0]
    piece[...] = jnp.zeros(piece.shape, wide)
    piece[0:experts, 0:PIECE] = router_ref[...]
    for row, ref in enumerate((gain_a_ref, shift_a_ref, gain_m_ref, shift_m_ref)):
        piece[experts + row : experts + row + 1, 0:PIECE] = ref[...]
    own_at = lax.broadcasted_iota(jnp.int32, (128, width), 0)
    own_to = lax.broadcasted_iota(jnp.int32, (128, width), 1) - shard * PIECE
    own_pick = jnp.where(jnp.logical_and(own_at == own_to, own_at < PIECE), 1.0, 0.0).astype(low)
    kept = kept_ref[...] == 1
    table_buf[...] = jnp.zeros(table_buf.shape, wide)
    table_buf[8:10, 0:256] = jnp.full((2, 256), experts, wide)
    table_buf[8:10, 0:SEQ] = jnp.where(kept, expert_ref[...], experts).astype(wide)
    table_buf[8:10, 256 : 256 + SEQ] = jnp.where(kept, slot_ref[...], 0).astype(wide)
    smalls[0] = (
        jnp.dot(piece[...].astype(low), own_pick, preferred_element_type=wide) + table_buf[...]
    ).astype(low)
    for j in range(1, 8):
        small_copies.append(send(smalls.at[0], smalls.at[j], j))
    wq[own_rows, :] = qkv_ref[...].astype(low)
    gather_q = Gather(weight_view(wq), (0, 48), (48, 48))
    gather_q.begin()
    wp[own_rows, :] = proj_ref[...].astype(low)
    res_grad[192:SENT_ROWS, :] = jnp.zeros((SENT_ROWS - 192, width), wide)
    res_grad[0:SEQ, :] = cot_ref[...].astype(wide)
    rows_buf[ups_base : ups_base + SENT_ROWS, :] = res_grad[...].astype(low)
    resid[192:TILE_ROWS, :] = jnp.zeros((TILE_ROWS - 192, width), wide)
    resid[0:SEQ, :] = tok_ref[...].astype(wide)
    inputs = resid[...]
    normed, inverse = normalize(inputs)
    normed_a[...] = normed
    inv_a[...] = inverse

    def inner_cast(e):
        for d in range(8):
            grad_in[e, d * PIECE : (d + 1) * PIECE, :] = stage[
                :, d * part : (d + 1) * part
            ].astype(low)

    part = win.shape[2]
    for e in range(experts):
        staged.wait()
        inner_cast(e)
        if e < experts - 1:
            staged = local(inner_hbm.at[e + 1], stage)
    gather_q.pass_on()
    half_at = (rep % 2) * (PIECE // 2)

    def inner_half(j):
        return pl.ds(pl.multiple_of(peers[j] * PIECE + half_at, 16), PIECE // 2)

    inner_own = local(grad_in.at[:, own_rows, :], win.at[:, own_rows, :])
    inner_passed = []

    def inner_pass(numbers):
        for j in numbers:
            inner_copies[j].wait_recv()
            rows = win.at[:, inner_half(j), :]
            inner_passed.append(send(rows, rows, 8))

    for copy in small_copies:
        copy.wait_recv()
    total = smalls[0].astype(wide)
    for j in range(1, 8):
        total = total + smalls[j].astype(wide)
    small_sum[...] = total
    gain_first, shift_first = small_sum[3:4, :], small_sum[4:5, :]
    gain_second, shift_second = small_sum[5:6, :], small_sum[6:7, :]
    ln_a[...] = (normed_a[...] * gain_first + shift_first).astype(low)
    slots = onehot.shape[1]
    slot_at = lax.broadcasted_iota(jnp.int32, (slots, TILE_ROWS), 0).astype(wide)

    def route_step(j, carry):
        table = smalls[j].astype(wide)
        first = table[8:9, 0:256] * CAP + table[8:9, 256:512]
        second = table[9:10, 0:256] * CAP + table[9:10, 256:512]
        hit = jnp.logical_or(slot_at == first, slot_at == second)
        onehot[j] = jnp.where(hit, 1.0, 0.0).astype(low)
        return carry

    lax.fori_loop(0, 8, route_step, 0)
    gather_q.last()
    gather_p = Gather(weight_view(wp), (0, 48), (48, 48))
    gather_p.begin()
    for copy in gather_q.from_s:
        copy.wait_recv()

    def triple_step(i, carry):
        columns = pl.ds(off(i, 384), 384)
        tri[:, columns] = jnp.dot(
            ln_a[...], wq[:, columns], preferred_element_type=wide
        ).astype(low)
        return carry

    lax.fori_loop(0, 6, triple_step, 0)
    gather_p.pass_on()
    inner_copies = {
        j: send(
            grad_in.at[:, inner_half(j), :],
            win.at[:, inner_half(0), :],
            j,
        )
        for j in range(1, 8)
    }

    lane = lax.broadcasted_iota(jnp.int32, (TILE_ROWS, 128), 1)
    key_at = lax.broadcasted_iota(jnp.int32, (TILE_ROWS, TILE_ROWS), 1)

    def head_columns(p, third):
        return pl.ds(pl.multiple_of(third * width + p * 128, 128), 128)

    def contract(a, b, da, db):
        return lax.dot_general(a, b, (((da,), (db,)), ((), ())), preferred_element_type=wide)

    def one_head(values, side):
        return jnp.where((lane < 64) == (side == 0), values, jnp.zeros_like(values))

    def attend(p, carry):
        queries = tri[:, head_columns(p, 0)]
        key_rows = tri[:, head_columns(p, 1)]
        value_rows = tri[:, head_columns(p, 2)]
        mixed = []
        for side in range(2):
            scores = contract(one_head(queries, side), key_rows, 1, 1) * score_scale
            scores = jnp.where(key_at < SEQ, scores, NEGATIVE)
            powers = jnp.exp(scores - jnp.max(scores, axis=-1, keepdims=True))
            weights = powers / jnp.sum(powers, axis=-1, keepdims=True)
            probs[2 * p + side] = weights
            mixed.append(jnp.dot(weights.astype(low), value_rows, preferred_element_type=wide))
        heads[:, head_columns(p, 0)] = jnp.where(lane < 64, mixed[0], mixed[1]).astype(low)
        return carry

    lax.fori_loop(0, 6, attend, 0)
    gather_p.last()
    for copy in gather_p.from_s:
        copy.wait_recv()
    residual = resid[...] + jnp.dot(
        heads[...], wp[...], preferred_element_type=wide
    )
    resid[...] = residual
    normed, inverse = normalize(residual)
    mean_m[...] = jnp.mean(residual, axis=-1, keepdims=True)
    inv_m[...] = inverse
    ln_two = (normed * gain_second + shift_second).astype(low)
    rows_buf[0:SENT_ROWS, :] = ln_two[0:SENT_ROWS, :]
    gather_l = Gather(row_view(0), (0, 112), (112, 96))
    gather_l.begin()
    inner_pass((1, 2, 3, 4, 5, 6, 7))
    router = small_sum[...].astype(low)
    lane16 = lax.broadcasted_iota(jnp.int32, (slots, 16), 1)
    expert_of = lax.broadcasted_iota(jnp.int32, (slots, 16), 0)
    own_lane = jnp.logical_and(expert_of >= lane16 * CAP, expert_of < lane16 * CAP + CAP)

    def expert_rows(e, j, blocks=1):
        return pl.ds(pl.multiple_of((e * 8 + j) * CAP, 16), blocks * CAP)

    def dispatch_step(j, carry):
        picks = onehot[j]
        ln_rows = rows_buf[pl.ds(off(j, TILE_ROWS), TILE_ROWS), :]
        sent = jnp.dot(picks, ln_rows, preferred_element_type=wide).astype(low)
        logits = jnp.where(lane16 < experts, contract(sent, router, 1, 1), NEGATIVE)
        powers = jnp.exp(logits - jnp.max(logits, axis=-1, keepdims=True))
        chances = powers / jnp.sum(powers, axis=-1, keepdims=True)
        for e in range(experts):
            rows = expert_rows(e, j)
            work[rows, :] = sent[e * CAP : (e + 1) * CAP]
            route[rows, :] = chances[e * CAP : (e + 1) * CAP]
        return carry

    def upward_step(j, carry):
        up_rows = rows_buf[pl.ds(pl.multiple_of(ups_base + j * TILE_ROWS, 16), TILE_ROWS), :]
        ups = jnp.dot(onehot[j], up_rows, preferred_element_type=wide)
        chances = jnp.concatenate([route[expert_rows(e, j), :] for e in range(experts)], axis=0)
        gate = jnp.sum(jnp.where(own_lane, chances, 0.0), axis=-1, keepdims=True)
        upward = (ups * gate).astype(low)
        for e in range(experts):
            og[expert_rows(e, j), :] = upward[e * CAP : (e + 1) * CAP]
        return carry

    def hidden_step(g):
        def step(e, carry):
            rows = pl.ds(g * 2 * CAP, 2 * CAP)
            sent = work[expert_rows(e, 2 * g, 2), :]
            value = jnp.dot(sent, win[e], preferred_element_type=wide)
            square = value * value
            bend = jnp.tanh(0.7978845608028654 * value * (1.0 + 0.044715 * square))
            act[e, rows, :] = (0.5 * value * (1.0 + bend)).astype(low)
            slope[e, rows, :] = (
                0.5 * (1.0 + bend)
                + 0.5
                * value
                * (1.0 - bend * bend)
                * (0.7978845608028654 * (1.0 + 0.134145 * square))
            ).astype(low)
            return carry

        lax.fori_loop(0, experts, step, 0)

    gather_l.pass_on()
    gather_u = Gather(row_view(ups_base), (0, 112), (112, 96))
    gather_u.begin()
    gather_l.from_s[0].wait_recv()
    lax.fori_loop(0, 2, dispatch_step, 0)
    gather_l.last()
    for g in range(1, 3):
        gather_l.from_s[g].wait_recv()
        lax.fori_loop(2 * g, 2 * g + 2, dispatch_step, 0)
    inner_own.wait()
    for copy in inner_passed:
        copy.wait_recv()
    hidden_step(0)
    gather_u.pass_on()
    hidden_step(1)
    hidden_step(2)
    gather_l.from_s[3].wait_recv()
    lax.fori_loop(6, 8, dispatch_step, 0)
    gather_u.last()
    hidden_step(3)
    for copy in gather_u.from_s:
        copy.wait_recv()
    lax.fori_loop(0, 8, upward_step, 0)

    ready, raised, left = [], [], []

    class Copies:
        def __init__(self, own, mid, end, out, rows):
            self.own, self.mid, self.end, self.out, self.rows = own, mid, end, out, rows
            self.up = describe(own, end, (shard, pair))
            self.over = describe(own, mid, (shard, across))
            self.down = describe(end, end, (shard, pair))
            self.write = pltpu.make_async_copy(end, out, local_sems.at[local_count[0]])
            local_count[0] += 1

        def add(self, target, other):
            size = self.rows

            def step(i, carry):
                at = pl.ds(pl.multiple_of(i * size, 16), size)
                target[at, :] = (
                    self.own[at, :].astype(wide) + other[at, :].astype(wide)
                ).astype(low)
                return carry

            lax.fori_loop(0, target.shape[0] // size, step, 0)

        def rise(self):
            ready.append(self)
            pump()

        def cross(self):
            self.up.wait_recv()
            self.add(self.own, self.end)
            self.over.start()

        def fall(self):
            self.over.wait_recv()
            self.add(self.end, self.mid)
            self.down.start()
            self.write.start()

    out_cut, in_cut = part // CUTS, grad_in_own.shape[2] // CUTS
    out_copies = [
        Copies(
            *(
                ref.at[e, pl.ds(h * out_cut, out_cut)]
                for ref in (grad_out, mid_out, end_out, go_hbm)
            ),
            48,
        )
        for e in range(experts)
        for h in range(CUTS)
    ]
    in_copies = [
        Copies(
            *(
                ref.at[e, :, pl.ds(h * in_cut, in_cut)]
                for ref in (grad_in_own, mid_in, end_in, gi_hbm)
            ),
            48,
        )
        for e in range(experts)
        for h in range(CUTS)
    ]
    attn_copies = {
        p: Copies(
            *(ref.at[pl.ds(p * PIECE, size)] for ref in (grad_attn, mid_attn, end_attn, ga_hbm)),
            size // 2 if size > 16 else size,
        )
        for p, size in ((3, PIECE), (2, PIECE), (1, PIECE), (0, PIECE), (4, 16))
    }
    all_copies = out_copies + in_copies + list(attn_copies.values())

    def pump():
        @pl.when(is_end)
        def _():
            while len(raised) < len(ready) and len(raised) < len(left) + DEPTH:
                ready[len(raised)].up.start()
                raised.append(1)

    plan = []
    moment = 0.0
    for number, copies in enumerate(all_copies):
        span = Z_STEP if number < 2 * experts * CUTS else 3.2
        moment += span
        plan.append((moment + span + Z_LAG, 0, copies))
        plan.append((moment + 3 * span + 2 * Z_LAG, 1, copies))
    plan.sort(key=lambda step: step[:2])

    def tend(until):
        steps = []
        while plan and plan[0][0] <= until:
            steps.append(plan.pop(0))
        for _, kind, copies in steps:
            if kind == 0:
                assert len(raised) > len(left)

            @pl.when(is_mid)
            def _():
                (copies.fall if kind else copies.cross)()

            if kind == 0:

                @pl.when(is_end)
                def _():
                    copies.up.wait_send()

                left.append(1)
                pump()

    for e in range(experts):
        grad_out[e] = contract(act[e], og[expert_rows(e, 0, 8), :], 0, 0).astype(low)
        for h in range(CUTS):
            out_copies[CUTS * e + h].rise()

    settle(gather_l.all)
    settle(inner_copies.values())
    settle(gather_u.all)
    route_grad[...] = jnp.zeros(route_grad.shape, wide)
    half = act.shape[1] // 2
    lane_h = lax.broadcasted_iota(jnp.int32, (half, 16), 1)

    def inner_step(i, carry):
        e = i // 2
        rows = pl.ds(off(i % 2, half), half)
        flat = pl.ds(pl.multiple_of(i * half, 16), half)
        inner = contract(og[flat, :], outer_ref[e], 1, 1) * slope[e, rows, :].astype(wide)
        slope[e, rows, :] = inner.astype(low)
        return carry

    def back_step(i, carry):
        e = i // 2
        rows = pl.ds(off(i % 2, half), half)
        flat = pl.ds(pl.multiple_of(i * half, 16), half)
        upward = og[flat, :]
        gone = jnp.dot(act[e, rows, :], outer_ref[e], preferred_element_type=wide)
        chances = route[flat, :]
        gate = jnp.sum(jnp.where(lane_h == e, chances, 0.0), axis=-1, keepdims=True)
        pull = jnp.sum(upward.astype(wide) * gone, axis=-1, keepdims=True)
        logit = (pull * (jnp.where(lane_h == e, 1.0, 0.0) - chances)).astype(low)
        logit = jnp.where(lane_h < experts, logit, jnp.zeros_like(logit))
        rows_buf[flat, :] = (gone * gate).astype(low)
        og[flat, :] = (
            contract(slope[e, rows, :], win[e], 1, 1)
            + jnp.dot(logit, router, preferred_element_type=wide)
        ).astype(low)
        route_grad[...] += contract(logit, work[flat, :], 0, 0)
        return carry

    grad_in_copies = []

    def grad_in_send(e):
        target = grad_in_own.at[e, :, pl.ds(off(shard, part), part)]
        grad_in_copies.append(
            [
                send(grad_in.at[e, pl.ds(off(peers[j], PIECE), PIECE), :], target, j)
                for j in range(1, 8)
            ]
        )
        grad_in_copies[e].append(local(grad_in.at[e, own_rows, :], target))

    def grad_in_wait(e):
        for copy in grad_in_copies[e][:7]:
            copy.wait_recv()
        grad_in_copies[e][7].wait()
        for h in range(CUTS):
            in_copies[CUTS * e + h].rise()

    for e in range(experts):
        lax.fori_loop(2 * e, 2 * e + 2, inner_step, 0)
        grad_in[e] = contract(work[expert_rows(e, 0, 8), :], slope[e], 0, 0).astype(low)
        if e < experts - 1:
            grad_in_send(e)
        tend(4 + 2 * e)
    for e in range(experts):
        lax.fori_loop(2 * e, 2 * e + 2, back_step, 0)
        tend(10.5 + 2.3 * e)

    def combine_back(j):
        joined = jnp.concatenate([og[expert_rows(e, j), :] for e in range(experts)], axis=0)
        return contract(onehot[j], joined, 0, 0)[0:SENT_ROWS]

    def combine_out(j):
        joined = jnp.concatenate(
            [rows_buf[expert_rows(e, j), :] for e in range(experts)], axis=0
        )
        return contract(onehot[j], joined, 0, 0)[0:SENT_ROWS]

    stage_out = experts * 8 * CAP

    def odd_back(i, carry):
        st_back[i] = combine_back(2 * i + 1).astype(low)
        return carry

    lax.fori_loop(0, 4, odd_back, 0)
    swap_back = send(st_back, sr_back, 1)
    tend(17)

    def odd_out(i, carry):
        rows = pl.ds(pl.multiple_of(stage_out + i * SENT_ROWS, 16), SENT_ROWS)
        rows_buf[rows, :] = combine_out(2 * i + 1).astype(low)
        return carry

    lax.fori_loop(0, 4, odd_out, 0)
    tend(19)
    swap_back.wait_recv()

    def even_back(i, carry):
        sr_back[i] = (combine_back(2 * i) + sr_back[i].astype(wide)).astype(low)
        return carry

    lax.fori_loop(0, 4, even_back, 0)
    back_copies = [send(sr_back.at[i], rr_back.at[i - 1], 2 * i) for i in range(1, 4)]
    swap_out = send(rows_buf.at[pl.ds(stage_out, 4 * SENT_ROWS)], sr_out, 1)
    tend(22)
    swap_out.wait_recv()

    def even_out(i, carry):
        rows = pl.ds(off(i, SENT_ROWS), SENT_ROWS)
        sr_out[rows, :] = (combine_out(2 * i) + sr_out[rows, :].astype(wide)).astype(low)
        return carry

    lax.fori_loop(0, 4, even_out, 0)
    tend(25)
    for e in range(experts - 1):
        grad_in_wait(e)
    tend(38)

    for copy in back_copies:
        copy.wait_recv()
    grad_in_send(experts - 1)
    ln_grad = sr_back[0].astype(wide)
    for i in range(3):
        ln_grad = ln_grad + rr_back[i].astype(wide)
    normed = (resid[0:SENT_ROWS, :] - mean_m[0:SENT_ROWS, :]) * inv_m[0:SENT_ROWS, :]
    gain_m_grad = jnp.sum(ln_grad * normed, axis=0, keepdims=True)
    shift_m_grad = jnp.sum(ln_grad, axis=0, keepdims=True)
    upstream = res_grad[...]
    residual_grad = upstream + norm_back(
        ln_grad * gain_second, normed, inv_m[0:SENT_ROWS, :]
    )
    res_grad[...] = residual_grad
    agrad[...] = jnp.zeros(agrad.shape, low)
    agrad[0:SENT_ROWS, :] = residual_grad.astype(low)
    mgrad[...] = contract(agrad[...], wp[...], 1, 1).astype(low)

    def grad_rows(part, j):
        return pl.ds(pl.multiple_of(part * width + peers[j] * PIECE, 16), PIECE)

    def kept_rows(part, i):
        return pl.ds((i * 4 + part) * PIECE, PIECE)

    def come_rows(part, i):
        return pl.ds((16 + i * 4 + part) * PIECE, PIECE)

    def share(part):
        return [
            send(work.at[grad_rows(part, 2 * i + 1)], og.at[kept_rows(part, i)], 1)
            for i in range(4)
        ]

    def gather_share(part, copies):
        sent = []
        for i in range(4):
            copies[i].wait_recv()
            rows = kept_rows(part, i)
            og[rows, :] = (
                work[grad_rows(part, 2 * i), :].astype(wide) + og[rows, :].astype(wide)
            ).astype(low)
            if i > 0:
                sent.append(send(og.at[rows], og.at[come_rows(part, i - 1)], 2 * i))
        return sent

    def total_share(part, copies):
        total = og[kept_rows(part, 0), :].astype(wide)
        for i in range(3):
            copies[i].wait_recv()
            total = total + og[come_rows(part, i), :].astype(wide)
        grad_attn[pl.ds(part * PIECE, PIECE), :] = total.astype(low)
        attn_copies[part].rise()

    def attend_back(p, carry):
        queries = tri[:, head_columns(p, 0)]
        key_rows = tri[:, head_columns(p, 1)]
        value_rows = tri[:, head_columns(p, 2)]
        mixed = mgrad[:, head_columns(p, 0)]
        results = []
        for side in range(2):
            weights = probs[2 * p + side]
            value_grad = contract(weights.astype(low), mixed, 0, 0)
            weight_grad = contract(one_head(mixed, side), value_rows, 1, 1)
            score_grad = (
                weights
                * (weight_grad - jnp.sum(weights * weight_grad, axis=-1, keepdims=True))
                * score_scale
            ).astype(low)
            query_grad = jnp.dot(score_grad, key_rows, preferred_element_type=wide)
            key_grad = contract(score_grad, queries, 0, 0)
            results.append((query_grad, key_grad, value_grad))
        for third in range(3):
            tri[:, head_columns(p, third)] = jnp.where(
                lane < 64, results[0][third], results[1][third]
            ).astype(low)
        return carry

    work[3 * width : 4 * width, :] = contract(heads[...], agrad[...], 0, 0).astype(low)
    share_p = share(3)
    tend(43)
    lax.fori_loop(0, 3, attend_back, 0)
    tend(46)
    lax.fori_loop(3, 6, attend_back, 0)
    tend(50)

    def weight_grad_of(part):
        work[part * width : (part + 1) * width, :] = contract(
            ln_a[...], tri[:, part * width : (part + 1) * width], 0, 0
        ).astype(low)

    weight_grad_of(2)
    share_v = share(2)
    come_p = gather_share(3, share_p)
    weight_grad_of(1)
    share_k = share(1)
    come_v = gather_share(2, share_v)
    weight_grad_of(0)
    share_q = share(0)
    come_k = gather_share(1, share_k)
    tend(54)
    ln_grad = contract(tri[0:SENT_ROWS, :], wq[...], 1, 1)
    come_q = gather_share(0, share_q)
    normed = normed_a[0:SENT_ROWS, :]
    gain_a_grad = jnp.sum(ln_grad * normed, axis=0, keepdims=True)
    shift_a_grad = jnp.sum(ln_grad, axis=0, keepdims=True)
    row16 = lax.broadcasted_iota(jnp.int32, (16, width), 0)
    small = jnp.where(row16 < experts, route_grad[...], 0.0)
    for row, value in (
        (3, gain_a_grad),
        (4, shift_a_grad),
        (5, gain_m_grad),
        (6, shift_m_grad),
    ):
        small = small + jnp.where(row16 == row, value, 0.0)
    small_grad[0] = small.astype(low)
    swap = send(small_grad.at[0], small_swap.at[0], 1)
    igrad_ref[...] = (
        res_grad[...] + norm_back(ln_grad * gain_first, normed, inv_a[0:SENT_ROWS, :])
    ).astype(low)
    grad_in_wait(experts - 1)
    tend(57)
    for step in range(2):
        swap.wait_recv()
        small_grad[step + 1] = (
            small_grad[step].astype(wide) + small_swap[step].astype(wide)
        ).astype(low)
        swap = send(small_grad.at[step + 1], small_swap.at[step + 1], 2 << step)
        tend(60 + 3 * step)
    tend(72)
    total_share(3, come_p)
    total_share(2, come_v)
    tend(76)
    total_share(1, come_k)
    total_share(0, come_q)
    out_sends = [
        send(sr_out.at[pl.ds(i * SENT_ROWS, SENT_ROWS)], rr_out.at[i - 1], 2 * i)
        for i in range(1, 4)
    ]
    swap.wait_recv()
    grad_attn[4 * PIECE : 4 * PIECE + 16, :] = (
        small_grad[2].astype(wide) + small_swap[2].astype(wide)
    ).astype(low)
    attn_copies[4].rise()
    tend(84)
    output = resid[0:SENT_ROWS, :] + sr_out[0:SENT_ROWS, :].astype(wide)
    for i in range(3):
        out_sends[i].wait_recv()
        output = output + rr_out[i].astype(wide)
    out_ref[...] = output.astype(low)
    tend(1000)
    for copies in all_copies:

        @pl.when(is_end)
        def _():
            copies.down.wait_recv()
            copies.write.start()

        @pl.when(is_mid)
        def _():
            copies.over.wait_send()
            copies.down.wait_send()

    for copies in all_copies:
        copies.write.wait()
    assert count[0] <= send_sems.shape[0] and local_count[0] <= local_sems.shape[0]
    piece_ref[...] = contract(end_attn[4 * PIECE : 4 * PIECE + 16, :], own_pick, 1, 1)
    for copy in unsent:
        if id(copy) not in settled:
            copy.wait_send()


def finish(
    out_in,
    igrad_in,
    outer_in,
    inner_in,
    attn_in,
    small_in,
    out_ref,
    igrad_ref,
    outer_ref,
    inner_ref,
    qkv_ref,
    proj_ref,
    router_ref,
    gain_a_ref,
    shift_a_ref,
    gain_m_ref,
    shift_m_ref,
):
    wide = jnp.float32
    outer_ref[...] = outer_in[...].astype(wide)
    inner_ref[...] = inner_in[...].astype(wide)

    @pl.when(pl.program_id(0) == 0)
    def _():
        rows, width = out_ref.shape
        out_ref[...] = out_in[0:rows, :]
        igrad_ref[...] = igrad_in[0:rows, :]
        for third in range(3):
            qkv_ref[:, third * width : (third + 1) * width] = attn_in[
                third * PIECE : (third + 1) * PIECE, :
            ].astype(wide)
        proj_ref[...] = attn_in[3 * PIECE : 4 * PIECE, :].astype(wide)
        experts = router_ref.shape[0]
        router_ref[...] = small_in[0:experts, 0:PIECE]
        for row, ref in enumerate((gain_a_ref, shift_a_ref, gain_m_ref, shift_m_ref)):
            ref[...] = small_in[experts + row : experts + row + 1, 0:PIECE]


def grouped(
    tokens,
    cotangent,
    expert_index,
    slot_index,
    kept_mask,
    gain_attn,
    shift_attn,
    w_qkv,
    w_proj,
    gain_moe,
    shift_moe,
    w_router,
    w_in,
    w_out,
):
    low = jnp.bfloat16
    wide = jnp.float32
    rows, width = tokens.shape
    owned, experts, hidden = w_in.shape
    part = w_out.shape[0]
    shard = lax.axis_index("shard")
    outer = jnp.transpose(w_out, (1, 0, 2)).astype(low)
    slots = experts * CAP
    total_slots = 8 * slots
    vmem = pltpu.VMEM
    token_shape = jax.ShapeDtypeStruct((SENT_ROWS, width), low)
    attn_rows = 4 * PIECE + 16
    scratch = [
        vmem((owned, hidden), wide),
        vmem((16, 128), wide),
        vmem((16, width), wide),
        vmem((8, 16, width), low),
        vmem((16, width), wide),
        vmem((width, 3 * width), low),
        vmem((width, width), low),
        vmem((experts, width, part), low),
        vmem((TILE_ROWS, width), wide),
        vmem((TILE_ROWS, 1), wide),
        vmem((TILE_ROWS, width), low),
        vmem((TILE_ROWS, 3 * width), low),
        vmem((HEADS, TILE_ROWS, TILE_ROWS), wide),
        vmem((TILE_ROWS, width), low),
        vmem((TILE_ROWS, width), wide),
        vmem((TILE_ROWS, 1), wide),
        vmem((TILE_ROWS, 1), wide),
        vmem((16 * TILE_ROWS, width), low),
        vmem((8, slots, TILE_ROWS), low),
        vmem((4 * width, width), low),
        vmem((total_slots, width), low),
        vmem((total_slots, 16), wide),
        vmem((experts, 8 * CAP, part), low),
        vmem((experts, 8 * CAP, part), low),
        vmem((16, width), wide),
        vmem((4, SENT_ROWS, width), low),
        vmem((4, SENT_ROWS, width), low),
        vmem((3, SENT_ROWS, width), low),
        vmem((4 * SENT_ROWS, width), low),
        vmem((3, SENT_ROWS, width), low),
        vmem((experts, width, part), low),
        vmem((experts, owned, hidden), low),
        vmem((experts, part, width), low),
        vmem((attn_rows, width), low),
        vmem((experts, owned, hidden), low),
        vmem((experts, part, width), low),
        vmem((attn_rows, width), low),
        vmem((experts, owned, hidden), low),
        vmem((experts, part, width), low),
        vmem((attn_rows, width), low),
        vmem((SENT_ROWS, width), wide),
        vmem((TILE_ROWS, width), low),
        vmem((TILE_ROWS, width), low),
        vmem((3, 16, width), low),
        vmem((3, 16, width), low),
        pltpu.SemaphoreType.DMA((256,)),
        pltpu.SemaphoreType.DMA((256,)),
        pltpu.SemaphoreType.DMA((48,)),
    ]
    inside = pl.BlockSpec(memory_space=vmem)
    outside = pl.BlockSpec(memory_space=pl.ANY)
    output, input_grad, outer_sum, inner_sum, attn_sum, small_sum = pl.pallas_call(
        mega,
        out_shape=(
            token_shape,
            token_shape,
            jax.ShapeDtypeStruct((experts, part, width), low),
            jax.ShapeDtypeStruct((experts, owned, hidden), low),
            jax.ShapeDtypeStruct((attn_rows, width), low),
            jax.ShapeDtypeStruct((16, 128), wide),
        ),
        in_specs=[inside] * 12 + [outside, inside],
        out_specs=(inside, inside, outside, outside, outside, inside),
        scratch_shapes=scratch,
        compiler_params=pltpu.CompilerParams(
            collective_id=0, has_side_effects=True, vmem_limit_bytes=VMEM_BYTES
        ),
    )(
        tokens,
        cotangent,
        expert_index.T,
        slot_index.T,
        kept_mask.T,
        gain_attn.reshape(1, owned),
        shift_attn.reshape(1, owned),
        gain_moe.reshape(1, owned),
        shift_moe.reshape(1, owned),
        w_router.T,
        w_qkv,
        w_proj,
        jnp.transpose(w_in, (1, 0, 2)),
        outer,
    )

    def whole(*shape):
        return pl.BlockSpec(shape, lambda e: (0,) * len(shape))

    def one(*shape):
        return pl.BlockSpec((1, *shape), lambda e: (e, 0, 0))

    finals = pl.pallas_call(
        finish,
        grid=(experts,),
        out_shape=(
            jax.ShapeDtypeStruct((rows, width), low),
            jax.ShapeDtypeStruct((rows, width), low),
            jax.ShapeDtypeStruct((experts, part, width), wide),
            jax.ShapeDtypeStruct((experts, owned, hidden), wide),
            jax.ShapeDtypeStruct((owned, 3 * width), wide),
            jax.ShapeDtypeStruct((owned, width), wide),
            jax.ShapeDtypeStruct((experts, owned), wide),
        )
        + (jax.ShapeDtypeStruct((1, owned), wide),) * 4,
        in_specs=[
            whole(SENT_ROWS, width),
            whole(SENT_ROWS, width),
            one(part, width),
            one(owned, hidden),
            whole(attn_rows, width),
            whole(16, 128),
        ],
        out_specs=(
            whole(rows, width),
            whole(rows, width),
            one(part, width),
            one(owned, hidden),
            whole(owned, 3 * width),
            whole(owned, width),
            whole(experts, owned),
        )
        + (whole(1, owned),) * 4,
        compiler_params=pltpu.CompilerParams(vmem_limit_bytes=VMEM_BYTES // 2),
    )(output, input_grad, outer_sum, inner_sum, attn_sum, small_sum)
    return (
        finals[0],
        finals[1],
        finals[7].reshape(owned),
        finals[8].reshape(owned),
        finals[4],
        finals[5],
        finals[9].reshape(owned),
        finals[10].reshape(owned),
        finals[6].T,
        jnp.transpose(finals[3], (1, 0, 2)),
        jnp.transpose(finals[2], (1, 0, 2)),
    )


def solution(mesh):
    sizes = (mesh.shape["shard"], mesh.shape["rep"])
    return jax.shard_map(
        grouped if sizes == (8, 4) else shards,
        mesh=mesh,
        in_specs=(
            P(("shard", "rep"), None),
            P(("shard", "rep"), None),
            P(("shard", "rep"), None),
            P(("shard", "rep"), None),
            P(("shard", "rep"), None),
            P("shard"),
            P("shard"),
            P("shard", None),
            P("shard", None),
            P("shard"),
            P("shard"),
            P("shard", None),
            P("shard", None, None),
            P("shard", None, None),
        ),
        out_specs=(
            P(("shard", "rep"), None),
            P(("shard", "rep"), None),
            P("shard"),
            P("shard"),
            P("shard", None),
            P("shard", None),
            P("shard"),
            P("shard"),
            P("shard", None),
            P("shard", None, None),
            P("shard", None, None),
        ),
        check_vma=False,
    )
```

```python
import jax
import jax.numpy as jnp
from jax import lax
from jax.experimental import pallas as pl
from jax.experimental.pallas import tpu as pltpu
from jax.sharding import PartitionSpec as P

MESH = pl.DeviceIdType.MESH
VMEM_BYTES = 64 * 1024 * 1024 - 256 * 1024

HEADS = 12
HEAD_DIM = 64
SEQ = 197
CAP = 112


epsilon = 1e-06
score_scale = 0.125


def normalize(inputs):
    centred = inputs - jnp.mean(inputs, axis=-1, keepdims=True)
    inverse = lax.rsqrt(jnp.mean(centred * centred, axis=-1, keepdims=True) + epsilon)
    return (centred * inverse, inverse)


def norm_back(upstream, normed, inverse):
    return inverse * (
        upstream
        - jnp.mean(upstream, axis=-1, keepdims=True)
        - normed * jnp.mean(upstream * normed, axis=-1, keepdims=True)
    )


def to_heads(matrix, images):
    return matrix.reshape(images, -1, HEADS, HEAD_DIM)


def shards(
    tokens,
    cotangent,
    expert_index,
    slot_index,
    kept_mask,
    gain_attn,
    shift_attn,
    w_qkv,
    w_proj,
    gain_moe,
    shift_moe,
    w_router,
    w_in,
    w_out,
):
    model_width = tokens.shape[1]
    images = tokens.shape[0] // SEQ
    rows = tokens.shape[0]
    experts = w_in.shape[1]
    group = lax.axis_size("shard")
    low = jnp.bfloat16
    wide = jnp.float32

    def gathered(value):
        return lax.all_gather(value, "shard", axis=0, tiled=True)

    qkv_full = gathered(w_qkv.astype(low))
    proj_full = gathered(w_proj.astype(low))
    smalls = gathered(
        jnp.concatenate(
            [
                jnp.stack([gain_attn, shift_attn, gain_moe, shift_moe], axis=1),
                w_router,
            ],
            axis=1,
        ).astype(low)
    )
    gain_first, shift_first, gain_second, shift_second = (
        smalls[:, index].astype(wide) for index in range(4)
    )
    router_full = smalls[:, 4:]
    inner_part = lax.all_to_all(w_in.astype(low), "shard", split_axis=2, concat_axis=0, tiled=True)
    outer_part = w_out.astype(low)
    upstream_all = gathered(cotangent).reshape(group, rows, model_width)
    flat_slots = jnp.where(kept_mask == 1, expert_index * CAP + slot_index, -1)
    slots_all = gathered(flat_slots).reshape(group, rows, 2)
    slot_numbers = jnp.arange(experts * CAP, dtype=jnp.int32)
    picks = slots_all[:, None, :, :] == slot_numbers[None, :, None, None]
    placed = jnp.any(picks, axis=-1)
    placed_low = placed.astype(low)

    inputs = tokens.astype(wide)
    normed_one, inverse_one = normalize(inputs)
    ln_one = (normed_one * gain_first + shift_first).astype(low)
    triple = jnp.dot(ln_one, qkv_full, preferred_element_type=wide).astype(low)
    queries = to_heads(triple[:, :model_width], images)
    key_rows = to_heads(triple[:, model_width : 2 * model_width], images)
    value_rows = to_heads(triple[:, 2 * model_width :], images)
    scores = (
        jnp.einsum("ishd,ithd->ihst", queries, key_rows, preferred_element_type=wide) * score_scale
    )
    attn_probs = jax.nn.softmax(scores, axis=-1)
    mixed_heads = (
        jnp.einsum(
            "ihst,ithd->ishd", attn_probs.astype(low), value_rows, preferred_element_type=wide
        )
        .reshape(-1, model_width)
        .astype(low)
    )
    residual = inputs + jnp.dot(mixed_heads, proj_full, preferred_element_type=wide)
    normed_two, inverse_two = normalize(residual)
    ln_two = (normed_two * gain_second + shift_second).astype(low)
    ln_two_all = gathered(ln_two).reshape(group, rows, model_width)
    logits = jnp.einsum("btd,de->bte", ln_two_all, router_full, preferred_element_type=wide)
    probs_all = jax.nn.softmax(logits, axis=-1)
    me = lax.axis_index("shard")
    router_probs = lax.dynamic_index_in_dim(probs_all, me, 0, keepdims=False)
    placed_own = lax.dynamic_index_in_dim(placed, me, 0, keepdims=False).astype(wide)
    probs_slots = jnp.repeat(jnp.transpose(probs_all, (0, 2, 1)), CAP, axis=1)
    gate_slots = jnp.sum(placed.astype(wide) * probs_slots, axis=-1)

    def to_slots(values):
        return jnp.einsum("bst,btd->bsd", placed_low, values, preferred_element_type=wide)

    def to_experts(values):
        width = values.shape[-1]
        return jnp.transpose(values.reshape(group, experts, CAP, width), (1, 0, 2, 3)).reshape(
            experts, group * CAP, width
        )

    def from_experts(values):
        width = values.shape[-1]
        return jnp.transpose(values.reshape(experts, group, CAP, width), (1, 0, 2, 3)).reshape(
            group, experts * CAP, width
        )

    def to_tokens(values):
        return jnp.einsum("bst,bsd->btd", placed_low, values, preferred_element_type=wide)

    dispatched = to_experts(to_slots(ln_two_all).astype(low))
    upstream_slots = to_slots(upstream_all)
    outer_grad = to_experts((upstream_slots * gate_slots[:, :, None]).astype(low))
    hidden_pre = jnp.einsum("ecd,def->ecf", dispatched, inner_part, preferred_element_type=wide)
    hidden_act, gelu_pull = jax.vjp(jax.nn.gelu, hidden_pre)
    active = hidden_act.astype(low)
    outer_wgrad = jnp.einsum("ecf,ecd->fed", active, outer_grad, preferred_element_type=wide)
    outer_owned = lax.psum(outer_wgrad.astype(low), "rep").astype(wide)
    active_grad = jnp.einsum("ecd,fed->ecf", outer_grad, outer_part, preferred_element_type=wide)
    inner_grad = gelu_pull(active_grad)[0].astype(low)
    inner_wgrad = jnp.einsum("ecd,ecf->def", dispatched, inner_grad, preferred_element_type=wide)
    inner_rows = lax.all_to_all(
        inner_wgrad.astype(low).reshape(group, -1, experts, inner_part.shape[2]),
        "shard",
        split_axis=0,
        concat_axis=0,
        tiled=True,
    )
    slot_grad = from_experts(
        jnp.einsum("ecf,def->ecd", inner_grad, inner_part, preferred_element_type=wide).astype(low)
    )

    def scattered(values):
        return lax.psum_scatter(values, "shard", scatter_dimension=0, tiled=True)

    raise_grad = scattered(to_tokens(slot_grad).astype(low).reshape(-1, model_width)).astype(wide)
    expert_out = from_experts(
        jnp.einsum("ecf,fed->ecd", active, outer_part, preferred_element_type=wide)
    )
    mixture = scattered(
        to_tokens((expert_out * gate_slots[:, :, None]).astype(low))
        .astype(low)
        .reshape(-1, model_width)
    )
    output = (residual + mixture.astype(wide)).astype(low)
    gate_part = scattered(jnp.sum(expert_out * upstream_slots, axis=-1)).reshape(experts * CAP)
    prob_grad = jnp.transpose(
        jnp.sum((placed_own * gate_part[:, None]).reshape(experts, CAP, rows), axis=1)
    )
    upstream = cotangent.astype(wide)
    logit_grad = (
        router_probs * (prob_grad - jnp.sum(router_probs * prob_grad, axis=-1, keepdims=True))
    ).astype(low)
    ln_two_grad = raise_grad + jnp.einsum(
        "te,de->td", logit_grad, router_full, preferred_element_type=wide
    )
    router_wgrad = jnp.einsum("td,te->de", ln_two, logit_grad, preferred_element_type=wide)
    gain_two_grad = jnp.sum(ln_two_grad * normed_two, axis=0)
    shift_two_grad = jnp.sum(ln_two_grad, axis=0)
    residual_grad = upstream + norm_back(ln_two_grad * gain_second, normed_two, inverse_two)
    attn_grad = residual_grad.astype(low)
    proj_wgrad = jnp.einsum("tc,td->cd", mixed_heads, attn_grad, preferred_element_type=wide)
    mixed_grad = to_heads(
        jnp.einsum("td,cd->tc", attn_grad, proj_full, preferred_element_type=wide).astype(low),
        images,
    )
    value_grad = jnp.einsum(
        "ihst,ishd->ithd", attn_probs.astype(low), mixed_grad, preferred_element_type=wide
    )
    prob_attn_grad = jnp.einsum(
        "ishd,ithd->ihst", mixed_grad, value_rows, preferred_element_type=wide
    )
    score_grad = (
        attn_probs
        * (prob_attn_grad - jnp.sum(attn_probs * prob_attn_grad, axis=-1, keepdims=True))
        * score_scale
    ).astype(low)
    query_grad = jnp.einsum("ihst,ithd->ishd", score_grad, key_rows, preferred_element_type=wide)
    key_grad = jnp.einsum("ihst,ishd->ithd", score_grad, queries, preferred_element_type=wide)
    triple_grad = jnp.concatenate(
        [
            query_grad.reshape(-1, model_width),
            key_grad.reshape(-1, model_width),
            value_grad.reshape(-1, model_width),
        ],
        axis=1,
    ).astype(low)
    qkv_wgrad = jnp.einsum("tc,td->cd", ln_one, triple_grad, preferred_element_type=wide)
    ln_one_grad = jnp.einsum("td,cd->tc", triple_grad, qkv_full, preferred_element_type=wide)
    gain_one_grad = jnp.sum(ln_one_grad * normed_one, axis=0)
    shift_one_grad = jnp.sum(ln_one_grad, axis=0)
    input_grad = (
        residual_grad + norm_back(ln_one_grad * gain_first, normed_one, inverse_one)
    ).astype(low)
    small_grads = jnp.concatenate(
        [
            jnp.stack([gain_one_grad, shift_one_grad, gain_two_grad, shift_two_grad], axis=1),
            router_wgrad,
        ],
        axis=1,
    )
    attn_shares = scattered(jnp.concatenate([qkv_wgrad, proj_wgrad, small_grads], axis=1).astype(low))
    inner_flat, attn_total = lax.psum((inner_rows, attn_shares), "rep")
    inner_owned = jnp.transpose(inner_flat.astype(wide), (1, 2, 0, 3)).reshape(w_in.shape)
    attn_total = attn_total.astype(wide)
    wide_end = w_qkv.shape[1]
    small_end = wide_end + model_width
    return (
        output,
        input_grad,
        attn_total[:, small_end],
        attn_total[:, small_end + 1],
        attn_total[:, :wide_end],
        attn_total[:, wide_end:small_end],
        attn_total[:, small_end + 2],
        attn_total[:, small_end + 3],
        attn_total[:, small_end + 4 :],
        inner_owned,
        outer_owned,
    )


TILE_ROWS = 256
SENT_ROWS = 208
CUTS = 4
Z_STEP = 2.4
Z_LAG = 0.5
DEPTH = 3
PIECE = 96
NEGATIVE = -1e30


def mega(
    tok_ref,
    cot_ref,
    expert_ref,
    slot_ref,
    kept_ref,
    gain_a_ref,
    shift_a_ref,
    gain_m_ref,
    shift_m_ref,
    router_ref,
    qkv_ref,
    proj_ref,
    inner_hbm,
    outer_hbm,
    out_ref,
    igrad_ref,
    go_hbm,
    gi_hbm,
    ga_hbm,
    piece_ref,
    stage,
    outer_ref,
    piece,
    table_buf,
    smalls,
    small_sum,
    wq,
    wp,
    win,
    normed_a,
    inv_a,
    ln_a,
    tri,
    probs,
    heads,
    resid,
    mean_m,
    inv_m,
    rows_buf,
    onehot,
    work,
    og,
    route,
    act,
    slope,
    route_grad,
    st_back,
    sr_back,
    rr_back,
    sr_out,
    rr_out,
    grad_in,
    grad_in_own,
    grad_out,
    grad_attn,
    mid_in,
    mid_out,
    mid_attn,
    end_in,
    end_out,
    end_attn,
    res_grad,
    agrad,
    mgrad,
    small_grad,
    small_swap,
    send_sems,
    recv_sems,
    local_sems,
):
    low = jnp.bfloat16
    wide = jnp.float32
    width = tok_ref.shape[1]
    shard = lax.axis_index("shard")
    rep = lax.axis_index("rep")

    def flip(j):
        out = shard
        for bit in range(3):
            if (j >> bit) & 1:
                out = out + (1 - 2 * ((shard // (1 << bit)) % 2)) * (1 << bit)
        return out

    peers = [flip(j) for j in range(8)]
    pair = rep + 1 - 2 * (rep % 2)
    across = 3 - rep
    is_mid = jnp.logical_and(rep >= 1, rep <= 2)
    is_end = jnp.logical_not(is_mid)

    ups_base = 8 * TILE_ROWS
    for position in range(16):
        rows_buf[pl.ds(position * TILE_ROWS + SENT_ROWS, TILE_ROWS - SENT_ROWS), :] = jnp.zeros(
            (TILE_ROWS - SENT_ROWS, width), low
        )
    barrier = pltpu.get_barrier_semaphore()
    for j in range(1, 8):
        pl.semaphore_signal(barrier, inc=1, device_id=(peers[j], rep), device_id_type=MESH)
    pl.semaphore_signal(barrier, inc=1, device_id=(shard, pair), device_id_type=MESH)

    @pl.when(is_mid)
    def _():
        pl.semaphore_signal(barrier, inc=1, device_id=(shard, across), device_id_type=MESH)
        pl.semaphore_wait(barrier, 9)

    @pl.when(is_end)
    def _():
        pl.semaphore_wait(barrier, 8)

    count = [0]
    unsent = []
    settled = []

    def describe(src, dst, device):
        index = count[0]
        count[0] += 1
        return pltpu.make_async_remote_copy(
            src_ref=src,
            dst_ref=dst,
            send_sem=send_sems.at[index],
            recv_sem=recv_sems.at[index],
            device_id=device,
            device_id_type=MESH,
        )

    def send(src, dst, j):
        copy = describe(src, dst, (peers[j], rep) if j < 8 else (shard, pair))
        copy.start()
        unsent.append(copy)
        return copy

    def settle(copies):
        for copy in copies:
            copy.wait_send()
            settled.append(id(copy))

    local_count = [0]

    def local(src, dst):
        copy = pltpu.make_async_copy(src, dst, local_sems.at[local_count[0]])
        local_count[0] += 1
        copy.start()
        return copy

    def off(value, unit):
        return pl.multiple_of(value * unit, unit)

    class Gather:
        def __init__(self, view, first, second):
            self.view, self.first, self.second = view, first, second
            self.all = []

        def put(self, at, to, j, half=None):
            copy = send(self.view(at, at, half), self.view(at, to, half), j)
            self.all.append(copy)
            return copy

        def begin(self):
            self.from_x = self.put(0, 2, 2)
            self.from_y = self.put(0, 4, 4)
            self.from_s = [self.put(0, 1, 1)]

        def pass_on(self):
            self.from_x.wait_recv()
            self.far = [self.put(2, 6, 4, self.first)]
            self.from_s.append(self.put(2, 3, 1))
            self.from_y.wait_recv()
            self.far.append(self.put(4, 6, 2, self.second))
            self.from_s.append(self.put(4, 5, 1))

        def last(self):
            for copy in self.far:
                copy.wait_recv()
            self.from_s.append(self.put(6, 7, 1))

    def weight_view(ref):
        def view(at, to, half):
            start = off(peers[at], PIECE)
            if half is None:
                return ref.at[pl.ds(start, PIECE)]
            return ref.at[pl.ds(start + half[0], half[1])]

        return view

    def row_view(base):
        def view(at, to, half):
            first, size = half if half is not None else (0, SENT_ROWS)
            return rows_buf.at[pl.ds(base + to * TILE_ROWS + first, size)]

        return view

    own_rows = pl.ds(off(shard, PIECE), PIECE)
    small_copies = []
    staged = local(inner_hbm.at[0], stage)
    tall, wide_cut = outer_ref.shape[1] // 2, 256

    def outer_stage(e):
        return [
            local(
                outer_hbm.at[e, pl.ds(h * tall, tall), pl.ds(c * wide_cut, wide_cut)],
                probs.at[(e % 2) * 6 + h * 3 + c, pl.ds(0, tall)],
            )
            for h in range(2)
            for c in range(3)
        ]

    outer_staged = [outer_stage(0), outer_stage(1)]
    experts = router_ref.shape[0]
    piece[...] = jnp.zeros(piece.shape, wide)
    piece[0:experts, 0:PIECE] = router_ref[...]
    for row, ref in enumerate((gain_a_ref, shift_a_ref, gain_m_ref, shift_m_ref)):
        piece[experts + row : experts + row + 1, 0:PIECE] = ref[...]
    own_at = lax.broadcasted_iota(jnp.int32, (128, width), 0)
    own_to = lax.broadcasted_iota(jnp.int32, (128, width), 1) - shard * PIECE
    own_pick = jnp.where(jnp.logical_and(own_at == own_to, own_at < PIECE), 1.0, 0.0).astype(low)
    kept = kept_ref[...] == 1
    table_buf[...] = jnp.zeros(table_buf.shape, wide)
    table_buf[8:10, 0:256] = jnp.full((2, 256), experts, wide)
    table_buf[8:10, 0:SEQ] = jnp.where(kept, expert_ref[...], experts).astype(wide)
    table_buf[8:10, 256 : 256 + SEQ] = jnp.where(kept, slot_ref[...], 0).astype(wide)
    smalls[0] = (
        jnp.dot(piece[...].astype(low), own_pick, preferred_element_type=wide) + table_buf[...]
    ).astype(low)
    for j in range(1, 8):
        small_copies.append(send(smalls.at[0], smalls.at[j], j))
    wq[own_rows, :] = qkv_ref[...].astype(low)
    gather_q = Gather(weight_view(wq), (0, 48), (48, 48))
    gather_q.begin()
    wp[own_rows, :] = proj_ref[...].astype(low)
    res_grad[192:SENT_ROWS, :] = jnp.zeros((SENT_ROWS - 192, width), wide)
    res_grad[0:SEQ, :] = cot_ref[...].astype(wide)
    rows_buf[ups_base : ups_base + SENT_ROWS, :] = res_grad[...].astype(low)
    resid[192:TILE_ROWS, :] = jnp.zeros((TILE_ROWS - 192, width), wide)
    resid[0:SEQ, :] = tok_ref[...].astype(wide)
    inputs = resid[...]
    normed, inverse = normalize(inputs)
    normed_a[...] = normed
    inv_a[...] = inverse

    def inner_cast(e):
        for d in range(8):
            grad_in[e, d * PIECE : (d + 1) * PIECE, :] = stage[
                :, d * part : (d + 1) * part
            ].astype(low)

    part = win.shape[2]
    for e in range(experts):
        staged.wait()
        inner_cast(e)
        if e < experts - 1:
            staged = local(inner_hbm.at[e + 1], stage)
        for copy in outer_staged[e]:
            copy.wait()
        for h in range(2):
            for c in range(3):
                outer_ref[e, h * tall : (h + 1) * tall, c * wide_cut : (c + 1) * wide_cut] = probs[
                    (e % 2) * 6 + h * 3 + c, 0:tall, :
                ].astype(low)
        if e == 0:
            outer_staged.append(outer_stage(2))
    gather_q.pass_on()
    half_at = (rep % 2) * (PIECE // 2)

    def inner_half(j):
        return pl.ds(pl.multiple_of(peers[j] * PIECE + half_at, 16), PIECE // 2)

    inner_own = local(grad_in.at[:, own_rows, :], win.at[:, own_rows, :])
    inner_passed = []

    def inner_pass(numbers):
        for j in numbers:
            inner_copies[j].wait_recv()
            rows = win.at[:, inner_half(j), :]
            inner_passed.append(send(rows, rows, 8))

    for copy in small_copies:
        copy.wait_recv()
    total = smalls[0].astype(wide)
    for j in range(1, 8):
        total = total + smalls[j].astype(wide)
    small_sum[...] = total
    gain_first, shift_first = small_sum[3:4, :], small_sum[4:5, :]
    gain_second, shift_second = small_sum[5:6, :], small_sum[6:7, :]
    ln_a[...] = (normed_a[...] * gain_first + shift_first).astype(low)
    slots = onehot.shape[1]
    slot_at = lax.broadcasted_iota(jnp.int32, (slots, TILE_ROWS), 0).astype(wide)

    def route_step(j, carry):
        table = smalls[j].astype(wide)
        first = table[8:9, 0:256] * CAP + table[8:9, 256:512]
        second = table[9:10, 0:256] * CAP + table[9:10, 256:512]
        hit = jnp.logical_or(slot_at == first, slot_at == second)
        onehot[j] = jnp.where(hit, 1.0, 0.0).astype(low)
        return carry

    lax.fori_loop(0, 8, route_step, 0)
    gather_q.last()
    gather_p = Gather(weight_view(wp), (0, 48), (48, 48))
    gather_p.begin()
    for copy in gather_q.from_s:
        copy.wait_recv()

    def triple_step(i, carry):
        columns = pl.ds(off(i, 384), 384)
        tri[:, columns] = jnp.dot(
            ln_a[...], wq[:, columns], preferred_element_type=wide
        ).astype(low)
        return carry

    lax.fori_loop(0, 6, triple_step, 0)
    gather_p.pass_on()
    inner_copies = {
        j: send(
            grad_in.at[:, inner_half(j), :],
            win.at[:, inner_half(0), :],
            j,
        )
        for j in range(1, 8)
    }

    lane = lax.broadcasted_iota(jnp.int32, (TILE_ROWS, 128), 1)
    key_at = lax.broadcasted_iota(jnp.int32, (TILE_ROWS, TILE_ROWS), 1)

    def head_columns(p, third):
        return pl.ds(pl.multiple_of(third * width + p * 128, 128), 128)

    def contract(a, b, da, db):
        return lax.dot_general(a, b, (((da,), (db,)), ((), ())), preferred_element_type=wide)

    def one_head(values, side):
        return jnp.where((lane < 64) == (side == 0), values, jnp.zeros_like(values))

    def attend(p, carry):
        queries = tri[:, head_columns(p, 0)]
        key_rows = tri[:, head_columns(p, 1)]
        value_rows = tri[:, head_columns(p, 2)]
        mixed = []
        for side in range(2):
            scores = contract(one_head(queries, side), key_rows, 1, 1) * score_scale
            scores = jnp.where(key_at < SEQ, scores, NEGATIVE)
            powers = jnp.exp(scores - jnp.max(scores, axis=-1, keepdims=True))
            weights = powers / jnp.sum(powers, axis=-1, keepdims=True)
            probs[2 * p + side] = weights
            mixed.append(jnp.dot(weights.astype(low), value_rows, preferred_element_type=wide))
        heads[:, head_columns(p, 0)] = jnp.where(lane < 64, mixed[0], mixed[1]).astype(low)
        return carry

    lax.fori_loop(0, 6, attend, 0)
    gather_p.last()
    for copy in gather_p.from_s:
        copy.wait_recv()
    residual = resid[...] + jnp.dot(
        heads[...], wp[...], preferred_element_type=wide
    )
    resid[...] = residual
    normed, inverse = normalize(residual)
    mean_m[...] = jnp.mean(residual, axis=-1, keepdims=True)
    inv_m[...] = inverse
    ln_two = (normed * gain_second + shift_second).astype(low)
    rows_buf[0:SENT_ROWS, :] = ln_two[0:SENT_ROWS, :]
    gather_l = Gather(row_view(0), (0, 112), (112, 96))
    gather_l.begin()
    inner_pass((1, 2, 3, 4, 5, 6, 7))
    router = small_sum[...].astype(low)
    lane16 = lax.broadcasted_iota(jnp.int32, (slots, 16), 1)
    expert_of = lax.broadcasted_iota(jnp.int32, (slots, 16), 0)
    own_lane = jnp.logical_and(expert_of >= lane16 * CAP, expert_of < lane16 * CAP + CAP)

    def expert_rows(e, j, blocks=1):
        return pl.ds(pl.multiple_of((e * 8 + j) * CAP, 16), blocks * CAP)

    def dispatch_step(j, carry):
        picks = onehot[j]
        ln_rows = rows_buf[pl.ds(off(j, TILE_ROWS), TILE_ROWS), :]
        sent = jnp.dot(picks, ln_rows, preferred_element_type=wide).astype(low)
        logits = jnp.where(lane16 < experts, contract(sent, router, 1, 1), NEGATIVE)
        powers = jnp.exp(logits - jnp.max(logits, axis=-1, keepdims=True))
        chances = powers / jnp.sum(powers, axis=-1, keepdims=True)
        for e in range(experts):
            rows = expert_rows(e, j)
            work[rows, :] = sent[e * CAP : (e + 1) * CAP]
            route[rows, :] = chances[e * CAP : (e + 1) * CAP]
        return carry

    def upward_step(j, carry):
        up_rows = rows_buf[pl.ds(pl.multiple_of(ups_base + j * TILE_ROWS, 16), TILE_ROWS), :]
        ups = jnp.dot(onehot[j], up_rows, preferred_element_type=wide)
        chances = jnp.concatenate([route[expert_rows(e, j), :] for e in range(experts)], axis=0)
        gate = jnp.sum(jnp.where(own_lane, chances, 0.0), axis=-1, keepdims=True)
        upward = (ups * gate).astype(low)
        for e in range(experts):
            og[expert_rows(e, j), :] = upward[e * CAP : (e + 1) * CAP]
        return carry

    def hidden_step(g):
        def step(e, carry):
            rows = pl.ds(g * 2 * CAP, 2 * CAP)
            sent = work[expert_rows(e, 2 * g, 2), :]
            value = jnp.dot(sent, win[e], preferred_element_type=wide)
            square = value * value
            bend = jnp.tanh(0.7978845608028654 * value * (1.0 + 0.044715 * square))
            act[e, rows, :] = (0.5 * value * (1.0 + bend)).astype(low)
            slope[e, rows, :] = (
                0.5 * (1.0 + bend)
                + 0.5
                * value
                * (1.0 - bend * bend)
                * (0.7978845608028654 * (1.0 + 0.134145 * square))
            ).astype(low)
            return carry

        lax.fori_loop(0, experts, step, 0)

    gather_l.pass_on()
    gather_u = Gather(row_view(ups_base), (0, 112), (112, 96))
    gather_u.begin()
    gather_l.from_s[0].wait_recv()
    lax.fori_loop(0, 2, dispatch_step, 0)
    gather_l.last()
    for g in range(1, 3):
        gather_l.from_s[g].wait_recv()
        lax.fori_loop(2 * g, 2 * g + 2, dispatch_step, 0)
    gather_u.pass_on()
    inner_own.wait()
    for copy in inner_passed:
        copy.wait_recv()
    hidden_step(0)
    hidden_step(1)
    hidden_step(2)
    gather_l.from_s[3].wait_recv()
    lax.fori_loop(6, 8, dispatch_step, 0)
    gather_u.last()
    hidden_step(3)
    for copy in gather_u.from_s:
        copy.wait_recv()
    lax.fori_loop(0, 8, upward_step, 0)

    ready, raised, left = [], [], []

    class Copies:
        def __init__(self, own, mid, end, out, rows):
            self.own, self.mid, self.end, self.out, self.rows = own, mid, end, out, rows
            self.up = describe(own, end, (shard, pair))
            self.over = describe(own, mid, (shard, across))
            self.down = describe(end, end, (shard, pair))
            self.write = pltpu.make_async_copy(end, out, local_sems.at[local_count[0]])
            local_count[0] += 1

        def add(self, target, other):
            size = self.rows

            def step(i, carry):
                at = pl.ds(pl.multiple_of(i * size, 16), size)
                target[at, :] = (
                    self.own[at, :].astype(wide) + other[at, :].astype(wide)
                ).astype(low)
                return carry

            lax.fori_loop(0, target.shape[0] // size, step, 0)

        def rise(self):
            ready.append(self)
            pump()

        def cross(self):
            self.up.wait_recv()
            self.add(self.own, self.end)
            self.over.start()

        def fall(self):
            self.over.wait_recv()
            self.add(self.end, self.mid)
            self.down.start()
            self.write.start()

    out_cut, in_cut = part // CUTS, grad_in_own.shape[2] // CUTS
    out_copies = [
        Copies(
            *(
                ref.at[e, pl.ds(h * out_cut, out_cut)]
                for ref in (grad_out, mid_out, end_out, go_hbm)
            ),
            48,
        )
        for e in range(experts)
        for h in range(CUTS)
    ]
    in_copies = [
        Copies(
            *(
                ref.at[e, :, pl.ds(h * in_cut, in_cut)]
                for ref in (grad_in_own, mid_in, end_in, gi_hbm)
            ),
            48,
        )
        for e in range(experts)
        for h in range(CUTS)
    ]
    attn_copies = {
        p: Copies(
            *(ref.at[pl.ds(p * PIECE, size)] for ref in (grad_attn, mid_attn, end_attn, ga_hbm)),
            size // 2 if size > 16 else size,
        )
        for p, size in ((3, PIECE), (2, PIECE), (1, PIECE), (0, PIECE), (4, 16))
    }
    all_copies = out_copies + in_copies + list(attn_copies.values())

    def pump():
        @pl.when(is_end)
        def _():
            while len(raised) < len(ready) and len(raised) < len(left) + DEPTH:
                ready[len(raised)].up.start()
                raised.append(1)

    plan = []
    moment = 0.0
    for number, copies in enumerate(all_copies):
        span = Z_STEP if number < 2 * experts * CUTS else 3.2
        moment += span
        plan.append((moment + span + Z_LAG, 0, copies))
        plan.append((moment + 3 * span + 2 * Z_LAG, 1, copies))
    plan.sort(key=lambda step: step[:2])

    def tend(until):
        while plan and plan[0][0] <= until:
            _, kind, copies = plan[0]
            if kind == 0 and len(ready) <= len(left):
                break
            plan.pop(0)

            @pl.when(is_mid)
            def _():
                (copies.fall if kind else copies.cross)()

            if kind == 0:

                @pl.when(is_end)
                def _():
                    copies.up.wait_send()

                left.append(1)
                pump()

    for e in range(experts):
        grad_out[e] = contract(act[e], og[expert_rows(e, 0, 8), :], 0, 0).astype(low)
        for h in range(CUTS):
            out_copies[CUTS * e + h].rise()

    settle(gather_l.all)
    settle(inner_copies.values())
    settle(gather_u.all)
    route_grad[...] = jnp.zeros(route_grad.shape, wide)
    half = act.shape[1] // 2
    lane_h = lax.broadcasted_iota(jnp.int32, (half, 16), 1)

    def inner_step(i, carry):
        e = i // 2
        rows = pl.ds(off(i % 2, half), half)
        flat = pl.ds(pl.multiple_of(i * half, 16), half)
        inner = contract(og[flat, :], outer_ref[e], 1, 1) * slope[e, rows, :].astype(wide)
        slope[e, rows, :] = inner.astype(low)
        return carry

    def back_step(i, carry):
        e = i // 2
        rows = pl.ds(off(i % 2, half), half)
        flat = pl.ds(pl.multiple_of(i * half, 16), half)
        upward = og[flat, :]
        gone = jnp.dot(act[e, rows, :], outer_ref[e], preferred_element_type=wide)
        chances = route[flat, :]
        gate = jnp.sum(jnp.where(lane_h == e, chances, 0.0), axis=-1, keepdims=True)
        pull = jnp.sum(upward.astype(wide) * gone, axis=-1, keepdims=True)
        logit = (pull * (jnp.where(lane_h == e, 1.0, 0.0) - chances)).astype(low)
        logit = jnp.where(lane_h < experts, logit, jnp.zeros_like(logit))
        rows_buf[flat, :] = (gone * gate).astype(low)
        og[flat, :] = (
            contract(slope[e, rows, :], win[e], 1, 1)
            + jnp.dot(logit, router, preferred_element_type=wide)
        ).astype(low)
        route_grad[...] += contract(logit, work[flat, :], 0, 0)
        return carry

    grad_in_copies = []

    def grad_in_send(e):
        target = grad_in_own.at[e, :, pl.ds(off(shard, part), part)]
        grad_in_copies.append(
            [
                send(grad_in.at[e, pl.ds(off(peers[j], PIECE), PIECE), :], target, j)
                for j in range(1, 8)
            ]
        )
        grad_in_copies[e].append(local(grad_in.at[e, own_rows, :], target))

    def grad_in_wait(e):
        for copy in grad_in_copies[e][:7]:
            copy.wait_recv()
        grad_in_copies[e][7].wait()
        for h in range(CUTS):
            in_copies[CUTS * e + h].rise()

    for e in range(experts):
        lax.fori_loop(2 * e, 2 * e + 2, inner_step, 0)
        grad_in[e] = contract(work[expert_rows(e, 0, 8), :], slope[e], 0, 0).astype(low)
        if e < experts - 1:
            grad_in_send(e)
        tend(4 + 2 * e)
    for e in range(experts):
        lax.fori_loop(2 * e, 2 * e + 2, back_step, 0)
        tend(10.5 + 2.3 * e)

    def combine_back(j):
        joined = jnp.concatenate([og[expert_rows(e, j), :] for e in range(experts)], axis=0)
        return contract(onehot[j], joined, 0, 0)[0:SENT_ROWS]

    def combine_out(j):
        joined = jnp.concatenate(
            [rows_buf[expert_rows(e, j), :] for e in range(experts)], axis=0
        )
        return contract(onehot[j], joined, 0, 0)[0:SENT_ROWS]

    stage_out = experts * 8 * CAP

    def odd_back(i, carry):
        st_back[i] = combine_back(2 * i + 1).astype(low)
        return carry

    lax.fori_loop(0, 4, odd_back, 0)
    swap_back = send(st_back, sr_back, 1)
    tend(17)

    def odd_out(i, carry):
        rows = pl.ds(pl.multiple_of(stage_out + i * SENT_ROWS, 16), SENT_ROWS)
        rows_buf[rows, :] = combine_out(2 * i + 1).astype(low)
        return carry

    lax.fori_loop(0, 4, odd_out, 0)
    tend(19)
    swap_back.wait_recv()

    def even_back(i, carry):
        sr_back[i] = (combine_back(2 * i) + sr_back[i].astype(wide)).astype(low)
        return carry

    lax.fori_loop(0, 4, even_back, 0)
    back_copies = [send(sr_back.at[i], rr_back.at[i - 1], 2 * i) for i in range(1, 4)]
    swap_out = send(rows_buf.at[pl.ds(stage_out, 4 * SENT_ROWS)], sr_out, 1)
    tend(22)
    swap_out.wait_recv()

    def even_out(i, carry):
        rows = pl.ds(off(i, SENT_ROWS), SENT_ROWS)
        sr_out[rows, :] = (combine_out(2 * i) + sr_out[rows, :].astype(wide)).astype(low)
        return carry

    lax.fori_loop(0, 4, even_out, 0)
    tend(25)
    for e in range(experts - 1):
        grad_in_wait(e)
    tend(38)

    for copy in back_copies:
        copy.wait_recv()
    grad_in_send(experts - 1)
    ln_grad = sr_back[0].astype(wide)
    for i in range(3):
        ln_grad = ln_grad + rr_back[i].astype(wide)
    normed = (resid[0:SENT_ROWS, :] - mean_m[0:SENT_ROWS, :]) * inv_m[0:SENT_ROWS, :]
    gain_m_grad = jnp.sum(ln_grad * normed, axis=0, keepdims=True)
    shift_m_grad = jnp.sum(ln_grad, axis=0, keepdims=True)
    upstream = res_grad[...]
    residual_grad = upstream + norm_back(
        ln_grad * gain_second, normed, inv_m[0:SENT_ROWS, :]
    )
    res_grad[...] = residual_grad
    agrad[...] = jnp.zeros(agrad.shape, low)
    agrad[0:SENT_ROWS, :] = residual_grad.astype(low)
    mgrad[...] = contract(agrad[...], wp[...], 1, 1).astype(low)

    def grad_rows(part, j):
        return pl.ds(pl.multiple_of(part * width + peers[j] * PIECE, 16), PIECE)

    def kept_rows(part, i):
        return pl.ds((i * 4 + part) * PIECE, PIECE)

    def come_rows(part, i):
        return pl.ds((16 + i * 4 + part) * PIECE, PIECE)

    def share(part):
        return [
            send(work.at[grad_rows(part, 2 * i + 1)], og.at[kept_rows(part, i)], 1)
            for i in range(4)
        ]

    def gather_share(part, copies):
        sent = []
        for i in range(4):
            copies[i].wait_recv()
            rows = kept_rows(part, i)
            og[rows, :] = (
                work[grad_rows(part, 2 * i), :].astype(wide) + og[rows, :].astype(wide)
            ).astype(low)
            if i > 0:
                sent.append(send(og.at[rows], og.at[come_rows(part, i - 1)], 2 * i))
        return sent

    def total_share(part, copies):
        total = og[kept_rows(part, 0), :].astype(wide)
        for i in range(3):
            copies[i].wait_recv()
            total = total + og[come_rows(part, i), :].astype(wide)
        grad_attn[pl.ds(part * PIECE, PIECE), :] = total.astype(low)
        attn_copies[part].rise()

    def attend_back(p, carry):
        queries = tri[:, head_columns(p, 0)]
        key_rows = tri[:, head_columns(p, 1)]
        value_rows = tri[:, head_columns(p, 2)]
        mixed = mgrad[:, head_columns(p, 0)]
        results = []
        for side in range(2):
            weights = probs[2 * p + side]
            value_grad = contract(weights.astype(low), mixed, 0, 0)
            weight_grad = contract(one_head(mixed, side), value_rows, 1, 1)
            score_grad = (
                weights
                * (weight_grad - jnp.sum(weights * weight_grad, axis=-1, keepdims=True))
                * score_scale
            ).astype(low)
            query_grad = jnp.dot(score_grad, key_rows, preferred_element_type=wide)
            key_grad = contract(score_grad, queries, 0, 0)
            results.append((query_grad, key_grad, value_grad))
        for third in range(3):
            tri[:, head_columns(p, third)] = jnp.where(
                lane < 64, results[0][third], results[1][third]
            ).astype(low)
        return carry

    work[3 * width : 4 * width, :] = contract(heads[...], agrad[...], 0, 0).astype(low)
    share_p = share(3)
    tend(43)
    lax.fori_loop(0, 3, attend_back, 0)
    tend(46)
    lax.fori_loop(3, 6, attend_back, 0)
    tend(50)

    def weight_grad_of(part):
        work[part * width : (part + 1) * width, :] = contract(
            ln_a[...], tri[:, part * width : (part + 1) * width], 0, 0
        ).astype(low)

    weight_grad_of(2)
    share_v = share(2)
    come_p = gather_share(3, share_p)
    weight_grad_of(1)
    share_k = share(1)
    come_v = gather_share(2, share_v)
    weight_grad_of(0)
    share_q = share(0)
    come_k = gather_share(1, share_k)
    tend(54)
    ln_grad = contract(tri[0:SENT_ROWS, :], wq[...], 1, 1)
    come_q = gather_share(0, share_q)
    normed = normed_a[0:SENT_ROWS, :]
    gain_a_grad = jnp.sum(ln_grad * normed, axis=0, keepdims=True)
    shift_a_grad = jnp.sum(ln_grad, axis=0, keepdims=True)
    row16 = lax.broadcasted_iota(jnp.int32, (16, width), 0)
    small = jnp.where(row16 < experts, route_grad[...], 0.0)
    for row, value in (
        (3, gain_a_grad),
        (4, shift_a_grad),
        (5, gain_m_grad),
        (6, shift_m_grad),
    ):
        small = small + jnp.where(row16 == row, value, 0.0)
    small_grad[0] = small.astype(low)
    swap = send(small_grad.at[0], small_swap.at[0], 1)
    igrad_ref[...] = (
        res_grad[...] + norm_back(ln_grad * gain_first, normed, inv_a[0:SENT_ROWS, :])
    ).astype(low)
    grad_in_wait(experts - 1)
    tend(57)
    for step in range(2):
        swap.wait_recv()
        small_grad[step + 1] = (
            small_grad[step].astype(wide) + small_swap[step].astype(wide)
        ).astype(low)
        swap = send(small_grad.at[step + 1], small_swap.at[step + 1], 2 << step)
        tend(60 + 3 * step)
    out_sends = [
        send(sr_out.at[pl.ds(i * SENT_ROWS, SENT_ROWS)], rr_out.at[i - 1], 2 * i)
        for i in range(1, 4)
    ]
    tend(72)
    total_share(3, come_p)
    total_share(2, come_v)
    tend(76)
    total_share(1, come_k)
    total_share(0, come_q)
    swap.wait_recv()
    grad_attn[4 * PIECE : 4 * PIECE + 16, :] = (
        small_grad[2].astype(wide) + small_swap[2].astype(wide)
    ).astype(low)
    attn_copies[4].rise()
    tend(84)
    tend(1000)
    output = resid[0:SENT_ROWS, :] + sr_out[0:SENT_ROWS, :].astype(wide)
    for i in range(3):
        out_sends[i].wait_recv()
        output = output + rr_out[i].astype(wide)
    out_ref[...] = output.astype(low)
    for copies in all_copies:

        @pl.when(is_end)
        def _():
            copies.down.wait_recv()
            copies.write.start()

        @pl.when(is_mid)
        def _():
            copies.over.wait_send()
            copies.down.wait_send()

    for copies in all_copies:
        copies.write.wait()
    assert count[0] <= send_sems.shape[0] and local_count[0] <= local_sems.shape[0]
    piece_ref[...] = contract(end_attn[4 * PIECE : 4 * PIECE + 16, :], own_pick, 1, 1)
    for copy in unsent:
        if id(copy) not in settled:
            copy.wait_send()


def finish(
    out_in,
    igrad_in,
    outer_in,
    inner_in,
    attn_in,
    small_in,
    out_ref,
    igrad_ref,
    outer_ref,
    inner_ref,
    qkv_ref,
    proj_ref,
    router_ref,
    gain_a_ref,
    shift_a_ref,
    gain_m_ref,
    shift_m_ref,
):
    wide = jnp.float32
    outer_ref[...] = outer_in[...].astype(wide)
    inner_ref[...] = inner_in[...].astype(wide)

    @pl.when(pl.program_id(0) == 0)
    def _():
        rows, width = out_ref.shape
        out_ref[...] = out_in[0:rows, :]
        igrad_ref[...] = igrad_in[0:rows, :]
        for third in range(3):
            qkv_ref[:, third * width : (third + 1) * width] = attn_in[
                third * PIECE : (third + 1) * PIECE, :
            ].astype(wide)
        proj_ref[...] = attn_in[3 * PIECE : 4 * PIECE, :].astype(wide)
        experts = router_ref.shape[0]
        router_ref[...] = small_in[0:experts, 0:PIECE]
        for row, ref in enumerate((gain_a_ref, shift_a_ref, gain_m_ref, shift_m_ref)):
            ref[...] = small_in[experts + row : experts + row + 1, 0:PIECE]


def grouped(
    tokens,
    cotangent,
    expert_index,
    slot_index,
    kept_mask,
    gain_attn,
    shift_attn,
    w_qkv,
    w_proj,
    gain_moe,
    shift_moe,
    w_router,
    w_in,
    w_out,
):
    low = jnp.bfloat16
    wide = jnp.float32
    rows, width = tokens.shape
    owned, experts, hidden = w_in.shape
    part = w_out.shape[0]
    shard = lax.axis_index("shard")
    slots = experts * CAP
    total_slots = 8 * slots
    vmem = pltpu.VMEM
    token_shape = jax.ShapeDtypeStruct((SENT_ROWS, width), low)
    attn_rows = 4 * PIECE + 16
    scratch = [
        vmem((owned, hidden), wide),
        vmem((experts, part, width), low),
        vmem((16, 128), wide),
        vmem((16, width), wide),
        vmem((8, 16, width), low),
        vmem((16, width), wide),
        vmem((width, 3 * width), low),
        vmem((width, width), low),
        vmem((experts, width, part), low),
        vmem((TILE_ROWS, width), wide),
        vmem((TILE_ROWS, 1), wide),
        vmem((TILE_ROWS, width), low),
        vmem((TILE_ROWS, 3 * width), low),
        vmem((HEADS, TILE_ROWS, TILE_ROWS), wide),
        vmem((TILE_ROWS, width), low),
        vmem((TILE_ROWS, width), wide),
        vmem((TILE_ROWS, 1), wide),
        vmem((TILE_ROWS, 1), wide),
        vmem((16 * TILE_ROWS, width), low),
        vmem((8, slots, TILE_ROWS), low),
        vmem((4 * width, width), low),
        vmem((total_slots, width), low),
        vmem((total_slots, 16), wide),
        vmem((experts, 8 * CAP, part), low),
        vmem((experts, 8 * CAP, part), low),
        vmem((16, width), wide),
        vmem((4, SENT_ROWS, width), low),
        vmem((4, SENT_ROWS, width), low),
        vmem((3, SENT_ROWS, width), low),
        vmem((4 * SENT_ROWS, width), low),
        vmem((3, SENT_ROWS, width), low),
        vmem((experts, width, part), low),
        vmem((experts, owned, hidden), low),
        vmem((experts, part, width), low),
        vmem((attn_rows, width), low),
        vmem((experts, owned, hidden), low),
        vmem((experts, part, width), low),
        vmem((attn_rows, width), low),
        vmem((experts, owned, hidden), low),
        vmem((experts, part, width), low),
        vmem((attn_rows, width), low),
        vmem((SENT_ROWS, width), wide),
        vmem((TILE_ROWS, width), low),
        vmem((TILE_ROWS, width), low),
        vmem((3, 16, width), low),
        vmem((3, 16, width), low),
        pltpu.SemaphoreType.DMA((256,)),
        pltpu.SemaphoreType.DMA((256,)),
        pltpu.SemaphoreType.DMA((64,)),
    ]
    inside = pl.BlockSpec(memory_space=vmem)
    outside = pl.BlockSpec(memory_space=pl.ANY)
    output, input_grad, outer_sum, inner_sum, attn_sum, small_sum = pl.pallas_call(
        mega,
        out_shape=(
            token_shape,
            token_shape,
            jax.ShapeDtypeStruct((experts, part, width), low),
            jax.ShapeDtypeStruct((experts, owned, hidden), low),
            jax.ShapeDtypeStruct((attn_rows, width), low),
            jax.ShapeDtypeStruct((16, 128), wide),
        ),
        in_specs=[inside] * 12 + [outside, outside],
        out_specs=(inside, inside, outside, outside, outside, inside),
        scratch_shapes=scratch,
        compiler_params=pltpu.CompilerParams(
            collective_id=0, has_side_effects=True, vmem_limit_bytes=VMEM_BYTES
        ),
    )(
        tokens,
        cotangent,
        expert_index.T,
        slot_index.T,
        kept_mask.T,
        gain_attn.reshape(1, owned),
        shift_attn.reshape(1, owned),
        gain_moe.reshape(1, owned),
        shift_moe.reshape(1, owned),
        w_router.T,
        w_qkv,
        w_proj,
        jnp.transpose(w_in, (1, 0, 2)),
        jnp.transpose(w_out, (1, 0, 2)),
    )

    def whole(*shape):
        return pl.BlockSpec(shape, lambda e: (0,) * len(shape))

    def one(*shape):
        return pl.BlockSpec((1, *shape), lambda e: (e, 0, 0))

    finals = pl.pallas_call(
        finish,
        grid=(experts,),
        out_shape=(
            jax.ShapeDtypeStruct((rows, width), low),
            jax.ShapeDtypeStruct((rows, width), low),
            jax.ShapeDtypeStruct((experts, part, width), wide),
            jax.ShapeDtypeStruct((experts, owned, hidden), wide),
            jax.ShapeDtypeStruct((owned, 3 * width), wide),
            jax.ShapeDtypeStruct((owned, width), wide),
            jax.ShapeDtypeStruct((experts, owned), wide),
        )
        + (jax.ShapeDtypeStruct((1, owned), wide),) * 4,
        in_specs=[
            whole(SENT_ROWS, width),
            whole(SENT_ROWS, width),
            one(part, width),
            one(owned, hidden),
            whole(attn_rows, width),
            whole(16, 128),
        ],
        out_specs=(
            whole(rows, width),
            whole(rows, width),
            one(part, width),
            one(owned, hidden),
            whole(owned, 3 * width),
            whole(owned, width),
            whole(experts, owned),
        )
        + (whole(1, owned),) * 4,
        compiler_params=pltpu.CompilerParams(vmem_limit_bytes=VMEM_BYTES),
    )(output, input_grad, outer_sum, inner_sum, attn_sum, small_sum)
    return (
        finals[0],
        finals[1],
        finals[7].reshape(owned),
        finals[8].reshape(owned),
        finals[4],
        finals[5],
        finals[9].reshape(owned),
        finals[10].reshape(owned),
        finals[6].T,
        jnp.transpose(finals[3], (1, 0, 2)),
        jnp.transpose(finals[2], (1, 0, 2)),
    )


def solution(mesh):
    sizes = (mesh.shape["shard"], mesh.shape["rep"])
    return jax.shard_map(
        grouped if sizes == (8, 4) else shards,
        mesh=mesh,
        in_specs=(
            P(("shard", "rep"), None),
            P(("shard", "rep"), None),
            P(("shard", "rep"), None),
            P(("shard", "rep"), None),
            P(("shard", "rep"), None),
            P("shard"),
            P("shard"),
            P("shard", None),
            P("shard", None),
            P("shard"),
            P("shard"),
            P("shard", None),
            P("shard", None, None),
            P("shard", None, None),
        ),
        out_specs=(
            P(("shard", "rep"), None),
            P(("shard", "rep"), None),
            P("shard"),
            P("shard"),
            P("shard", None),
            P("shard", None),
            P("shard"),
            P("shard"),
            P("shard", None),
            P("shard", None, None),
            P("shard", None, None),
        ),
        check_vma=False,
    )
```

```python
import jax
import jax.numpy as jnp
from jax import lax
from jax.experimental import pallas as pl
from jax.experimental.pallas import tpu as pltpu
from jax.sharding import PartitionSpec as P

MESH = pl.DeviceIdType.MESH
VMEM_BYTES = 64 * 1024 * 1024 - 256 * 1024

HEADS = 12
HEAD_DIM = 64
SEQ = 197
CAP = 112


epsilon = 1e-06
score_scale = 0.125


def normalize(inputs):
    centred = inputs - jnp.mean(inputs, axis=-1, keepdims=True)
    inverse = lax.rsqrt(jnp.mean(centred * centred, axis=-1, keepdims=True) + epsilon)
    return (centred * inverse, inverse)


def norm_back(upstream, normed, inverse):
    return inverse * (
        upstream
        - jnp.mean(upstream, axis=-1, keepdims=True)
        - normed * jnp.mean(upstream * normed, axis=-1, keepdims=True)
    )


def to_heads(matrix, images):
    return matrix.reshape(images, -1, HEADS, HEAD_DIM)


def shards(
    tokens,
    cotangent,
    expert_index,
    slot_index,
    kept_mask,
    gain_attn,
    shift_attn,
    w_qkv,
    w_proj,
    gain_moe,
    shift_moe,
    w_router,
    w_in,
    w_out,
):
    model_width = tokens.shape[1]
    images = tokens.shape[0] // SEQ
    rows = tokens.shape[0]
    experts = w_in.shape[1]
    group = lax.axis_size("shard")
    low = jnp.bfloat16
    wide = jnp.float32

    def gathered(value):
        return lax.all_gather(value, "shard", axis=0, tiled=True)

    qkv_full = gathered(w_qkv.astype(low))
    proj_full = gathered(w_proj.astype(low))
    smalls = gathered(
        jnp.concatenate(
            [
                jnp.stack([gain_attn, shift_attn, gain_moe, shift_moe], axis=1),
                w_router,
            ],
            axis=1,
        ).astype(low)
    )
    gain_first, shift_first, gain_second, shift_second = (
        smalls[:, index].astype(wide) for index in range(4)
    )
    router_full = smalls[:, 4:]
    inner_part = lax.all_to_all(w_in.astype(low), "shard", split_axis=2, concat_axis=0, tiled=True)
    outer_part = w_out.astype(low)
    upstream_all = gathered(cotangent).reshape(group, rows, model_width)
    flat_slots = jnp.where(kept_mask == 1, expert_index * CAP + slot_index, -1)
    slots_all = gathered(flat_slots).reshape(group, rows, 2)
    slot_numbers = jnp.arange(experts * CAP, dtype=jnp.int32)
    picks = slots_all[:, None, :, :] == slot_numbers[None, :, None, None]
    placed = jnp.any(picks, axis=-1)
    placed_low = placed.astype(low)

    inputs = tokens.astype(wide)
    normed_one, inverse_one = normalize(inputs)
    ln_one = (normed_one * gain_first + shift_first).astype(low)
    triple = jnp.dot(ln_one, qkv_full, preferred_element_type=wide).astype(low)
    queries = to_heads(triple[:, :model_width], images)
    key_rows = to_heads(triple[:, model_width : 2 * model_width], images)
    value_rows = to_heads(triple[:, 2 * model_width :], images)
    scores = (
        jnp.einsum("ishd,ithd->ihst", queries, key_rows, preferred_element_type=wide) * score_scale
    )
    attn_probs = jax.nn.softmax(scores, axis=-1)
    mixed_heads = (
        jnp.einsum(
            "ihst,ithd->ishd", attn_probs.astype(low), value_rows, preferred_element_type=wide
        )
        .reshape(-1, model_width)
        .astype(low)
    )
    residual = inputs + jnp.dot(mixed_heads, proj_full, preferred_element_type=wide)
    normed_two, inverse_two = normalize(residual)
    ln_two = (normed_two * gain_second + shift_second).astype(low)
    ln_two_all = gathered(ln_two).reshape(group, rows, model_width)
    logits = jnp.einsum("btd,de->bte", ln_two_all, router_full, preferred_element_type=wide)
    probs_all = jax.nn.softmax(logits, axis=-1)
    me = lax.axis_index("shard")
    router_probs = lax.dynamic_index_in_dim(probs_all, me, 0, keepdims=False)
    placed_own = lax.dynamic_index_in_dim(placed, me, 0, keepdims=False).astype(wide)
    probs_slots = jnp.repeat(jnp.transpose(probs_all, (0, 2, 1)), CAP, axis=1)
    gate_slots = jnp.sum(placed.astype(wide) * probs_slots, axis=-1)

    def to_slots(values):
        return jnp.einsum("bst,btd->bsd", placed_low, values, preferred_element_type=wide)

    def to_experts(values):
        width = values.shape[-1]
        return jnp.transpose(values.reshape(group, experts, CAP, width), (1, 0, 2, 3)).reshape(
            experts, group * CAP, width
        )

    def from_experts(values):
        width = values.shape[-1]
        return jnp.transpose(values.reshape(experts, group, CAP, width), (1, 0, 2, 3)).reshape(
            group, experts * CAP, width
        )

    def to_tokens(values):
        return jnp.einsum("bst,bsd->btd", placed_low, values, preferred_element_type=wide)

    dispatched = to_experts(to_slots(ln_two_all).astype(low))
    upstream_slots = to_slots(upstream_all)
    outer_grad = to_experts((upstream_slots * gate_slots[:, :, None]).astype(low))
    hidden_pre = jnp.einsum("ecd,def->ecf", dispatched, inner_part, preferred_element_type=wide)
    hidden_act, gelu_pull = jax.vjp(jax.nn.gelu, hidden_pre)
    active = hidden_act.astype(low)
    outer_wgrad = jnp.einsum("ecf,ecd->fed", active, outer_grad, preferred_element_type=wide)
    outer_owned = lax.psum(outer_wgrad.astype(low), "rep").astype(wide)
    active_grad = jnp.einsum("ecd,fed->ecf", outer_grad, outer_part, preferred_element_type=wide)
    inner_grad = gelu_pull(active_grad)[0].astype(low)
    inner_wgrad = jnp.einsum("ecd,ecf->def", dispatched, inner_grad, preferred_element_type=wide)
    inner_rows = lax.all_to_all(
        inner_wgrad.astype(low).reshape(group, -1, experts, inner_part.shape[2]),
        "shard",
        split_axis=0,
        concat_axis=0,
        tiled=True,
    )
    slot_grad = from_experts(
        jnp.einsum("ecf,def->ecd", inner_grad, inner_part, preferred_element_type=wide).astype(low)
    )

    def scattered(values):
        return lax.psum_scatter(values, "shard", scatter_dimension=0, tiled=True)

    raise_grad = scattered(to_tokens(slot_grad).astype(low).reshape(-1, model_width)).astype(wide)
    expert_out = from_experts(
        jnp.einsum("ecf,fed->ecd", active, outer_part, preferred_element_type=wide)
    )
    mixture = scattered(
        to_tokens((expert_out * gate_slots[:, :, None]).astype(low))
        .astype(low)
        .reshape(-1, model_width)
    )
    output = (residual + mixture.astype(wide)).astype(low)
    gate_part = scattered(jnp.sum(expert_out * upstream_slots, axis=-1)).reshape(experts * CAP)
    prob_grad = jnp.transpose(
        jnp.sum((placed_own * gate_part[:, None]).reshape(experts, CAP, rows), axis=1)
    )
    upstream = cotangent.astype(wide)
    logit_grad = (
        router_probs * (prob_grad - jnp.sum(router_probs * prob_grad, axis=-1, keepdims=True))
    ).astype(low)
    ln_two_grad = raise_grad + jnp.einsum(
        "te,de->td", logit_grad, router_full, preferred_element_type=wide
    )
    router_wgrad = jnp.einsum("td,te->de", ln_two, logit_grad, preferred_element_type=wide)
    gain_two_grad = jnp.sum(ln_two_grad * normed_two, axis=0)
    shift_two_grad = jnp.sum(ln_two_grad, axis=0)
    residual_grad = upstream + norm_back(ln_two_grad * gain_second, normed_two, inverse_two)
    attn_grad = residual_grad.astype(low)
    proj_wgrad = jnp.einsum("tc,td->cd", mixed_heads, attn_grad, preferred_element_type=wide)
    mixed_grad = to_heads(
        jnp.einsum("td,cd->tc", attn_grad, proj_full, preferred_element_type=wide).astype(low),
        images,
    )
    value_grad = jnp.einsum(
        "ihst,ishd->ithd", attn_probs.astype(low), mixed_grad, preferred_element_type=wide
    )
    prob_attn_grad = jnp.einsum(
        "ishd,ithd->ihst", mixed_grad, value_rows, preferred_element_type=wide
    )
    score_grad = (
        attn_probs
        * (prob_attn_grad - jnp.sum(attn_probs * prob_attn_grad, axis=-1, keepdims=True))
        * score_scale
    ).astype(low)
    query_grad = jnp.einsum("ihst,ithd->ishd", score_grad, key_rows, preferred_element_type=wide)
    key_grad = jnp.einsum("ihst,ishd->ithd", score_grad, queries, preferred_element_type=wide)
    triple_grad = jnp.concatenate(
        [
            query_grad.reshape(-1, model_width),
            key_grad.reshape(-1, model_width),
            value_grad.reshape(-1, model_width),
        ],
        axis=1,
    ).astype(low)
    qkv_wgrad = jnp.einsum("tc,td->cd", ln_one, triple_grad, preferred_element_type=wide)
    ln_one_grad = jnp.einsum("td,cd->tc", triple_grad, qkv_full, preferred_element_type=wide)
    gain_one_grad = jnp.sum(ln_one_grad * normed_one, axis=0)
    shift_one_grad = jnp.sum(ln_one_grad, axis=0)
    input_grad = (
        residual_grad + norm_back(ln_one_grad * gain_first, normed_one, inverse_one)
    ).astype(low)
    small_grads = jnp.concatenate(
        [
            jnp.stack([gain_one_grad, shift_one_grad, gain_two_grad, shift_two_grad], axis=1),
            router_wgrad,
        ],
        axis=1,
    )
    attn_shares = scattered(jnp.concatenate([qkv_wgrad, proj_wgrad, small_grads], axis=1).astype(low))
    inner_flat, attn_total = lax.psum((inner_rows, attn_shares), "rep")
    inner_owned = jnp.transpose(inner_flat.astype(wide), (1, 2, 0, 3)).reshape(w_in.shape)
    attn_total = attn_total.astype(wide)
    wide_end = w_qkv.shape[1]
    small_end = wide_end + model_width
    return (
        output,
        input_grad,
        attn_total[:, small_end],
        attn_total[:, small_end + 1],
        attn_total[:, :wide_end],
        attn_total[:, wide_end:small_end],
        attn_total[:, small_end + 2],
        attn_total[:, small_end + 3],
        attn_total[:, small_end + 4 :],
        inner_owned,
        outer_owned,
    )


TILE_ROWS = 256
SENT_ROWS = 208
CUTS = 4
Z_STEP = 2.4
Z_LAG = 0.5
DEPTH = 3
PIECE = 96
NEGATIVE = -1e30


def mega(
    tok_ref,
    cot_ref,
    expert_ref,
    slot_ref,
    kept_ref,
    gain_a_ref,
    shift_a_ref,
    gain_m_ref,
    shift_m_ref,
    router_ref,
    qkv_ref,
    proj_ref,
    inner_hbm,
    outer_hbm,
    out_ref,
    igrad_ref,
    go_hbm,
    gi_hbm,
    ga_hbm,
    piece_ref,
    stage,
    outer_ref,
    piece,
    table_buf,
    smalls,
    small_sum,
    wq,
    wp,
    win,
    normed_a,
    inv_a,
    ln_a,
    tri,
    probs,
    heads,
    resid,
    mean_m,
    inv_m,
    rows_buf,
    onehot,
    work,
    og,
    route,
    act,
    slope,
    route_grad,
    st_back,
    sr_back,
    rr_back,
    sr_out,
    rr_out,
    grad_in,
    grad_in_own,
    grad_out,
    grad_attn,
    mid_in,
    mid_out,
    mid_attn,
    end_in,
    end_out,
    end_attn,
    res_grad,
    agrad,
    mgrad,
    small_grad,
    small_swap,
    send_sems,
    recv_sems,
    local_sems,
):
    low = jnp.bfloat16
    wide = jnp.float32
    width = tok_ref.shape[1]
    shard = lax.axis_index("shard")
    rep = lax.axis_index("rep")

    def flip(j):
        out = shard
        for bit in range(3):
            if (j >> bit) & 1:
                out = out + (1 - 2 * ((shard // (1 << bit)) % 2)) * (1 << bit)
        return out

    peers = [flip(j) for j in range(8)]
    pair = rep + 1 - 2 * (rep % 2)
    across = 3 - rep
    is_mid = jnp.logical_and(rep >= 1, rep <= 2)
    is_end = jnp.logical_not(is_mid)

    ups_base = 8 * TILE_ROWS
    for position in range(16):
        rows_buf[pl.ds(position * TILE_ROWS + SENT_ROWS, TILE_ROWS - SENT_ROWS), :] = jnp.zeros(
            (TILE_ROWS - SENT_ROWS, width), low
        )
    barrier = pltpu.get_barrier_semaphore()
    for j in range(1, 8):
        pl.semaphore_signal(barrier, inc=1, device_id=(peers[j], rep), device_id_type=MESH)
    pl.semaphore_signal(barrier, inc=1, device_id=(shard, pair), device_id_type=MESH)

    @pl.when(is_mid)
    def _():
        pl.semaphore_signal(barrier, inc=1, device_id=(shard, across), device_id_type=MESH)
        pl.semaphore_wait(barrier, 9)

    @pl.when(is_end)
    def _():
        pl.semaphore_wait(barrier, 8)

    count = [0]
    unsent = []
    settled = []

    def describe(src, dst, device):
        index = count[0]
        count[0] += 1
        return pltpu.make_async_remote_copy(
            src_ref=src,
            dst_ref=dst,
            send_sem=send_sems.at[index],
            recv_sem=recv_sems.at[index],
            device_id=device,
            device_id_type=MESH,
        )

    def send(src, dst, j):
        copy = describe(src, dst, (peers[j], rep) if j < 8 else (shard, pair))
        copy.start()
        unsent.append(copy)
        return copy

    def settle(copies):
        for copy in copies:
            copy.wait_send()
            settled.append(id(copy))

    local_count = [0]

    def local(src, dst):
        copy = pltpu.make_async_copy(src, dst, local_sems.at[local_count[0]])
        local_count[0] += 1
        copy.start()
        return copy

    def off(value, unit):
        return pl.multiple_of(value * unit, unit)

    class Gather:
        def __init__(self, view, first, second):
            self.view, self.first, self.second = view, first, second
            self.all = []

        def put(self, at, to, j, half=None):
            copy = send(self.view(at, at, half), self.view(at, to, half), j)
            self.all.append(copy)
            return copy

        def begin(self):
            self.from_x = self.put(0, 2, 2)
            self.from_y = self.put(0, 4, 4)
            self.from_s = [self.put(0, 1, 1)]

        def pass_on(self):
            self.from_x.wait_recv()
            self.far = [self.put(2, 6, 4, self.first)]
            self.from_s.append(self.put(2, 3, 1))
            self.from_y.wait_recv()
            self.far.append(self.put(4, 6, 2, self.second))
            self.from_s.append(self.put(4, 5, 1))

        def last(self):
            for copy in self.far:
                copy.wait_recv()
            self.from_s.append(self.put(6, 7, 1))

    def weight_view(ref):
        def view(at, to, half):
            start = off(peers[at], PIECE)
            if half is None:
                return ref.at[pl.ds(start, PIECE)]
            return ref.at[pl.ds(start + half[0], half[1])]

        return view

    def row_view(base):
        def view(at, to, half):
            first, size = half if half is not None else (0, SENT_ROWS)
            return rows_buf.at[pl.ds(base + to * TILE_ROWS + first, size)]

        return view

    own_rows = pl.ds(off(shard, PIECE), PIECE)
    small_copies = []
    staged = local(inner_hbm.at[0], stage)
    tall, wide_cut = outer_ref.shape[1] // 2, 256

    def outer_stage(e):
        return [
            local(
                outer_hbm.at[e, pl.ds(h * tall, tall), pl.ds(c * wide_cut, wide_cut)],
                probs.at[(e % 2) * 6 + h * 3 + c, pl.ds(0, tall)],
            )
            for h in range(2)
            for c in range(3)
        ]

    outer_staged = [outer_stage(0), outer_stage(1)]
    experts = router_ref.shape[0]
    piece[...] = jnp.zeros(piece.shape, wide)
    piece[0:experts, 0:PIECE] = router_ref[...]
    for row, ref in enumerate((gain_a_ref, shift_a_ref, gain_m_ref, shift_m_ref)):
        piece[experts + row : experts + row + 1, 0:PIECE] = ref[...]
    own_at = lax.broadcasted_iota(jnp.int32, (128, width), 0)
    own_to = lax.broadcasted_iota(jnp.int32, (128, width), 1) - shard * PIECE
    own_pick = jnp.where(jnp.logical_and(own_at == own_to, own_at < PIECE), 1.0, 0.0).astype(low)
    kept = kept_ref[...] == 1
    table_buf[...] = jnp.zeros(table_buf.shape, wide)
    table_buf[8:10, 0:256] = jnp.full((2, 256), experts, wide)
    table_buf[8:10, 0:SEQ] = jnp.where(kept, expert_ref[...], experts).astype(wide)
    table_buf[8:10, 256 : 256 + SEQ] = jnp.where(kept, slot_ref[...], 0).astype(wide)
    smalls[0] = (
        jnp.dot(piece[...].astype(low), own_pick, preferred_element_type=wide) + table_buf[...]
    ).astype(low)
    for j in range(1, 8):
        small_copies.append(send(smalls.at[0], smalls.at[j], j))
    wq[own_rows, :] = qkv_ref[...].astype(low)
    gather_q = Gather(weight_view(wq), (0, 48), (48, 48))
    gather_q.begin()
    wp[own_rows, :] = proj_ref[...].astype(low)
    res_grad[192:SENT_ROWS, :] = jnp.zeros((SENT_ROWS - 192, width), wide)
    res_grad[0:SEQ, :] = cot_ref[...].astype(wide)
    rows_buf[ups_base : ups_base + SENT_ROWS, :] = res_grad[...].astype(low)
    resid[192:TILE_ROWS, :] = jnp.zeros((TILE_ROWS - 192, width), wide)
    resid[0:SEQ, :] = tok_ref[...].astype(wide)
    inputs = resid[...]
    normed, inverse = normalize(inputs)
    normed_a[...] = normed
    inv_a[...] = inverse

    def inner_cast(e):
        for d in range(8):
            grad_in[e, d * PIECE : (d + 1) * PIECE, :] = stage[
                :, d * part : (d + 1) * part
            ].astype(low)

    part = win.shape[2]
    for e in range(experts):
        staged.wait()
        inner_cast(e)
        if e < experts - 1:
            staged = local(inner_hbm.at[e + 1], stage)
        for copy in outer_staged[e]:
            copy.wait()
        for h in range(2):
            for c in range(3):
                outer_ref[e, h * tall : (h + 1) * tall, c * wide_cut : (c + 1) * wide_cut] = probs[
                    (e % 2) * 6 + h * 3 + c, 0:tall, :
                ].astype(low)
        if e == 0:
            outer_staged.append(outer_stage(2))
    gather_q.pass_on()
    half_at = (rep % 2) * (PIECE // 2)

    def inner_half(j):
        return pl.ds(pl.multiple_of(peers[j] * PIECE + half_at, 16), PIECE // 2)

    inner_own = local(grad_in.at[:, own_rows, :], win.at[:, own_rows, :])
    inner_passed = []

    def inner_pass(numbers):
        for j in numbers:
            inner_copies[j].wait_recv()
            rows = win.at[:, inner_half(j), :]
            inner_passed.append(send(rows, rows, 8))

    for copy in small_copies:
        copy.wait_recv()
    total = smalls[0].astype(wide)
    for j in range(1, 8):
        total = total + smalls[j].astype(wide)
    small_sum[...] = total
    gain_first, shift_first = small_sum[3:4, :], small_sum[4:5, :]
    gain_second, shift_second = small_sum[5:6, :], small_sum[6:7, :]
    ln_a[...] = (normed_a[...] * gain_first + shift_first).astype(low)
    slots = onehot.shape[1]
    slot_at = lax.broadcasted_iota(jnp.int32, (slots, TILE_ROWS), 0).astype(wide)

    def route_step(j, carry):
        table = smalls[j].astype(wide)
        first = table[8:9, 0:256] * CAP + table[8:9, 256:512]
        second = table[9:10, 0:256] * CAP + table[9:10, 256:512]
        hit = jnp.logical_or(slot_at == first, slot_at == second)
        onehot[j] = jnp.where(hit, 1.0, 0.0).astype(low)
        return carry

    lax.fori_loop(0, 8, route_step, 0)
    gather_q.last()
    gather_p = Gather(weight_view(wp), (0, 48), (48, 48))
    gather_p.begin()
    for copy in gather_q.from_s:
        copy.wait_recv()

    def triple_step(i, carry):
        columns = pl.ds(off(i, 384), 384)
        tri[:, columns] = jnp.dot(
            ln_a[...], wq[:, columns], preferred_element_type=wide
        ).astype(low)
        return carry

    lax.fori_loop(0, 6, triple_step, 0)
    gather_p.pass_on()
    inner_copies = {
        j: send(
            grad_in.at[:, inner_half(j), :],
            win.at[:, inner_half(0), :],
            j,
        )
        for j in range(1, 8)
    }

    lane = lax.broadcasted_iota(jnp.int32, (TILE_ROWS, 128), 1)
    key_at = lax.broadcasted_iota(jnp.int32, (TILE_ROWS, TILE_ROWS), 1)

    def head_columns(p, third):
        return pl.ds(pl.multiple_of(third * width + p * 128, 128), 128)

    def contract(a, b, da, db):
        return lax.dot_general(a, b, (((da,), (db,)), ((), ())), preferred_element_type=wide)

    def one_head(values, side):
        return jnp.where((lane < 64) == (side == 0), values, jnp.zeros_like(values))

    def attend(p, carry):
        queries = tri[:, head_columns(p, 0)]
        key_rows = tri[:, head_columns(p, 1)]
        value_rows = tri[:, head_columns(p, 2)]
        mixed = []
        for side in range(2):
            scores = contract(one_head(queries, side), key_rows, 1, 1) * score_scale
            scores = jnp.where(key_at < SEQ, scores, NEGATIVE)
            powers = jnp.exp(scores - jnp.max(scores, axis=-1, keepdims=True))
            weights = powers / jnp.sum(powers, axis=-1, keepdims=True)
            probs[2 * p + side] = weights
            mixed.append(jnp.dot(weights.astype(low), value_rows, preferred_element_type=wide))
        heads[:, head_columns(p, 0)] = jnp.where(lane < 64, mixed[0], mixed[1]).astype(low)
        return carry

    lax.fori_loop(0, 6, attend, 0, unroll=2)
    gather_p.last()
    for copy in gather_p.from_s:
        copy.wait_recv()
    residual = resid[...] + jnp.dot(
        heads[...], wp[...], preferred_element_type=wide
    )
    resid[...] = residual
    normed, inverse = normalize(residual)
    mean_m[...] = jnp.mean(residual, axis=-1, keepdims=True)
    inv_m[...] = inverse
    ln_two = (normed * gain_second + shift_second).astype(low)
    rows_buf[0:SENT_ROWS, :] = ln_two[0:SENT_ROWS, :]
    gather_l = Gather(row_view(0), (0, 112), (112, 96))
    gather_l.begin()
    inner_pass((1, 2, 3, 4, 5, 6, 7))
    router = small_sum[...].astype(low)
    lane16 = lax.broadcasted_iota(jnp.int32, (slots, 16), 1)
    expert_of = lax.broadcasted_iota(jnp.int32, (slots, 16), 0)
    own_lane = jnp.logical_and(expert_of >= lane16 * CAP, expert_of < lane16 * CAP + CAP)

    def expert_rows(e, j, blocks=1):
        return pl.ds(pl.multiple_of((e * 8 + j) * CAP, 16), blocks * CAP)

    def dispatch_step(j, carry):
        picks = onehot[j]
        ln_rows = rows_buf[pl.ds(off(j, TILE_ROWS), TILE_ROWS), :]
        sent = jnp.dot(picks, ln_rows, preferred_element_type=wide).astype(low)
        logits = jnp.where(lane16 < experts, contract(sent, router, 1, 1), NEGATIVE)
        powers = jnp.exp(logits - jnp.max(logits, axis=-1, keepdims=True))
        chances = powers / jnp.sum(powers, axis=-1, keepdims=True)
        for e in range(experts):
            rows = expert_rows(e, j)
            work[rows, :] = sent[e * CAP : (e + 1) * CAP]
            route[rows, :] = chances[e * CAP : (e + 1) * CAP]
        return carry

    def upward_step(j, carry):
        up_rows = rows_buf[pl.ds(pl.multiple_of(ups_base + j * TILE_ROWS, 16), TILE_ROWS), :]
        ups = jnp.dot(onehot[j], up_rows, preferred_element_type=wide)
        chances = jnp.concatenate([route[expert_rows(e, j), :] for e in range(experts)], axis=0)
        gate = jnp.sum(jnp.where(own_lane, chances, 0.0), axis=-1, keepdims=True)
        upward = (ups * gate).astype(low)
        for e in range(experts):
            og[expert_rows(e, j), :] = upward[e * CAP : (e + 1) * CAP]
        return carry

    def hidden_step(g):
        def step(e, carry):
            rows = pl.ds(g * 2 * CAP, 2 * CAP)
            sent = work[expert_rows(e, 2 * g, 2), :]
            value = jnp.dot(sent, win[e], preferred_element_type=wide)
            square = value * value
            bend = jnp.tanh(0.7978845608028654 * value * (1.0 + 0.044715 * square))
            act[e, rows, :] = (0.5 * value * (1.0 + bend)).astype(low)
            slope[e, rows, :] = (
                0.5 * (1.0 + bend)
                + 0.5
                * value
                * (1.0 - bend * bend)
                * (0.7978845608028654 * (1.0 + 0.134145 * square))
            ).astype(low)
            return carry

        lax.fori_loop(0, experts, step, 0, unroll=True)

    gather_l.pass_on()
    gather_u = Gather(row_view(ups_base), (0, 112), (112, 96))
    gather_u.begin()
    gather_l.from_s[0].wait_recv()
    lax.fori_loop(0, 2, dispatch_step, 0)
    gather_l.last()
    for g in range(1, 3):
        gather_l.from_s[g].wait_recv()
        lax.fori_loop(2 * g, 2 * g + 2, dispatch_step, 0)
    gather_u.pass_on()
    inner_own.wait()
    for copy in inner_passed:
        copy.wait_recv()
    hidden_step(0)
    hidden_step(1)
    hidden_step(2)
    gather_l.from_s[3].wait_recv()
    lax.fori_loop(6, 8, dispatch_step, 0)
    gather_u.last()
    hidden_step(3)
    for copy in gather_u.from_s:
        copy.wait_recv()
    lax.fori_loop(0, 8, upward_step, 0, unroll=2)

    ready, raised, left = [], [], []

    class Copies:
        def __init__(self, own, mid, end, out, rows):
            self.own, self.mid, self.end, self.out, self.rows = own, mid, end, out, rows
            self.up = describe(own, end, (shard, pair))
            self.over = describe(own, mid, (shard, across))
            self.down = describe(end, end, (shard, pair))
            self.write = pltpu.make_async_copy(end, out, local_sems.at[local_count[0]])
            local_count[0] += 1

        def add(self, target, other):
            size = self.rows

            def step(i, carry):
                at = pl.ds(pl.multiple_of(i * size, 16), size)
                target[at, :] = (
                    self.own[at, :].astype(wide) + other[at, :].astype(wide)
                ).astype(low)
                return carry

            lax.fori_loop(0, target.shape[0] // size, step, 0)

        def rise(self):
            ready.append(self)
            pump()

        def cross(self):
            self.up.wait_recv()
            self.add(self.own, self.end)
            self.over.start()

        def fall(self):
            self.over.wait_recv()
            self.add(self.end, self.mid)
            self.down.start()
            self.write.start()

    out_cut, in_cut = part // CUTS, grad_in_own.shape[2] // CUTS
    out_copies = [
        Copies(
            *(
                ref.at[e, pl.ds(h * out_cut, out_cut)]
                for ref in (grad_out, mid_out, end_out, go_hbm)
            ),
            48,
        )
        for e in range(experts)
        for h in range(CUTS)
    ]
    in_copies = [
        Copies(
            *(
                ref.at[e, :, pl.ds(h * in_cut, in_cut)]
                for ref in (grad_in_own, mid_in, end_in, gi_hbm)
            ),
            48,
        )
        for e in range(experts)
        for h in range(CUTS)
    ]
    attn_copies = {
        p: Copies(
            *(ref.at[pl.ds(p * PIECE, size)] for ref in (grad_attn, mid_attn, end_attn, ga_hbm)),
            size // 2 if size > 16 else size,
        )
        for p, size in ((3, PIECE), (2, PIECE), (1, PIECE), (0, PIECE), (4, 16))
    }
    all_copies = out_copies + in_copies + list(attn_copies.values())

    def pump():
        @pl.when(is_end)
        def _():
            while len(raised) < len(ready) and len(raised) < len(left) + DEPTH:
                ready[len(raised)].up.start()
                raised.append(1)

    plan = []
    moment = 0.0
    for number, copies in enumerate(all_copies):
        span = Z_STEP if number < 2 * experts * CUTS else 3.2
        moment += span
        plan.append((moment + span + Z_LAG, 0, copies))
        plan.append((moment + 3 * span + 2 * Z_LAG, 1, copies))
    plan.sort(key=lambda step: step[:2])

    def tend(until):
        while plan and plan[0][0] <= until:
            _, kind, copies = plan[0]
            if kind == 0 and len(ready) <= len(left):
                break
            plan.pop(0)

            @pl.when(is_mid)
            def _():
                (copies.fall if kind else copies.cross)()

            if kind == 0:

                @pl.when(is_end)
                def _():
                    copies.up.wait_send()

                left.append(1)
                pump()

    for e in range(experts):
        grad_out[e] = contract(act[e], og[expert_rows(e, 0, 8), :], 0, 0).astype(low)
        for h in range(CUTS):
            out_copies[CUTS * e + h].rise()

    settle(gather_l.all)
    settle(inner_copies.values())
    settle(gather_u.all)
    route_grad[...] = jnp.zeros(route_grad.shape, wide)
    half = act.shape[1] // 2
    lane_h = lax.broadcasted_iota(jnp.int32, (half, 16), 1)

    def inner_step(i, carry):
        e = i // 2
        rows = pl.ds(off(i % 2, half), half)
        flat = pl.ds(pl.multiple_of(i * half, 16), half)
        inner = contract(og[flat, :], outer_ref[e], 1, 1) * slope[e, rows, :].astype(wide)
        slope[e, rows, :] = inner.astype(low)
        return carry

    def back_step(i, carry):
        e = i // 2
        rows = pl.ds(off(i % 2, half), half)
        flat = pl.ds(pl.multiple_of(i * half, 16), half)
        upward = og[flat, :]
        gone = jnp.dot(act[e, rows, :], outer_ref[e], preferred_element_type=wide)
        chances = route[flat, :]
        gate = jnp.sum(jnp.where(lane_h == e, chances, 0.0), axis=-1, keepdims=True)
        pull = jnp.sum(upward.astype(wide) * gone, axis=-1, keepdims=True)
        logit = (pull * (jnp.where(lane_h == e, 1.0, 0.0) - chances)).astype(low)
        logit = jnp.where(lane_h < experts, logit, jnp.zeros_like(logit))
        rows_buf[flat, :] = (gone * gate).astype(low)
        og[flat, :] = (
            contract(slope[e, rows, :], win[e], 1, 1)
            + jnp.dot(logit, router, preferred_element_type=wide)
        ).astype(low)
        route_grad[...] += contract(logit, work[flat, :], 0, 0)
        return carry

    grad_in_copies = []

    def grad_in_send(e):
        target = grad_in_own.at[e, :, pl.ds(off(shard, part), part)]
        grad_in_copies.append(
            [
                send(grad_in.at[e, pl.ds(off(peers[j], PIECE), PIECE), :], target, j)
                for j in range(1, 8)
            ]
        )
        grad_in_copies[e].append(local(grad_in.at[e, own_rows, :], target))

    def grad_in_wait(e):
        for copy in grad_in_copies[e][:7]:
            copy.wait_recv()
        grad_in_copies[e][7].wait()
        for h in range(CUTS):
            in_copies[CUTS * e + h].rise()

    for e in range(experts):
        lax.fori_loop(2 * e, 2 * e + 2, inner_step, 0)
        grad_in[e] = contract(work[expert_rows(e, 0, 8), :], slope[e], 0, 0).astype(low)
        if e < experts - 1:
            grad_in_send(e)
        tend(4 + 2 * e)
    for e in range(experts):
        lax.fori_loop(2 * e, 2 * e + 2, back_step, 0, unroll=True)
        tend(10.5 + 2.3 * e)

    def combine_back(j):
        joined = jnp.concatenate([og[expert_rows(e, j), :] for e in range(experts)], axis=0)
        return contract(onehot[j], joined, 0, 0)[0:SENT_ROWS]

    def combine_out(j):
        joined = jnp.concatenate(
            [rows_buf[expert_rows(e, j), :] for e in range(experts)], axis=0
        )
        return contract(onehot[j], joined, 0, 0)[0:SENT_ROWS]

    stage_out = experts * 8 * CAP

    def odd_back(i, carry):
        st_back[i] = combine_back(2 * i + 1).astype(low)
        return carry

    lax.fori_loop(0, 4, odd_back, 0)
    swap_back = send(st_back, sr_back, 1)
    tend(17)

    def odd_out(i, carry):
        rows = pl.ds(pl.multiple_of(stage_out + i * SENT_ROWS, 16), SENT_ROWS)
        rows_buf[rows, :] = combine_out(2 * i + 1).astype(low)
        return carry

    lax.fori_loop(0, 4, odd_out, 0)
    tend(19)
    swap_back.wait_recv()

    def even_back(i, carry):
        sr_back[i] = (combine_back(2 * i) + sr_back[i].astype(wide)).astype(low)
        return carry

    lax.fori_loop(0, 4, even_back, 0)
    back_copies = [send(sr_back.at[i], rr_back.at[i - 1], 2 * i) for i in range(1, 4)]
    swap_out = send(rows_buf.at[pl.ds(stage_out, 4 * SENT_ROWS)], sr_out, 1)
    tend(22)
    swap_out.wait_recv()

    def even_out(i, carry):
        rows = pl.ds(off(i, SENT_ROWS), SENT_ROWS)
        sr_out[rows, :] = (combine_out(2 * i) + sr_out[rows, :].astype(wide)).astype(low)
        return carry

    lax.fori_loop(0, 4, even_out, 0)
    tend(25)
    for e in range(experts - 1):
        grad_in_wait(e)
    tend(38)

    for copy in back_copies:
        copy.wait_recv()
    grad_in_send(experts - 1)
    ln_grad = sr_back[0].astype(wide)
    for i in range(3):
        ln_grad = ln_grad + rr_back[i].astype(wide)
    normed = (resid[0:SENT_ROWS, :] - mean_m[0:SENT_ROWS, :]) * inv_m[0:SENT_ROWS, :]
    gain_m_grad = jnp.sum(ln_grad * normed, axis=0, keepdims=True)
    shift_m_grad = jnp.sum(ln_grad, axis=0, keepdims=True)
    upstream = res_grad[...]
    residual_grad = upstream + norm_back(
        ln_grad * gain_second, normed, inv_m[0:SENT_ROWS, :]
    )
    res_grad[...] = residual_grad
    agrad[...] = jnp.zeros(agrad.shape, low)
    agrad[0:SENT_ROWS, :] = residual_grad.astype(low)
    mgrad[...] = contract(agrad[...], wp[...], 1, 1).astype(low)

    def grad_rows(part, j):
        return pl.ds(pl.multiple_of(part * width + peers[j] * PIECE, 16), PIECE)

    def kept_rows(part, i):
        return pl.ds((i * 4 + part) * PIECE, PIECE)

    def come_rows(part, i):
        return pl.ds((16 + i * 4 + part) * PIECE, PIECE)

    def share(part):
        return [
            send(work.at[grad_rows(part, 2 * i + 1)], og.at[kept_rows(part, i)], 1)
            for i in range(4)
        ]

    def gather_share(part, copies):
        sent = []
        for i in range(4):
            copies[i].wait_recv()
            rows = kept_rows(part, i)
            og[rows, :] = (
                work[grad_rows(part, 2 * i), :].astype(wide) + og[rows, :].astype(wide)
            ).astype(low)
            if i > 0:
                sent.append(send(og.at[rows], og.at[come_rows(part, i - 1)], 2 * i))
        return sent

    def total_share(part, copies):
        total = og[kept_rows(part, 0), :].astype(wide)
        for i in range(3):
            copies[i].wait_recv()
            total = total + og[come_rows(part, i), :].astype(wide)
        grad_attn[pl.ds(part * PIECE, PIECE), :] = total.astype(low)
        attn_copies[part].rise()

    def attend_back(p, carry):
        queries = tri[:, head_columns(p, 0)]
        key_rows = tri[:, head_columns(p, 1)]
        value_rows = tri[:, head_columns(p, 2)]
        mixed = mgrad[:, head_columns(p, 0)]
        results = []
        for side in range(2):
            weights = probs[2 * p + side]
            value_grad = contract(weights.astype(low), mixed, 0, 0)
            weight_grad = contract(one_head(mixed, side), value_rows, 1, 1)
            score_grad = (
                weights
                * (weight_grad - jnp.sum(weights * weight_grad, axis=-1, keepdims=True))
                * score_scale
            ).astype(low)
            query_grad = jnp.dot(score_grad, key_rows, preferred_element_type=wide)
            key_grad = contract(score_grad, queries, 0, 0)
            results.append((query_grad, key_grad, value_grad))
        for third in range(3):
            tri[:, head_columns(p, third)] = jnp.where(
                lane < 64, results[0][third], results[1][third]
            ).astype(low)
        return carry

    work[3 * width : 4 * width, :] = contract(heads[...], agrad[...], 0, 0).astype(low)
    share_p = share(3)
    tend(43)
    lax.fori_loop(0, 3, attend_back, 0, unroll=True)
    tend(46)
    lax.fori_loop(3, 6, attend_back, 0, unroll=True)
    tend(50)

    def weight_grad_of(part):
        work[part * width : (part + 1) * width, :] = contract(
            ln_a[...], tri[:, part * width : (part + 1) * width], 0, 0
        ).astype(low)

    weight_grad_of(2)
    share_v = share(2)
    come_p = gather_share(3, share_p)
    weight_grad_of(1)
    share_k = share(1)
    come_v = gather_share(2, share_v)
    weight_grad_of(0)
    share_q = share(0)
    come_k = gather_share(1, share_k)
    tend(54)
    ln_grad = contract(tri[0:SENT_ROWS, :], wq[...], 1, 1)
    come_q = gather_share(0, share_q)
    normed = normed_a[0:SENT_ROWS, :]
    gain_a_grad = jnp.sum(ln_grad * normed, axis=0, keepdims=True)
    shift_a_grad = jnp.sum(ln_grad, axis=0, keepdims=True)
    row16 = lax.broadcasted_iota(jnp.int32, (16, width), 0)
    small = jnp.where(row16 < experts, route_grad[...], 0.0)
    for row, value in (
        (3, gain_a_grad),
        (4, shift_a_grad),
        (5, gain_m_grad),
        (6, shift_m_grad),
    ):
        small = small + jnp.where(row16 == row, value, 0.0)
    small_grad[0] = small.astype(low)
    swap = send(small_grad.at[0], small_swap.at[0], 1)
    igrad_ref[...] = (
        res_grad[...] + norm_back(ln_grad * gain_first, normed, inv_a[0:SENT_ROWS, :])
    ).astype(low)
    grad_in_wait(experts - 1)
    tend(57)
    for step in range(2):
        swap.wait_recv()
        small_grad[step + 1] = (
            small_grad[step].astype(wide) + small_swap[step].astype(wide)
        ).astype(low)
        swap = send(small_grad.at[step + 1], small_swap.at[step + 1], 2 << step)
        tend(60 + 3 * step)
    tend(72)
    total_share(3, come_p)
    total_share(2, come_v)
    tend(76)
    total_share(1, come_k)
    total_share(0, come_q)
    out_sends = [
        send(sr_out.at[pl.ds(i * SENT_ROWS, SENT_ROWS)], rr_out.at[i - 1], 2 * i)
        for i in range(1, 4)
    ]
    swap.wait_recv()
    grad_attn[4 * PIECE : 4 * PIECE + 16, :] = (
        small_grad[2].astype(wide) + small_swap[2].astype(wide)
    ).astype(low)
    attn_copies[4].rise()
    tend(84)
    tend(1000)
    output = resid[0:SENT_ROWS, :] + sr_out[0:SENT_ROWS, :].astype(wide)
    for i in range(3):
        out_sends[i].wait_recv()
        output = output + rr_out[i].astype(wide)
    out_ref[...] = output.astype(low)
    for copies in all_copies:

        @pl.when(is_end)
        def _():
            copies.down.wait_recv()
            copies.write.start()

        @pl.when(is_mid)
        def _():
            copies.over.wait_send()
            copies.down.wait_send()

    for copies in all_copies:
        copies.write.wait()
    assert count[0] <= send_sems.shape[0] and local_count[0] <= local_sems.shape[0]
    piece_ref[...] = contract(end_attn[4 * PIECE : 4 * PIECE + 16, :], own_pick, 1, 1)
    for copy in unsent:
        if id(copy) not in settled:
            copy.wait_send()


def finish(
    out_in,
    igrad_in,
    outer_in,
    inner_in,
    attn_in,
    small_in,
    out_ref,
    igrad_ref,
    outer_ref,
    inner_ref,
    qkv_ref,
    proj_ref,
    router_ref,
    gain_a_ref,
    shift_a_ref,
    gain_m_ref,
    shift_m_ref,
):
    wide = jnp.float32
    outer_ref[...] = outer_in[...].astype(wide)
    inner_ref[...] = inner_in[...].astype(wide)

    @pl.when(pl.program_id(0) == 0)
    def _():
        rows, width = out_ref.shape
        out_ref[...] = out_in[0:rows, :]
        igrad_ref[...] = igrad_in[0:rows, :]
        for third in range(3):
            qkv_ref[:, third * width : (third + 1) * width] = attn_in[
                third * PIECE : (third + 1) * PIECE, :
            ].astype(wide)
        proj_ref[...] = attn_in[3 * PIECE : 4 * PIECE, :].astype(wide)
        experts = router_ref.shape[0]
        router_ref[...] = small_in[0:experts, 0:PIECE]
        for row, ref in enumerate((gain_a_ref, shift_a_ref, gain_m_ref, shift_m_ref)):
            ref[...] = small_in[experts + row : experts + row + 1, 0:PIECE]


def grouped(
    tokens,
    cotangent,
    expert_index,
    slot_index,
    kept_mask,
    gain_attn,
    shift_attn,
    w_qkv,
    w_proj,
    gain_moe,
    shift_moe,
    w_router,
    w_in,
    w_out,
):
    low = jnp.bfloat16
    wide = jnp.float32
    rows, width = tokens.shape
    owned, experts, hidden = w_in.shape
    part = w_out.shape[0]
    shard = lax.axis_index("shard")
    slots = experts * CAP
    total_slots = 8 * slots
    vmem = pltpu.VMEM
    token_shape = jax.ShapeDtypeStruct((SENT_ROWS, width), low)
    attn_rows = 4 * PIECE + 16
    scratch = [
        vmem((owned, hidden), wide),
        vmem((experts, part, width), low),
        vmem((16, 128), wide),
        vmem((16, width), wide),
        vmem((8, 16, width), low),
        vmem((16, width), wide),
        vmem((width, 3 * width), low),
        vmem((width, width), low),
        vmem((experts, width, part), low),
        vmem((TILE_ROWS, width), wide),
        vmem((TILE_ROWS, 1), wide),
        vmem((TILE_ROWS, width), low),
        vmem((TILE_ROWS, 3 * width), low),
        vmem((HEADS, TILE_ROWS, TILE_ROWS), wide),
        vmem((TILE_ROWS, width), low),
        vmem((TILE_ROWS, width), wide),
        vmem((TILE_ROWS, 1), wide),
        vmem((TILE_ROWS, 1), wide),
        vmem((16 * TILE_ROWS, width), low),
        vmem((8, slots, TILE_ROWS), low),
        vmem((4 * width, width), low),
        vmem((total_slots, width), low),
        vmem((total_slots, 16), wide),
        vmem((experts, 8 * CAP, part), low),
        vmem((experts, 8 * CAP, part), low),
        vmem((16, width), wide),
        vmem((4, SENT_ROWS, width), low),
        vmem((4, SENT_ROWS, width), low),
        vmem((3, SENT_ROWS, width), low),
        vmem((4 * SENT_ROWS, width), low),
        vmem((3, SENT_ROWS, width), low),
        vmem((experts, width, part), low),
        vmem((experts, owned, hidden), low),
        vmem((experts, part, width), low),
        vmem((attn_rows, width), low),
        vmem((experts, owned, hidden), low),
        vmem((experts, part, width), low),
        vmem((attn_rows, width), low),
        vmem((experts, owned, hidden), low),
        vmem((experts, part, width), low),
        vmem((attn_rows, width), low),
        vmem((SENT_ROWS, width), wide),
        vmem((TILE_ROWS, width), low),
        vmem((TILE_ROWS, width), low),
        vmem((3, 16, width), low),
        vmem((3, 16, width), low),
        pltpu.SemaphoreType.DMA((256,)),
        pltpu.SemaphoreType.DMA((256,)),
        pltpu.SemaphoreType.DMA((64,)),
    ]
    inside = pl.BlockSpec(memory_space=vmem)
    outside = pl.BlockSpec(memory_space=pl.ANY)
    output, input_grad, outer_sum, inner_sum, attn_sum, small_sum = pl.pallas_call(
        mega,
        out_shape=(
            token_shape,
            token_shape,
            jax.ShapeDtypeStruct((experts, part, width), low),
            jax.ShapeDtypeStruct((experts, owned, hidden), low),
            jax.ShapeDtypeStruct((attn_rows, width), low),
            jax.ShapeDtypeStruct((16, 128), wide),
        ),
        in_specs=[inside] * 12 + [outside, outside],
        out_specs=(inside, inside, outside, outside, outside, inside),
        scratch_shapes=scratch,
        compiler_params=pltpu.CompilerParams(
            collective_id=0, has_side_effects=True, vmem_limit_bytes=VMEM_BYTES
        ),
    )(
        tokens,
        cotangent,
        expert_index.T,
        slot_index.T,
        kept_mask.T,
        gain_attn.reshape(1, owned),
        shift_attn.reshape(1, owned),
        gain_moe.reshape(1, owned),
        shift_moe.reshape(1, owned),
        w_router.T,
        w_qkv,
        w_proj,
        jnp.transpose(w_in, (1, 0, 2)),
        jnp.transpose(w_out, (1, 0, 2)),
    )

    def whole(*shape):
        return pl.BlockSpec(shape, lambda e: (0,) * len(shape))

    def one(*shape):
        return pl.BlockSpec((1, *shape), lambda e: (e, 0, 0))

    finals = pl.pallas_call(
        finish,
        grid=(experts,),
        out_shape=(
            jax.ShapeDtypeStruct((rows, width), low),
            jax.ShapeDtypeStruct((rows, width), low),
            jax.ShapeDtypeStruct((experts, part, width), wide),
            jax.ShapeDtypeStruct((experts, owned, hidden), wide),
            jax.ShapeDtypeStruct((owned, 3 * width), wide),
            jax.ShapeDtypeStruct((owned, width), wide),
            jax.ShapeDtypeStruct((experts, owned), wide),
        )
        + (jax.ShapeDtypeStruct((1, owned), wide),) * 4,
        in_specs=[
            whole(SENT_ROWS, width),
            whole(SENT_ROWS, width),
            one(part, width),
            one(owned, hidden),
            whole(attn_rows, width),
            whole(16, 128),
        ],
        out_specs=(
            whole(rows, width),
            whole(rows, width),
            one(part, width),
            one(owned, hidden),
            whole(owned, 3 * width),
            whole(owned, width),
            whole(experts, owned),
        )
        + (whole(1, owned),) * 4,
        compiler_params=pltpu.CompilerParams(vmem_limit_bytes=VMEM_BYTES),
    )(output, input_grad, outer_sum, inner_sum, attn_sum, small_sum)
    return (
        finals[0],
        finals[1],
        finals[7].reshape(owned),
        finals[8].reshape(owned),
        finals[4],
        finals[5],
        finals[9].reshape(owned),
        finals[10].reshape(owned),
        finals[6].T,
        jnp.transpose(finals[3], (1, 0, 2)),
        jnp.transpose(finals[2], (1, 0, 2)),
    )


def solution(mesh):
    sizes = (mesh.shape["shard"], mesh.shape["rep"])
    return jax.shard_map(
        grouped if sizes == (8, 4) else shards,
        mesh=mesh,
        in_specs=(
            P(("shard", "rep"), None),
            P(("shard", "rep"), None),
            P(("shard", "rep"), None),
            P(("shard", "rep"), None),
            P(("shard", "rep"), None),
            P("shard"),
            P("shard"),
            P("shard", None),
            P("shard", None),
            P("shard"),
            P("shard"),
            P("shard", None),
            P("shard", None, None),
            P("shard", None, None),
        ),
        out_specs=(
            P(("shard", "rep"), None),
            P(("shard", "rep"), None),
            P("shard"),
            P("shard"),
            P("shard", None),
            P("shard", None),
            P("shard"),
            P("shard"),
            P("shard", None),
            P("shard", None, None),
            P("shard", None, None),
        ),
        check_vma=False,
    )
```
